32 devices in a mesh: shard: 8 (over y, x, core), replica: 4 (over z).
Axes of the slice: x: 2, y: 2, z: 4, core: 2. Of those that a mesh axis runs over, the one named last changes fastest.
Arguments:
- tokens: bfloat16 [4, 2048, 2048], P('replica', 'shard'), may hold values from -6 to 6
- segments: int32 [4, 2048], P('replica'), may hold values from 0 to 13, as said below
- positions: int32 [4, 2048], P('replica'), may hold values from 0 to 2046, as said below
- ln_gain: float32 [2048], replicated, may hold values from 0.5 to 1.5
- ln_bias: float32 [2048], replicated, may hold values from -3 to 3
- w_qkv: bfloat16 [2048, 3, 2048], P(None, None, 'shard'), may hold values from -0.125 to 0.125
- b_qkv: float32 [3, 2048], P(None, 'shard'), may hold values from -3 to 3
- w_up: bfloat16 [2048, 8192], P(None, 'shard'), may hold values from -0.125 to 0.125
- b_up: float32 [8192], P('shard'), may hold values from -3 to 3
- w_out: bfloat16 [2048, 2048], P('shard'), may hold values from -0.75 to 0.75
- b_out: float32 [2048], replicated, may hold values from -3 to 3
- w_down: bfloat16 [8192, 2048], P('shard'), may hold values from -0.0625 to 0.0625
- b_down: float32 [2048], replicated, may hold values from -3 to 3
- grad_out: bfloat16 [4, 2048, 2048], P('replica', 'shard'), may hold values from -6 to 6
Outputs:
- mixed: bfloat16 [4, 2048, 2048], P('replica', 'shard')
- grad_tokens: bfloat16 [4, 2048, 2048], P('replica', 'shard')
- grad_ln_gain: float32 [2048], replicated
- grad_ln_bias: float32 [2048], replicated
- grad_w_qkv: float32 [2048, 3, 2048], P(None, None, 'shard')
- grad_b_qkv: float32 [3, 2048], P(None, 'shard')
- grad_w_up: float32 [2048, 8192], P(None, 'shard')
- grad_b_up: float32 [8192], P('shard')
- grad_w_out: float32 [2048, 2048], P('shard')
- grad_b_out: float32 [2048], replicated
- grad_w_down: float32 [8192, 2048], P('shard')
- grad_b_down: float32 [2048], replicated
The draws below stay inside these ranges and needn't reach their ends.
Inputs may be any that keep to these rules, and one draw needn't show every extreme that they name: `segments`: A group holds 2 packed sequences of 1024 tokens in a row; no segment number appears in two sequences. Segment numbers never fall along a group. `positions`: within a segment a token's position is one more than that of the token before it.
All inputs are finite; a program needn't handle non-finite values.
Results may differ from the reference program's by a relative error of at most 0.018.
Values may be sent and summed in bfloat16 or wider, within the bound.
A program may use at most 192 MiB of HBM per device.

```python
import math
import jax
import jax.numpy as jnp
from jax import lax

D = 2048
HEADS = 32
HEAD_DIM = 64
FF = 8192
ROT = 32
SEQ = 1024
GROUP_TOK = 2048
GROUPS = 4


def segment_plan(key):
    per_group = GROUP_TOK // SEQ
    seq_rows = GROUPS * per_group
    quarter = SEQ // 4
    early_cuts = jax.random.randint(jax.random.fold_in(key, 11), (seq_rows, 3), 1, quarter)
    late_cuts = jax.random.randint(jax.random.fold_in(key, 12), (seq_rows, 3), SEQ - quarter + 1, SEQ)
    cut_points = jnp.concatenate([early_cuts, late_cuts], axis=1).astype(jnp.int32)
    token_ids = jnp.arange(SEQ, dtype=jnp.int32)
    passed = (token_ids[None, :, None] >= cut_points[:, None, :]).astype(jnp.int32)
    local_ids = jnp.sum(passed, axis=2).astype(jnp.int32)
    doc_start = jnp.max(passed * cut_points[:, None, :], axis=2)
    last_start = jnp.max(cut_points, axis=1).astype(jnp.int32)
    shifts = jax.random.randint(jax.random.fold_in(key, 13), (seq_rows, 7), 0, 1024).astype(jnp.int32)
    row_ids = jnp.arange(seq_rows, dtype=jnp.int32)[:, None]
    col_ids = jnp.arange(7, dtype=jnp.int32)[None, :]
    shifts = jnp.where((row_ids == 0) & (col_ids == 0), 0, shifts).astype(jnp.int32)
    shifts = jnp.where((row_ids == 0) & (col_ids == 6), 1023 + last_start[:, None], shifts).astype(jnp.int32)
    choose = (local_ids[:, :, None] == jnp.arange(7, dtype=jnp.int32)[None, None, :]).astype(jnp.int32)
    offsets_row = jnp.sum(choose * shifts[:, None, :], axis=2)
    seq_index = (jnp.arange(seq_rows, dtype=jnp.int32) % per_group).astype(jnp.int32)
    segment_ids = (local_ids + 7 * seq_index[:, None]).astype(jnp.int32)
    position_ids = (token_ids[None, :] - doc_start + offsets_row).astype(jnp.int32)
    return (segment_ids.reshape(GROUPS, GROUP_TOK), position_ids.reshape(GROUPS, GROUP_TOK))


def draw_segments(key, part):
    segment_ids, position_ids = segment_plan(key)
    return segment_ids


def draw_positions(key, part):
    segment_ids, position_ids = segment_plan(key)
    return position_ids


def block_levels(key, dims, shards, low, largest):
    def one(axis_at, shards_of):
        draws = jax.random.uniform(jax.random.fold_in(jax.random.fold_in(key, 6), axis_at), (shards_of,), jnp.float32, low / len(shards), largest / len(shards))
        return jnp.repeat(jnp.exp(draws), dims[axis_at] // shards_of).reshape((-1,) + (1,) * (len(dims) - axis_at - 1))

    level = one(*shards[0])
    for cut in shards[1:]:
        level = level * one(*cut)
    return level


def normal_values(stream_key, extent, spread, limit, pieces=(), kind=jnp.bfloat16):
    entries = jax.random.normal(stream_key, extent, jnp.float32) * spread
    if len(pieces) > 0:
        entries = block_levels(stream_key, extent, pieces, -0.22, 0.18) * entries
    return jnp.clip(entries, min=-limit, max=limit).astype(kind)


def setup_inputs(seed: int = 0) -> dict:
    seeds = jax.random.split(jax.random.key(seed), 15)
    tokens = normal_values(seeds[0], (GROUPS, GROUP_TOK, D), 1.0, 6.0, ((0, 4), (1, 8)))
    segments = draw_segments(jax.random.fold_in(seeds[14], 71), 0)
    positions = draw_positions(jax.random.fold_in(seeds[14], 71), 0)
    ln_gain = jnp.clip(1.0 + 0.1 * jax.random.normal(seeds[3], (D,), jnp.float32), 0.5, 1.5)
    ln_bias = normal_values(seeds[4], (D,), 0.3, 3.0, (), jnp.float32)
    w_qkv = normal_values(seeds[5], (D, 3, D), D ** -0.5, 0.125, ((2, 8),))
    b_qkv = normal_values(seeds[6], (3, D), 0.3, 3.0, ((1, 8),), jnp.float32)
    w_up = normal_values(seeds[7], (D, FF), D ** -0.5, 0.125, ((1, 8),))
    b_up = normal_values(seeds[8], (FF,), 0.3, 3.0, ((0, 8),), jnp.float32)
    w_out = normal_values(seeds[9], (D, D), (D // 32) ** -0.5, 0.75, ((0, 8),))
    b_out = normal_values(seeds[10], (D,), 0.3, 3.0, (), jnp.float32)
    w_down = normal_values(seeds[11], (FF, D), FF ** -0.5, 0.0625, ((0, 8),))
    b_down = normal_values(seeds[12], (D,), 0.3, 3.0, (), jnp.float32)
    grad_out = normal_values(seeds[13], (GROUPS, GROUP_TOK, D), 1.0, 6.0, ((0, 4), (1, 8)))
    return {"tokens": tokens, "segments": segments, "positions": positions, "ln_gain": ln_gain, "ln_bias": ln_bias, "w_qkv": w_qkv, "b_qkv": b_qkv, "w_up": w_up, "b_up": b_up, "w_out": w_out, "b_out": b_out, "w_down": w_down, "b_down": b_down, "grad_out": grad_out}


EPSILON = 1e-05
PRECISE = lax.Precision.HIGHEST

@jax.custom_vjp
def low(v):
    return lax.optimization_barrier(v.astype(jnp.bfloat16)).astype(jnp.float32)

@jax.custom_vjp
def low_back(v):
    return v

def low_keep(v):
    return (low(v), None)

def low_pass(kept, grad):
    return (grad,)

def back_keep(v):
    return (v, None)

def back_low(kept, grad):
    return (low(grad),)
low.defvjp(low_keep, low_pass)
low_back.defvjp(back_keep, back_low)

def angles(positions):
    frequency = jnp.exp(jnp.arange(ROT // 2, dtype=jnp.float32) * (-2.0 * math.log(10000.0) / ROT))
    phase_angle = positions.astype(jnp.float32)[:, None] * frequency[None, :]
    return (jnp.cos(phase_angle), jnp.sin(phase_angle))

def rotate(heads_in, cosine_part, sine_part):
    half_rot = ROT // 2
    first_part = heads_in[..., :half_rot]
    second_part = heads_in[..., half_rot:ROT]
    cosine_rows = cosine_part[:, None, :]
    sine_rows = sine_part[:, None, :]
    return jnp.concatenate([first_part * cosine_rows - second_part * sine_rows, second_part * cosine_rows + first_part * sine_rows, heads_in[..., ROT:]], axis=-1)

def block_forward(tokens, ln_gain, ln_bias, w_qkv, b_qkv, w_up, b_up, w_out, b_out, w_down, b_down, cosine_part, sine_part, segments):
    length = tokens.shape[0]
    centered = tokens - lax.optimization_barrier(jnp.mean(tokens, axis=1, keepdims=True))
    scaled = centered * lax.rsqrt(lax.optimization_barrier(jnp.mean(centered * centered, axis=1, keepdims=True)) + EPSILON)
    normed = low(scaled * ln_gain + ln_bias)
    projected = low_back(jnp.einsum('sd,dtc->stc', normed, w_qkv, precision=PRECISE) + b_qkv)
    queries = low(rotate(projected[:, 0].reshape(length, HEADS, HEAD_DIM), cosine_part, sine_part))
    keys_all = low(rotate(projected[:, 1].reshape(length, HEADS, HEAD_DIM), cosine_part, sine_part))
    values_all = low(projected[:, 2].reshape(length, HEADS, HEAD_DIM))
    block_rows = math.gcd(length, 512)
    key_ids = jnp.arange(length, dtype=jnp.int32)

    def attend(block_start):
        query_block = lax.dynamic_slice_in_dim(queries, block_start, block_rows, 0)
        query_ids = block_start + jnp.arange(block_rows, dtype=jnp.int32)
        query_segs = lax.dynamic_slice_in_dim(segments, block_start, block_rows, 0)
        scores = low_back(jnp.einsum('qhe,khe->hqk', query_block, keys_all, precision=PRECISE) * HEAD_DIM ** (-0.5))
        allowed = (query_ids[:, None] >= key_ids[None, :]) & (query_segs[:, None] == segments[None, :])
        scores = jnp.where(allowed[None], scores, -1e+30)
        row_max = lax.optimization_barrier(jnp.max(scores, axis=2, keepdims=True))
        weights = jnp.exp(scores - row_max)
        probability = weights / lax.optimization_barrier(jnp.sum(weights, axis=2, keepdims=True))
        return jnp.einsum('hqk,khe->qhe', low(probability), values_all, precision=PRECISE)
    starts = jnp.arange(length // block_rows, dtype=jnp.int32) * block_rows
    attended = lax.map(jax.checkpoint(attend), starts).reshape(length, D)
    attended = low(low_back(attended))
    up_proj = low_back(jnp.dot(normed, w_up, precision=PRECISE) + b_up)
    activation = low(jax.nn.gelu(up_proj, approximate=True))
    branches = jnp.dot(attended, w_out, precision=PRECISE) + b_out + jnp.dot(activation, w_down, precision=PRECISE) + b_down
    return tokens + branches

def reference(tokens, segments, positions, ln_gain, ln_bias, w_qkv, b_qkv, w_up, b_up, w_out, b_out, w_down, b_down, grad_out):
    params = tuple((array_item.astype(jnp.float32) for array_item in (ln_gain, ln_bias, w_qkv, b_qkv, w_up, b_up, w_out, b_out, w_down, b_down)))

    def one_group(totals, inputs):
        seq_tokens, seq_segments, seq_positions, seq_grad = inputs
        cosine_part, sine_part = angles(seq_positions)

        def forward(token_rows, *weights):
            return block_forward(token_rows, *weights, cosine_part, sine_part, seq_segments)
        result, pullback = jax.vjp(forward, seq_tokens.astype(jnp.float32), *params)
        gradients = pullback(seq_grad.astype(jnp.float32))
        totals = tuple((total_item + grad_item for total_item, grad_item in zip(totals, gradients[1:])))
        return (totals, (result.astype(jnp.bfloat16), gradients[0].astype(jnp.bfloat16)))
    starting = tuple((jnp.zeros_like(array_item) for array_item in params))
    totals, (mixed_out, grad_tokens) = lax.scan(one_group, starting, (tokens, segments, positions, grad_out))
    return (mixed_out, grad_tokens, totals[0], totals[1], totals[2], totals[3], totals[4], totals[5], totals[6], totals[7], totals[8], totals[9])
```

```python
import functools
import math

import jax
import jax.numpy as jnp
from jax import lax
from jax.experimental import pallas as pl
from jax.experimental.pallas import tpu as pltpu
from jax.sharding import PartitionSpec as P

HEAD_DIM = 64
ROT = 32


EPSILON = 1e-05
NEGATIVE = -1e30
VMEM_BYTES = 64 * 1024 * 1024


def angles(positions):
    frequency = jnp.exp(jnp.arange(ROT // 2, dtype=jnp.float32) * (-2.0 * math.log(10000.0) / ROT))
    phase_angle = positions.astype(jnp.float32)[:, None] * frequency[None, :]
    return (jnp.cos(phase_angle), jnp.sin(phase_angle))


def rotate(heads_in, cosine_part, sine_part):
    half_rot = ROT // 2
    first_part = heads_in[..., :half_rot]
    second_part = heads_in[..., half_rot:ROT]
    cosine_rows = cosine_part[:, None, :]
    sine_rows = sine_part[:, None, :]
    return jnp.concatenate(
        [
            first_part * cosine_rows - second_part * sine_rows,
            second_part * cosine_rows + first_part * sine_rows,
            heads_in[..., ROT:],
        ],
        axis=-1,
    )


def layer_norm(token_rows, gain_vector, bias_vector):
    centered = token_rows - jnp.mean(token_rows, axis=1, keepdims=True)
    scaled = centered * lax.rsqrt(jnp.mean(centered * centered, axis=1, keepdims=True) + EPSILON)
    return scaled * gain_vector + bias_vector


def take_rows(array_in, row_start, row_count):
    return lax.dynamic_slice_in_dim(array_in, row_start, row_count, 0)


def body(
    tokens,
    segments,
    positions,
    ln_gain,
    ln_bias,
    w_qkv,
    b_qkv,
    w_up,
    b_up,
    w_out,
    b_out,
    w_down,
    b_down,
    grad_out,
):
    local_rows = tokens[0].astype(jnp.float32)
    tok_rows, model_width = local_rows.shape
    length = tok_rows * lax.axis_size("shard")
    head_cols = w_qkv.shape[2]
    heads_here = head_cols // HEAD_DIM
    qkv_cols = 3 * head_cols
    split_shape = (length, heads_here, HEAD_DIM)
    scale_factor = HEAD_DIM ** (-0.5)
    cosine_part, sine_part = angles(positions[0])
    seq_segments = segments[0]
    normed_full, norm_back = jax.vjp(layer_norm, local_rows, ln_gain, ln_bias)
    normed = normed_full.astype(jnp.bfloat16)
    w_inner = jnp.concatenate([w_qkv.reshape(model_width, qkv_cols), w_up], axis=1)
    b_inner = jnp.concatenate([b_qkv.reshape(qkv_cols), b_up])
    gathered = lax.all_gather(normed, "shard", axis=0, tiled=True)
    inner_proj = jnp.dot(gathered, w_inner, preferred_element_type=jnp.float32)
    inner_proj = inner_proj + b_inner
    queries = rotate(inner_proj[:, :head_cols].reshape(split_shape), cosine_part, sine_part).astype(
        jnp.bfloat16
    )
    keys_all = rotate(
        inner_proj[:, head_cols : 2 * head_cols].reshape(split_shape), cosine_part, sine_part
    ).astype(jnp.bfloat16)
    values_all = inner_proj[:, 2 * head_cols : qkv_cols].reshape(split_shape).astype(jnp.bfloat16)
    up_proj = inner_proj[:, qkv_cols:]
    activation = jax.nn.gelu(up_proj, approximate=True).astype(jnp.bfloat16)
    block_rows = math.gcd(length, 512)
    block_count = length // block_rows
    offsets_block = jnp.arange(block_rows, dtype=jnp.int32)

    def block_scores(query_block, key_block, query_start, key_start):
        scores = (
            jnp.einsum("qhe,khe->hqk", query_block, key_block, preferred_element_type=jnp.float32)
            * scale_factor
        )
        query_ids = query_start + offsets_block
        key_ids = key_start + offsets_block
        query_segs = take_rows(seq_segments, query_start, block_rows)
        key_segs = take_rows(seq_segments, key_start, block_rows)
        allowed = (query_ids[:, None] >= key_ids[None, :]) & (
            query_segs[:, None] == key_segs[None, :]
        )
        return jnp.where(allowed[None], scores, NEGATIVE)

    def attend(query_index):
        query_start = query_index * block_rows
        query_block = take_rows(queries, query_start, block_rows)

        def first_pass(key_index, row_stats):
            row_max, row_sum = row_stats
            key_start = key_index * block_rows
            scores = block_scores(
                query_block, take_rows(keys_all, key_start, block_rows), query_start, key_start
            )
            new_max = jnp.maximum(row_max, jnp.max(scores, axis=2))
            row_sum = row_sum * jnp.exp(row_max - new_max) + jnp.sum(
                jnp.exp(scores - new_max[:, :, None]), axis=2
            )
            return (new_max, row_sum)

        row_max, row_sum = lax.fori_loop(
            0,
            query_index + 1,
            first_pass,
            (
                jnp.full((heads_here, block_rows), NEGATIVE, jnp.float32),
                jnp.zeros((heads_here, block_rows), jnp.float32),
            ),
        )

        def second_pass(key_index, total_out):
            key_start = key_index * block_rows
            scores = block_scores(
                query_block, take_rows(keys_all, key_start, block_rows), query_start, key_start
            )
            probability = (jnp.exp(scores - row_max[:, :, None]) / row_sum[:, :, None]).astype(
                jnp.bfloat16
            )
            return total_out + jnp.einsum(
                "hqk,khe->qhe",
                probability,
                take_rows(values_all, key_start, block_rows),
                preferred_element_type=jnp.float32,
            )

        attended_block = lax.fori_loop(
            0,
            query_index + 1,
            second_pass,
            jnp.zeros((block_rows, heads_here, HEAD_DIM), jnp.float32),
        )
        return (attended_block, row_max, row_sum)

    attended_full, row_maxes, row_sums = lax.map(attend, jnp.arange(block_count, dtype=jnp.int32))
    attended_full = attended_full.reshape(length, head_cols)
    attended = attended_full.astype(jnp.bfloat16)
    outer_act = jnp.concatenate([attended, activation], axis=1)
    w_outer = jnp.concatenate([w_out, w_down], axis=0)
    branches = lax.psum_scatter(
        jnp.dot(
            take_rows(outer_act, jnp.int32(0), lax.axis_size("shard") * tok_rows),
            w_outer,
            preferred_element_type=jnp.float32,
        ).astype(jnp.bfloat16),
        "shard",
        scatter_dimension=0,
        tiled=True,
    ).astype(jnp.float32)
    mixed_out = (local_rows + branches + b_out + b_down).astype(jnp.bfloat16)
    cotangent = grad_out[0]
    shard_piece = lax.all_gather(cotangent, "shard", axis=0, tiled=True)
    act_rows = take_rows(outer_act, jnp.int32(0), shard_piece.shape[0])
    weight_sum = jnp.einsum("sa,sd->ad", act_rows, shard_piece, preferred_element_type=jnp.float32)
    back_rows = jnp.einsum("sd,ad->sa", shard_piece, w_outer, preferred_element_type=jnp.float32)
    grad_outer = weight_sum
    back_attended = back_rows[:, :head_cols].astype(jnp.bfloat16).reshape(split_shape)
    delta_all = jnp.sum(
        back_attended.astype(jnp.float32) * attended_full.reshape(split_shape), axis=2
    ).T

    def key_pass(key_index, grads_all):
        grad_query, grad_key, grad_value = grads_all
        key_start = key_index * block_rows
        key_block = take_rows(keys_all, key_start, block_rows)
        value_block = take_rows(values_all, key_start, block_rows)

        def query_pass(query_index, inner_state):
            grad_query, key_total, value_total = inner_state
            query_start = query_index * block_rows
            query_block = take_rows(queries, query_start, block_rows)
            back_block = take_rows(back_attended, query_start, block_rows)
            delta_block = lax.dynamic_slice_in_dim(delta_all, query_start, block_rows, 1)
            scores = block_scores(query_block, key_block, query_start, key_start)
            probability = (
                jnp.exp(scores - row_maxes[query_index][:, :, None])
                / row_sums[query_index][:, :, None]
            )
            grad_prob = jnp.einsum(
                "qhe,khe->hqk", back_block, value_block, preferred_element_type=jnp.float32
            )
            grad_scores = (probability * (grad_prob - delta_block[:, :, None])).astype(jnp.bfloat16)
            value_total = value_total + jnp.einsum(
                "hqk,qhe->khe",
                probability.astype(jnp.bfloat16),
                back_block,
                preferred_element_type=jnp.float32,
            )
            key_total = key_total + jnp.einsum(
                "hqk,qhe->khe", grad_scores, query_block, preferred_element_type=jnp.float32
            )
            query_rows = take_rows(grad_query, query_start, block_rows) + jnp.einsum(
                "hqk,khe->qhe", grad_scores, key_block, preferred_element_type=jnp.float32
            )
            grad_query = lax.dynamic_update_slice_in_dim(grad_query, query_rows, query_start, 0)
            return (grad_query, key_total, value_total)

        empty_block = jnp.zeros((block_rows, heads_here, HEAD_DIM), jnp.float32)
        grad_query, key_total, value_total = lax.fori_loop(
            key_index, block_count, query_pass, (grad_query, empty_block, empty_block)
        )
        grad_key = lax.dynamic_update_slice_in_dim(grad_key, key_total, key_start, 0)
        grad_value = lax.dynamic_update_slice_in_dim(grad_value, value_total, key_start, 0)
        return (grad_query, grad_key, grad_value)

    empty_all = jnp.zeros(split_shape, jnp.float32)
    grad_query, grad_key, grad_value = lax.fori_loop(
        0, block_count, key_pass, (empty_all, empty_all, empty_all)
    )
    grad_query = rotate(grad_query * scale_factor, cosine_part, -sine_part)
    grad_key = rotate(grad_key * scale_factor, cosine_part, -sine_part)
    _, gelu_back = jax.vjp(functools.partial(jax.nn.gelu, approximate=True), up_proj)
    grad_up = gelu_back(back_rows[:, head_cols:])[0]
    grad_inner_rows = jnp.concatenate(
        [
            grad_query.reshape(length, head_cols),
            grad_key.reshape(length, head_cols),
            grad_value.reshape(length, head_cols),
            grad_up,
        ],
        axis=1,
    ).astype(jnp.bfloat16)
    grad_normed = lax.psum_scatter(
        jnp.einsum(
            "sa,da->sd",
            take_rows(grad_inner_rows, jnp.int32(0), lax.axis_size("shard") * tok_rows),
            w_inner,
            preferred_element_type=jnp.float32,
        ).astype(jnp.bfloat16),
        "shard",
        scatter_dimension=0,
        tiled=True,
    ).astype(jnp.float32)
    grad_local, grad_gain, grad_shift = norm_back(grad_normed)
    grad_tokens = (cotangent.astype(jnp.float32) + grad_local).astype(jnp.bfloat16)
    bias_inner = jnp.sum(grad_inner_rows, axis=0, dtype=jnp.float32)
    grad_inner = jnp.einsum(
        "sd,sa->da", gathered, grad_inner_rows, preferred_element_type=jnp.float32
    )
    grad_gain, grad_shift, bias_out = lax.psum(
        (grad_gain, grad_shift, jnp.sum(cotangent, axis=0, dtype=jnp.float32)), ("shard", "replica")
    )
    grad_inner, bias_inner, grad_outer = (
        lax.psum(grad_inner.astype(jnp.bfloat16), "replica").astype(jnp.float32),
        lax.psum(bias_inner.astype(jnp.bfloat16), "replica").astype(jnp.float32),
        lax.psum(grad_outer.astype(jnp.bfloat16), "replica").astype(jnp.float32),
    )
    return (
        mixed_out[None],
        grad_tokens[None],
        grad_gain,
        grad_shift,
        grad_inner[:, :qkv_cols].reshape(model_width, 3, head_cols),
        bias_inner[:qkv_cols].reshape(3, head_cols),
        grad_inner[:, qkv_cols:],
        bias_inner[qkv_cols:],
        grad_outer[:head_cols],
        bias_out,
        grad_outer[head_cols:],
        bias_out,
    )


SEQ = 1024
TILE = 256
BF = jnp.bfloat16
F32 = jnp.float32
MESH = pl.DeviceIdType.MESH
NN = (((1,), (0,)), ((), ()))
NT = (((1,), (1,)), ((), ()))
TN = (((0,), (0,)), ((), ()))
CHUNKS = 48
LAG_NEAR = 2
LAG_FAR = 4
TICKS = CHUNKS + LAG_FAR + 2


def dot(left, right, dims):
    return lax.dot_general(left, right, dims, preferred_element_type=F32)


def span(index, size):
    return pl.ds(pl.multiple_of(index * size, size), size)


def fused(
    tok,
    gloc,
    gain,
    bias,
    wqkv_h,
    bqkv,
    wup_h,
    bup,
    wout_h,
    bout,
    wdown_h,
    bdown,
    cos_t,
    sin_t,
    seg_row,
    mixed_o,
    gtok_o,
    small_o,
    ztot,
    zown,
    znear,
    zfar,
    nf,
    gf,
    act,
    gp,
    qkv,
    att,
    dout,
    dqkv,
    dk_acc,
    dv_acc,
    q_acc,
    o_acc,
    wqkv,
    wup,
    wout,
    wdown,
    seg_col,
    stage,
    near_b,
    own_b,
    far_b,
    own2_b,
    near2_b,
    send_n,
    send_f,
    tot_b,
    small,
    small_in,
    small_z,
    gat_send,
    gat_recv,
    w_sem,
    stage_sem,
    load_sem,
    nsend_sem,
    fsend_sem,
    tot_sem,
    near_sem,
    far_sem,
    rs_send,
    rs_recv,
    sm_send,
    sm_recv,
    smz_send,
    smz_recv,
    ready,
):
    T, D = nf.shape
    R = tok.shape[0]
    FF = act.shape[1]
    half = R // 2
    s = lax.axis_index("shard")
    r = lax.axis_index("replica")
    core = lax.rem(s, 2)
    xb = lax.rem(s // 2, 2)
    yb = s // 4
    inner = (r == 1) | (r == 2)
    outer = (r == 0) | (r == 3)

    def other(mx, my, mc):
        cc = core + mc - 2 * core * mc
        xx = xb + mx - 2 * xb * mx
        yy = yb + my - 2 * yb * my
        return yy * 4 + xx * 2 + cc

    sib = other(0, 0, 1)
    xn = other(1, 0, 0)
    yn = other(0, 1, 0)
    diag = other(1, 1, 0)
    far_r = jnp.where(r == 0, 1, jnp.where(r == 1, 2, jnp.where(r == 2, 1, 2)))
    near_r = jnp.where(r == 1, 0, jnp.where(r == 2, 3, r))

    def dev(shard_id, rep_id=None):
        return (r if rep_id is None else rep_id, shard_id)

    def to(shard_id):
        return {"shard": shard_id, "replica": r}

    def to_rep(rep_id):
        return {"shard": s, "replica": rep_id}

    barrier = pltpu.get_barrier_semaphore()
    for peer in (sib, xn, yn):
        pl.semaphore_signal(barrier, inc=1, device_id=to(peer), device_id_type=MESH)
    for step in (1, 2, 3):
        pl.semaphore_signal(
            barrier, inc=1, device_id=to_rep(lax.rem(r + step, 4)), device_id_type=MESH
        )

    loads = [
        pltpu.make_async_copy(wup_h, wup, w_sem.at[0]),
        pltpu.make_async_copy(gloc, gf.at[span(s, R), :], w_sem.at[1]),
        pltpu.make_async_copy(wqkv_h, wqkv, w_sem.at[2]),
        pltpu.make_async_copy(wdown_h, wdown, w_sem.at[3]),
        pltpu.make_async_copy(wout_h, wout, w_sem.at[4]),
    ]
    for item in loads:
        item.start()

    LN_ROWS = 32

    def norm_rows(i):
        x = tok[span(i, LN_ROWS), :].astype(F32)
        centered = x - jnp.mean(x, axis=1, keepdims=True)
        inv = lax.rsqrt(jnp.mean(centered * centered, axis=1, keepdims=True) + EPSILON)
        return centered * inv, inv

    @pl.loop(0, R // LN_ROWS)
    def _(i):
        scaled, _ = norm_rows(i)
        rows = pl.ds(pl.multiple_of(s * R + i * LN_ROWS, LN_ROWS), LN_ROWS)
        nf[rows, :] = (scaled * gain[...] + bias[...]).astype(BF)

    pl.semaphore_wait(barrier, 6)

    def piece(buf, owner, h, cols):
        if h is None:
            return buf.at[span(owner, R), cols]
        rows = pl.ds(pl.multiple_of(owner * R + h * half, half), half)
        return buf.at[rows, cols]

    GATHER = {
        0: (lambda: s, 0, lambda: xn),
        1: (lambda: s, 1, lambda: xn),
        2: (lambda: yn, 1, lambda: xn),
        3: (lambda: s, 1, lambda: yn),
        4: (lambda: s, 0, lambda: yn),
        5: (lambda: xn, 0, lambda: yn),
        6: (lambda: s, None, lambda: sib),
        7: (lambda: xn, 0, lambda: sib),
        8: (lambda: yn, 1, lambda: sib),
        9: (lambda: xn, 1, lambda: sib),
        10: (lambda: yn, 0, lambda: sib),
        11: (lambda: diag, 0, lambda: sib),
        12: (lambda: diag, 1, lambda: sib),
    }

    def gcopy(buf, kind, slot, cols):
        owner, h, target = GATHER[kind]
        ref = piece(buf, owner(), h, cols)
        return pltpu.make_async_remote_copy(
            src_ref=ref,
            dst_ref=ref,
            send_sem=gat_send.at[slot, kind],
            recv_sem=gat_recv.at[slot, kind],
            device_id=to(target()),
            device_id_type=MESH,
        )

    every = pl.ds(0, D)

    def n_start(*kinds):
        for kind in kinds:
            gcopy(nf, kind, 8, every).start()

    def n_wait(*kinds):
        for kind in kinds:
            gcopy(nf, kind, 8, every).wait_recv()

    def g_start(j, *kinds):
        for kind in kinds:
            gcopy(gf, kind, j, span(j, TILE)).start()

    def g_wait(j, *kinds):
        for kind in kinds:
            gcopy(gf, kind, j, span(j, TILE)).wait_recv()

    OWN = (0, 3, 6, 1, 4)
    n_start(*OWN)

    C0 = math.sqrt(2.0 / math.pi)
    C1 = 0.044715

    def up_block(owner):
        rows = span(owner, R)

        @pl.loop(0, FF // TILE)
        def _(n):
            cols = span(n, TILE)
            u = dot(nf[rows, :], wup[:, cols], NN) + bup[:, cols]
            sq = u * u
            t = jnp.tanh(C0 * (u + C1 * (sq * u)))
            cdf = 0.5 + 0.5 * t
            act[rows, cols] = (u * cdf).astype(BF)
            gp[rows, cols] = (
                cdf + (0.5 * C0) * u * (1.0 - t * t) * (1.0 + (3.0 * C1) * sq)
            ).astype(BF)

    def rope(z, rows, sign):
        parts = []
        for p in range(2):
            zp = z[:, p * 128 : (p + 1) * 128]
            c = cos_t[rows, :]
            sn = sin_t[rows, :]
            turned = pltpu.roll(zp, 112, 1) * sn - pltpu.roll(zp * sn, 16, 1)
            parts.append(zp * c + sign * turned)
        return jnp.concatenate(parts, axis=1)

    def qkv_block(owner):
        rows = span(owner, R)
        for t in range(3):
            z = dot(nf[rows, :], wqkv[t], NN) + bqkv[t : t + 1, :]
            if t < 2:
                z = rope(z, rows, 1.0)
            z = z.astype(BF)
            if t == 0:
                z = (z.astype(F32) * (HEAD_DIM**-0.5)).astype(BF)
            qkv[t, rows, :] = z

    loads[0].wait()
    loads[1].wait()
    up_block(s)
    n_wait(6)
    up_block(sib)

    @pl.loop(0, T // TILE)
    def _(i):
        line = seg_row[:, span(i, TILE)].astype(F32)
        seg_col[span(i, TILE), :] = jnp.transpose(jnp.broadcast_to(line, (128, TILE)))

    n_wait(0)
    n_start(5, 7)
    n_wait(3)
    n_start(2, 8)
    g_start(0, *OWN)
    n_wait(1)
    n_start(9)
    n_wait(4)
    n_start(10)
    g_start(1, *OWN)
    n_wait(7, 8, 9, 10)

    @pl.loop(0, 2)
    def _(mc):
        up_block(other(1, 0, mc))
        up_block(other(0, 1, mc))

    n_wait(5)
    n_start(11)
    n_wait(2)
    n_start(12)
    g_wait(0, 0)
    g_start(0, 5, 7)
    g_wait(0, 3)
    g_start(0, 2, 8)
    g_wait(0, 1)
    g_start(0, 9)
    g_wait(0, 4)
    g_start(0, 10)
    n_wait(11, 12)

    @pl.loop(0, 2)
    def _(mc):
        up_block(other(1, 1, mc))

    for item in loads[2:]:
        item.wait()

    def near_send(c):
        return pltpu.make_async_remote_copy(
            src_ref=zown.at[c],
            dst_ref=znear.at[c],
            send_sem=nsend_sem.at[lax.rem(c, 2)],
            recv_sem=near_sem.at[c],
            device_id=to_rep(far_r),
            device_id_type=MESH,
        )

    def mid_send(c):
        return pltpu.make_async_remote_copy(
            src_ref=send_n.at[lax.rem(c, 2)],
            dst_ref=zfar.at[c],
            send_sem=nsend_sem.at[lax.rem(c, 2)],
            recv_sem=far_sem.at[c],
            device_id=to_rep(far_r),
            device_id_type=MESH,
        )

    def back_send(c):
        return pltpu.make_async_remote_copy(
            src_ref=send_f.at[lax.rem(c, 2)],
            dst_ref=zfar.at[c],
            send_sem=fsend_sem.at[lax.rem(c, 2)],
            recv_sem=far_sem.at[c],
            device_id=to_rep(near_r),
            device_id_type=MESH,
        )

    def tot_copy(c):
        return pltpu.make_async_copy(
            tot_b.at[lax.rem(c, 2)], ztot.at[c], tot_sem.at[lax.rem(c, 2)]
        )

    def load(src, dst, i):
        return pltpu.make_async_copy(src, dst, load_sem.at[i])

    def add_blocks(outs, ins):
        @pl.loop(0, 8)
        def _(i):
            rows = pl.ds(pl.multiple_of(lax.rem(i, 4) * 64, 64), 64)
            b = i // 4
            vals = [x[b, rows, :].astype(F32) for x in ins]
            for ref, which in outs:
                total = vals[which[0]]
                for w in which[1:]:
                    total = total + vals[w]
                ref[b, rows, :] = total.astype(BF)

    def within(c):
        return (c >= 0) & (c < CHUNKS)

    def tick(k):
        c1 = k - 1

        @pl.when(inner & within(c1))
        def _():
            load(znear.at[c1], near_b, 0).wait()
            load(zown.at[c1], own_b, 1).wait()

            @pl.when(c1 >= 2)
            def _():
                mid_send(c1 - 2).wait_send()

            add_blocks([(send_n.at[lax.rem(c1, 2)], (0, 1))], [near_b, own_b])
            mid_send(c1).start()

        c2 = k - 1 - LAG_NEAR

        @pl.when(inner & within(c2))
        def _():
            load(zfar.at[c2], far_b, 2).wait()
            load(zown.at[c2], own2_b, 3).wait()
            load(znear.at[c2], near2_b, 4).wait()

            @pl.when(c2 >= 2)
            def _():
                back_send(c2 - 2).wait_send()
                tot_copy(c2 - 2).wait()

            slot = lax.rem(c2, 2)
            add_blocks(
                [(send_f.at[slot], (0, 1)), (tot_b.at[slot], (0, 1, 2))],
                [far_b, own2_b, near2_b],
            )
            back_send(c2).start()
            tot_copy(c2).start()

        c3 = k - 1 - LAG_FAR

        @pl.when(outer & within(c3))
        def _():
            load(zfar.at[c3], far_b, 2).wait()
            load(zown.at[c3], own2_b, 3).wait()

            @pl.when(c3 >= 2)
            def _():
                tot_copy(c3 - 2).wait()

            add_blocks([(tot_b.at[lax.rem(c3, 2)], (0, 1))], [far_b, own2_b])
            tot_copy(c3).start()

        @pl.when(outer & within(k))
        def _():
            @pl.when(k >= 2)
            def _():
                near_send(k - 2).wait_send()

            near_send(k).start()

        @pl.when(inner & within(k))
        def _():
            near_send(k).wait_recv()
            load(znear.at[k], near_b, 0).start()
            load(zown.at[k], own_b, 1).start()

        c4 = k - LAG_NEAR

        @pl.when(inner & within(c4))
        def _():
            mid_send(c4).wait_recv()
            load(zfar.at[c4], far_b, 2).start()
            load(zown.at[c4], own2_b, 3).start()
            load(znear.at[c4], near2_b, 4).start()

        c5 = k - LAG_FAR

        @pl.when(outer & within(c5))
        def _():
            back_send(c5).wait_recv()
            load(zfar.at[c5], far_b, 2).start()
            load(zown.at[c5], own2_b, 3).start()

    def keep(slot, c):
        return pltpu.make_async_copy(stage.at[slot], zown.at[c], stage_sem.at[slot])

    small[...] = jnp.zeros_like(small)

    @pl.loop(0, D // TILE)
    def _(j):
        @pl.when(j + 2 < D // TILE)
        def _():
            g_start(j + 2, *OWN)

        @pl.when(j + 1 < D // TILE)
        def _():
            g_wait(j + 1, 0)
            g_start(j + 1, 5, 7)
            g_wait(j + 1, 3)
            g_start(j + 1, 2, 8)
            g_wait(j + 1, 1)
            g_start(j + 1, 9)
            g_wait(j + 1, 4)
            g_start(j + 1, 10)

        g_wait(j, 5)
        g_start(j, 11)
        g_wait(j, 2)
        g_start(j, 12)
        g_wait(j, 6, 7, 8, 9, 10, 11, 12)

        @pl.loop(0, FF // 512)
        def _(h):
            part = dot(act[:, span(h, 512)], gf[:, span(j, TILE)], TN)
            stage[h, 0] = part[:TILE].astype(BF)
            stage[h, 1] = part[TILE:].astype(BF)
            keep(h, 2 * j + h).start()

        keep(0, 2 * j).wait()
        keep(1, 2 * j + 1).wait()
        tick(j)
        qkv_block(j)

    tick0 = D // TILE

    @pl.loop(0, T // 512)
    def _(i):
        rows = span(i, 512)

        @pl.loop(0, FF // TILE)
        def _(n):
            cols = span(n, TILE)
            ga = dot(gf[rows, :], wdown[cols, :], NT)
            gu = (ga * gp[rows, cols].astype(F32)).astype(BF)
            gp[rows, cols] = gu
            at = pl.ds(pl.multiple_of(3 * TILE + n * TILE, TILE), TILE)
            small[3:4, at] += jnp.sum(gu.astype(F32), axis=0, keepdims=True)

        tick(tick0 + i)

    tick0 += T // 512

    @pl.loop(0, D // 512)
    def _(i):
        @pl.loop(0, 2)
        def _(b):
            at = 2 * i + b
            part = dot(nf[:, span(at, TILE)], gp[...], TN)
            for q in range(4):
                stage[2 * b + q // 2, q % 2] = part[:, q * TILE : (q + 1) * TILE].astype(BF)
            keep(2 * b, 16 + 2 * at).start()
            keep(2 * b + 1, 17 + 2 * at).start()

        for q in range(4):
            keep(q, 16 + 4 * i + q).wait()
        tick(tick0 + i)

    tick0 += D // 512

    @pl.loop(0, T // 512)
    def _(i):
        rows = span(i, 512)
        dout[rows, :] = dot(gf[rows, :], wout[...], NT).astype(BF)

    tick(tick0)
    tick0 += 1

    HC = qkv.shape[2]
    heads = HC // HEAD_DIM
    blocks = SEQ // TILE

    def attend(seq, qb, h):
        base = seq * SEQ
        kmax = (qb + 1) * TILE
        qrows = pl.ds(pl.multiple_of(base + qb * TILE, TILE), TILE)
        krows = pl.ds(pl.multiple_of(base, SEQ), kmax)
        keep_lane = jnp.where(
            lax.broadcasted_iota(jnp.int32, (TILE, HC), 1) // HEAD_DIM == h, 1.0, 0.0
        )
        qh = (qkv[0, qrows, :].astype(F32) * keep_lane).astype(BF)
        doh32 = dout[qrows, :].astype(F32) * keep_lane
        doh = doh32.astype(BF)
        keys = qkv[1, krows, :]
        vals = qkv[2, krows, :]
        scores = dot(qh, keys, NT)
        allowed = (seg_col[qrows, 0:1] == seg_row[:, krows].astype(F32)) & (
            lax.broadcasted_iota(jnp.int32, (TILE, kmax), 1)
            <= lax.broadcasted_iota(jnp.int32, (TILE, kmax), 0) + qb * TILE
        )
        scores = jnp.where(allowed, scores, NEGATIVE)
        weights = jnp.exp(scores - jnp.max(scores, axis=1, keepdims=True))
        probs = weights * (1.0 / jnp.sum(weights, axis=1, keepdims=True))
        probs_low = probs.astype(BF)
        out = dot(probs_low, vals, NN) * keep_lane
        o_acc[...] += out
        delta = jnp.sum(doh32 * out, axis=1, keepdims=True)
        dprobs = dot(doh, vals, NT)
        ds = (probs * (dprobs - delta)).astype(BF)
        q_acc[...] += dot(ds, keys, NN) * keep_lane
        dk_acc[0:kmax, :] += dot(ds, qh, TN)
        dv_acc[0:kmax, :] += dot(probs_low, doh, TN)

    TICKS_OF = (1, 1, 2, 2)
    per_seq = sum(TICKS_OF)

    @pl.loop(0, T // SEQ)
    def _(seq):
        dk_acc[...] = jnp.zeros_like(dk_acc)
        dv_acc[...] = jnp.zeros_like(dv_acc)
        passed = 0
        for qb in range(blocks):
            n = TICKS_OF[qb]
            q_acc[...] = jnp.zeros_like(q_acc)
            o_acc[...] = jnp.zeros_like(o_acc)

            @pl.loop(0, n)
            def _(part):
                @pl.loop(0, heads // n)
                def _(h):
                    attend(seq, qb, part * (heads // n) + h)

                tick(tick0 + seq * per_seq + passed + part)

            passed += n
            qrows = pl.ds(pl.multiple_of(seq * SEQ + qb * TILE, TILE), TILE)
            att[qrows, :] = o_acc[...].astype(BF)
            dq = rope(q_acc[...] * (HEAD_DIM**-0.5), qrows, -1.0).astype(BF)
            dqkv[0, qrows, :] = dq
            small[3:4, 0:TILE] += jnp.sum(dq.astype(F32), axis=0, keepdims=True)

        @pl.loop(0, blocks)
        def _(b):
            rows = pl.ds(pl.multiple_of(seq * SEQ + b * TILE, TILE), TILE)
            dk = rope(dk_acc[span(b, TILE), :], rows, -1.0).astype(BF)
            dv = dv_acc[span(b, TILE), :].astype(BF)
            dqkv[1, rows, :] = dk
            dqkv[2, rows, :] = dv
            small[3:4, TILE : 2 * TILE] += jnp.sum(dk.astype(F32), axis=0, keepdims=True)
            small[3:4, 2 * TILE : 3 * TILE] += jnp.sum(
                dv.astype(F32), axis=0, keepdims=True
            )

    tick0 += (T // SEQ) * per_seq

    @pl.loop(0, 4)
    def _(i):
        part = dot(att[...], gf[:, span(i, 512)], TN)
        stage[i, 0] = part[:, :TILE].astype(BF)
        stage[i, 1] = part[:, TILE:].astype(BF)
        keep(i, 32 + i).start()

    for q in range(4):
        keep(q, 32 + q).wait()
    tick(tick0)
    tick0 += 1

    @pl.loop(0, 3)
    def _(t):
        @pl.loop(0, 4)
        def _(i):
            part = dot(nf[:, span(i, 512)], dqkv[t], TN)
            stage[i, 0] = part[:TILE].astype(BF)
            stage[i, 1] = part[TILE:].astype(BF)
            keep(i, 36 + 4 * t + i).start()

        for q in range(4):
            keep(q, 36 + 4 * t + q).wait()
        tick(tick0 + t)

    tick0 += 3

    for kind in range(13):
        gcopy(nf, kind, 8, every).wait_send()

    @pl.loop(0, D // TILE)
    def _(j):
        for kind in range(13):
            gcopy(gf, kind, j, span(j, TILE)).wait_send()

    for peer in (sib, xn, yn):
        pl.semaphore_signal(ready, inc=1, device_id=to(peer), device_id_type=MESH)
    pl.semaphore_wait(ready, 3)

    CHIPS = ((1, 1), (1, 0), (0, 1), (0, 0))

    def reduce_rows(which, product, buf, tick0):
        stages = (gf, nf)

        def blk(b, h=None):
            if h is None:
                return buf.at[b * R : (b + 1) * R, :]
            return buf.at[b * R + h * half : b * R + (h + 1) * half, :]

        def send(kind, src, dst, target):
            return pltpu.make_async_remote_copy(
                src_ref=src,
                dst_ref=dst,
                send_sem=rs_send.at[which, kind],
                recv_sem=rs_recv.at[which, kind],
                device_id=to(target),
                device_id_type=MESH,
            )

        def to_sib(i):
            return send(i, stages[i % 2].at[0:R, :], blk(1 + i), sib)

        steps = {
            4: lambda: send(4, blk(1, 0), blk(5, 0), xn),
            5: lambda: send(5, blk(1, 1), blk(5, 1), yn),
            6: lambda: send(6, blk(2, 0), blk(6, 0), xn),
            7: lambda: send(7, blk(3, 1), blk(6, 1), yn),
            8: lambda: send(8, blk(3, 0), blk(7, 0), yn),
            9: lambda: send(9, blk(2, 1), blk(7, 1), xn),
        }

        def sib_part(i):
            if i >= 2:
                to_sib(i - 2).wait_send()
            mx, my = CHIPS[i]
            rows = span(other(mx, my, 1), R)
            ref = stages[i % 2]

            @pl.loop(0, D // TILE)
            def _(n):
                ref[0:R, span(n, TILE)] = product(rows, n).astype(BF)

            to_sib(i).start()

        def own_part(i):
            mx, my = CHIPS[i]
            rows = span(other(mx, my, 0), R)
            to_sib(i).wait_recv()

            @pl.loop(0, D // TILE)
            def _(n):
                cols = span(n, TILE)
                total = product(rows, n) + buf[(1 + i) * R : (2 + i) * R, cols].astype(F32)
                buf[(1 + i) * R : (2 + i) * R, cols] = total.astype(BF)

        def add_half(dst, src):
            (db, dh), (sb, sh) = dst, src

            @pl.loop(0, half // 32)
            def _(i):
                a = pl.ds(pl.multiple_of(db * R + dh * half + i * 32, 32), 32)
                b = pl.ds(pl.multiple_of(sb * R + sh * half + i * 32, 32), 32)
                buf[a, :] = (buf[a, :].astype(F32) + buf[b, :].astype(F32)).astype(BF)

        sib_part(0)
        tick(tick0)
        sib_part(1)
        tick(tick0 + 1)
        own_part(0)
        steps[4]().start()
        steps[5]().start()
        tick(tick0 + 2)
        sib_part(2)
        tick(tick0 + 3)
        own_part(1)
        steps[6]().start()
        tick(tick0 + 4)
        sib_part(3)
        tick(tick0 + 5)
        own_part(2)
        steps[7]().start()
        steps[4]().wait_recv()
        add_half((3, 0), (5, 0))
        steps[8]().start()
        steps[5]().wait_recv()
        add_half((2, 1), (5, 1))
        steps[9]().start()
        tick(tick0 + 6)
        own_part(3)
        tick(tick0 + 7)
        for i in (2, 3):
            to_sib(i).wait_send()

        def finish():
            for kind in (6, 7, 8, 9):
                steps[kind]().wait_recv()

        def drain():
            for kind in range(4, 10):
                steps[kind]().wait_send()

        def total_rows(i):
            at = [
                pl.ds(pl.multiple_of(b * R + i * LN_ROWS, LN_ROWS), LN_ROWS) for b in (4, 6, 7)
            ]
            return sum(buf[a, :].astype(F32) for a in at)

        return finish, drain, total_rows

    def inner_product(rows, n):
        cols = span(n, TILE)
        total = dot(gp[rows, :], wup[cols, :], NT)
        for t in range(3):
            total = total + dot(dqkv[t, rows, :], wqkv[t, cols, :], NT)
        return total

    def outer_product(rows, n):
        cols = span(n, TILE)
        return dot(act[rows, :], wdown[:, cols], NN) + dot(att[rows, :], wout[:, cols], NN)

    finish2, drain2, rows2 = reduce_rows(0, inner_product, gf, tick0)
    tick0 += 8
    finish1, drain1, rows1 = reduce_rows(1, outer_product, nf, tick0)
    tick0 += 8

    finish2()

    @pl.loop(0, R // LN_ROWS)
    def _(i):
        rows = span(i, LN_ROWS)
        scaled, inv = norm_rows(i)
        gn = rows2(i)
        cot = gloc[rows, :].astype(F32)
        g = gn * gain[...]
        back = g - jnp.mean(g, axis=1, keepdims=True)
        back = back - scaled * jnp.mean(g * scaled, axis=1, keepdims=True)
        gtok_o[rows, :] = (cot + back * inv).astype(BF)
        small[0:1, :] += jnp.sum(gn * scaled, axis=0, keepdims=True)
        small[1:2, :] += jnp.sum(gn, axis=0, keepdims=True)
        small[2:3, :] += jnp.sum(cot, axis=0, keepdims=True)

    tick(tick0)
    tick0 += 1

    for step, peer in enumerate((sib, xn, yn)):
        copy = pltpu.make_async_remote_copy(
            src_ref=small,
            dst_ref=small_in.at[step],
            send_sem=sm_send.at[step],
            recv_sem=sm_recv.at[step],
            device_id=to(peer),
            device_id_type=MESH,
        )
        copy.start()
        copy.wait()
        small[0:3, :] += small_in[step, 0:3, :]
        if step == 1:
            tick(tick0)
            tick0 += 1

    for step in (1, 2, 3):
        pltpu.make_async_remote_copy(
            src_ref=small,
            dst_ref=small_z.at[step - 1],
            send_sem=smz_send.at[step - 1],
            recv_sem=smz_recv.at[step - 1],
            device_id=to_rep(lax.rem(r + step, 4)),
            device_id_type=MESH,
        ).start()

    finish1()

    @pl.loop(0, R // LN_ROWS)
    def _(i):
        rows = span(i, LN_ROWS)
        total = tok[rows, :].astype(F32) + rows1(i) + bout[...] + bdown[...]
        mixed_o[rows, :] = total.astype(BF)

    drain2()
    drain1()

    for step in (1, 2, 3):
        pltpu.make_async_remote_copy(
            src_ref=small,
            dst_ref=small_z.at[step - 1],
            send_sem=smz_send.at[step - 1],
            recv_sem=smz_recv.at[step - 1],
            device_id=to_rep(lax.rem(r + step, 4)),
            device_id_type=MESH,
        ).wait()
    small_o[...] = small[...] + small_z[0] + small_z[1] + small_z[2]

    @pl.loop(tick0, TICKS)
    def _(k):
        tick(k)

    for c in (CHUNKS - 2, CHUNKS - 1):
        tot_copy(c).wait()

        @pl.when(outer)
        def _():
            near_send(c).wait_send()

        @pl.when(inner)
        def _():
            mid_send(c).wait_send()
            back_send(c).wait_send()


def rope_tables(positions):
    cosine, sine = angles(positions)
    rest = HEAD_DIM - ROT
    length = cosine.shape[0]
    cos_t = jnp.concatenate([cosine, cosine, jnp.ones((length, rest), F32)], axis=1)
    sin_t = jnp.concatenate([-sine, jnp.zeros((length, rest + ROT // 2), F32)], axis=1)
    return jnp.tile(cos_t, (1, 2)), jnp.tile(sin_t, (1, 2))


def fused_body(
    tokens,
    segments,
    positions,
    ln_gain,
    ln_bias,
    w_qkv,
    b_qkv,
    w_up,
    b_up,
    w_out,
    b_out,
    w_down,
    b_down,
    grad_out,
):
    _, R, D = tokens.shape
    T = R * lax.axis_size("shard")
    HC = w_qkv.shape[2]
    FF = w_up.shape[1]
    cos_t, sin_t = rope_tables(positions[0])
    vmem = pl.BlockSpec(memory_space=pltpu.VMEM)
    hbm = pl.BlockSpec(memory_space=pl.ANY)
    block = (CHUNKS, 2, TILE, TILE)
    piece = (2, TILE, TILE)
    out_shape = (
        jax.ShapeDtypeStruct((R, D), BF),
        jax.ShapeDtypeStruct((R, D), BF),
        jax.ShapeDtypeStruct((8, D), F32),
        jax.ShapeDtypeStruct(block, BF),
        jax.ShapeDtypeStruct(block, BF),
        jax.ShapeDtypeStruct(block, BF),
        jax.ShapeDtypeStruct(block, BF),
    )
    dma = pltpu.SemaphoreType.DMA
    scratch = [
        pltpu.VMEM((T, D), BF),
        pltpu.VMEM((T, D), BF),
        pltpu.VMEM((T, FF), BF),
        pltpu.VMEM((T, FF), BF),
        pltpu.VMEM((3, T, HC), BF),
        pltpu.VMEM((T, HC), BF),
        pltpu.VMEM((T, HC), BF),
        pltpu.VMEM((3, T, HC), BF),
        pltpu.VMEM((SEQ, HC), F32),
        pltpu.VMEM((SEQ, HC), F32),
        pltpu.VMEM((TILE, HC), F32),
        pltpu.VMEM((TILE, HC), F32),
        pltpu.VMEM((3, D, HC), BF),
        pltpu.VMEM((D, FF), BF),
        pltpu.VMEM((HC, D), BF),
        pltpu.VMEM((FF, D), BF),
        pltpu.VMEM((T, 128), F32),
        pltpu.VMEM((4,) + piece, BF),
        pltpu.VMEM(piece, BF),
        pltpu.VMEM(piece, BF),
        pltpu.VMEM(piece, BF),
        pltpu.VMEM(piece, BF),
        pltpu.VMEM(piece, BF),
        pltpu.VMEM((2,) + piece, BF),
        pltpu.VMEM((2,) + piece, BF),
        pltpu.VMEM((2,) + piece, BF),
        pltpu.VMEM((8, D), F32),
        pltpu.VMEM((3, 8, D), F32),
        pltpu.VMEM((3, 8, D), F32),
        dma((9, 13)),
        dma((9, 13)),
        dma((5,)),
        dma((4,)),
        dma((5,)),
        dma((2,)),
        dma((2,)),
        dma((2,)),
        dma((CHUNKS,)),
        dma((CHUNKS,)),
        dma((2, 10)),
        dma((2, 10)),
        dma((3,)),
        dma((3,)),
        dma((3,)),
        dma((3,)),
        pltpu.SemaphoreType.REGULAR,
    ]
    mixed, gtok, small, ztot, _, _, _ = pl.pallas_call(
        fused,
        out_shape=out_shape,
        in_specs=[vmem] * 4 + [hbm, vmem, hbm, vmem, hbm, vmem, hbm] + [vmem] * 4,
        out_specs=(vmem, vmem, vmem, hbm, hbm, hbm, hbm),
        scratch_shapes=scratch,
        name="layer",
        compiler_params=pltpu.CompilerParams(
            collective_id=0, has_side_effects=True, vmem_limit_bytes=VMEM_BYTES
        ),
    )(
        tokens[0],
        grad_out[0],
        ln_gain[None],
        ln_bias[None],
        jnp.transpose(w_qkv, (1, 0, 2)),
        b_qkv,
        w_up,
        b_up[None],
        w_out,
        b_out[None],
        w_down,
        b_down[None],
        cos_t,
        sin_t,
        segments,
    )
    grads = ztot.astype(F32)
    g_down = grads[:16].reshape(8, 2, 2, TILE, TILE).transpose(1, 2, 3, 0, 4).reshape(FF, D)
    g_up = grads[16:32].reshape(8, 4, TILE, TILE).transpose(0, 2, 1, 3).reshape(D, FF)
    g_out = grads[32:36].reshape(8, TILE, TILE).transpose(1, 0, 2).reshape(HC, D)
    g_qkv = grads[36:].reshape(3, D, HC).transpose(1, 0, 2)
    bias_inner = small[3]
    return (
        mixed[None],
        gtok[None],
        small[0],
        small[1],
        g_qkv,
        bias_inner[: 3 * HC].reshape(3, HC),
        g_up,
        bias_inner[3 * HC : 3 * HC + FF],
        g_out,
        small[2],
        g_down,
        small[2],
    )


def fits_fused(mesh):
    return dict(mesh.shape) == {"shard": 8, "replica": 4}


def solution(mesh):
    placed = (
        P("replica", "shard", None),
        P("replica", None),
        P("replica", None),
        P(),
        P(),
        P(None, None, "shard"),
        P(None, "shard"),
        P(None, "shard"),
        P("shard"),
        P("shard", None),
        P(),
        P("shard", None),
        P(),
        P("replica", "shard", None),
    )
    return jax.shard_map(
        fused_body if fits_fused(mesh) else body,
        mesh=mesh,
        in_specs=placed,
        out_specs=(
            P("replica", "shard", None),
            P("replica", "shard", None),
            P(),
            P(),
            P(None, None, "shard"),
            P(None, "shard"),
            P(None, "shard"),
            P("shard"),
            P("shard", None),
            P(),
            P("shard", None),
            P(),
        ),
        check_vma=False,
    )
```

```python
import contextlib
import functools
import math

import jax
import jax.numpy as jnp
import numpy as np
from jax import lax
from jax.experimental import pallas as pl
from jax.experimental.pallas import tpu as pltpu
from jax.sharding import PartitionSpec as P

HEAD_DIM = 64
ROT = 32


EPSILON = 1e-05
NEGATIVE = -1e30
VMEM_BYTES = 64 * 1024 * 1024


def angles(positions):
    frequency = jnp.exp(jnp.arange(ROT // 2, dtype=jnp.float32) * (-2.0 * math.log(10000.0) / ROT))
    phase_angle = positions.astype(jnp.float32)[:, None] * frequency[None, :]
    return (jnp.cos(phase_angle), jnp.sin(phase_angle))


def rotate(heads_in, cosine_part, sine_part):
    half_rot = ROT // 2
    first_part = heads_in[..., :half_rot]
    second_part = heads_in[..., half_rot:ROT]
    cosine_rows = cosine_part[:, None, :]
    sine_rows = sine_part[:, None, :]
    return jnp.concatenate(
        [
            first_part * cosine_rows - second_part * sine_rows,
            second_part * cosine_rows + first_part * sine_rows,
            heads_in[..., ROT:],
        ],
        axis=-1,
    )


def layer_norm(token_rows, gain_vector, bias_vector):
    centered = token_rows - jnp.mean(token_rows, axis=1, keepdims=True)
    scaled = centered * lax.rsqrt(jnp.mean(centered * centered, axis=1, keepdims=True) + EPSILON)
    return scaled * gain_vector + bias_vector


def take_rows(array_in, row_start, row_count):
    return lax.dynamic_slice_in_dim(array_in, row_start, row_count, 0)


def body(
    tokens,
    segments,
    positions,
    ln_gain,
    ln_bias,
    w_qkv,
    b_qkv,
    w_up,
    b_up,
    w_out,
    b_out,
    w_down,
    b_down,
    grad_out,
):
    local_rows = tokens[0].astype(jnp.float32)
    tok_rows, model_width = local_rows.shape
    length = tok_rows * lax.axis_size("shard")
    head_cols = w_qkv.shape[2]
    heads_here = head_cols // HEAD_DIM
    qkv_cols = 3 * head_cols
    split_shape = (length, heads_here, HEAD_DIM)
    scale_factor = HEAD_DIM ** (-0.5)
    cosine_part, sine_part = angles(positions[0])
    seq_segments = segments[0]
    normed_full, norm_back = jax.vjp(layer_norm, local_rows, ln_gain, ln_bias)
    normed = normed_full.astype(jnp.bfloat16)
    w_inner = jnp.concatenate([w_qkv.reshape(model_width, qkv_cols), w_up], axis=1)
    b_inner = jnp.concatenate([b_qkv.reshape(qkv_cols), b_up])
    gathered = lax.all_gather(normed, "shard", axis=0, tiled=True)
    inner_proj = jnp.dot(gathered, w_inner, preferred_element_type=jnp.float32)
    inner_proj = inner_proj + b_inner
    queries = rotate(inner_proj[:, :head_cols].reshape(split_shape), cosine_part, sine_part).astype(
        jnp.bfloat16
    )
    keys_all = rotate(
        inner_proj[:, head_cols : 2 * head_cols].reshape(split_shape), cosine_part, sine_part
    ).astype(jnp.bfloat16)
    values_all = inner_proj[:, 2 * head_cols : qkv_cols].reshape(split_shape).astype(jnp.bfloat16)
    up_proj = inner_proj[:, qkv_cols:]
    activation = jax.nn.gelu(up_proj, approximate=True).astype(jnp.bfloat16)
    block_rows = math.gcd(length, 512)
    block_count = length // block_rows
    offsets_block = jnp.arange(block_rows, dtype=jnp.int32)

    def block_scores(query_block, key_block, query_start, key_start):
        scores = (
            jnp.einsum("qhe,khe->hqk", query_block, key_block, preferred_element_type=jnp.float32)
            * scale_factor
        )
        query_ids = query_start + offsets_block
        key_ids = key_start + offsets_block
        query_segs = take_rows(seq_segments, query_start, block_rows)
        key_segs = take_rows(seq_segments, key_start, block_rows)
        allowed = (query_ids[:, None] >= key_ids[None, :]) & (
            query_segs[:, None] == key_segs[None, :]
        )
        return jnp.where(allowed[None], scores, NEGATIVE)

    def attend(query_index):
        query_start = query_index * block_rows
        query_block = take_rows(queries, query_start, block_rows)

        def first_pass(key_index, row_stats):
            row_max, row_sum = row_stats
            key_start = key_index * block_rows
            scores = block_scores(
                query_block, take_rows(keys_all, key_start, block_rows), query_start, key_start
            )
            new_max = jnp.maximum(row_max, jnp.max(scores, axis=2))
            row_sum = row_sum * jnp.exp(row_max - new_max) + jnp.sum(
                jnp.exp(scores - new_max[:, :, None]), axis=2
            )
            return (new_max, row_sum)

        row_max, row_sum = lax.fori_loop(
            0,
            query_index + 1,
            first_pass,
            (
                jnp.full((heads_here, block_rows), NEGATIVE, jnp.float32),
                jnp.zeros((heads_here, block_rows), jnp.float32),
            ),
        )

        def second_pass(key_index, total_out):
            key_start = key_index * block_rows
            scores = block_scores(
                query_block, take_rows(keys_all, key_start, block_rows), query_start, key_start
            )
            probability = (jnp.exp(scores - row_max[:, :, None]) / row_sum[:, :, None]).astype(
                jnp.bfloat16
            )
            return total_out + jnp.einsum(
                "hqk,khe->qhe",
                probability,
                take_rows(values_all, key_start, block_rows),
                preferred_element_type=jnp.float32,
            )

        attended_block = lax.fori_loop(
            0,
            query_index + 1,
            second_pass,
            jnp.zeros((block_rows, heads_here, HEAD_DIM), jnp.float32),
        )
        return (attended_block, row_max, row_sum)

    attended_full, row_maxes, row_sums = lax.map(attend, jnp.arange(block_count, dtype=jnp.int32))
    attended_full = attended_full.reshape(length, head_cols)
    attended = attended_full.astype(jnp.bfloat16)
    outer_act = jnp.concatenate([attended, activation], axis=1)
    w_outer = jnp.concatenate([w_out, w_down], axis=0)
    branches = lax.psum_scatter(
        jnp.dot(
            take_rows(outer_act, jnp.int32(0), lax.axis_size("shard") * tok_rows),
            w_outer,
            preferred_element_type=jnp.float32,
        ).astype(jnp.bfloat16),
        "shard",
        scatter_dimension=0,
        tiled=True,
    ).astype(jnp.float32)
    mixed_out = (local_rows + branches + b_out + b_down).astype(jnp.bfloat16)
    cotangent = grad_out[0]
    shard_piece = lax.all_gather(cotangent, "shard", axis=0, tiled=True)
    act_rows = take_rows(outer_act, jnp.int32(0), shard_piece.shape[0])
    weight_sum = jnp.einsum("sa,sd->ad", act_rows, shard_piece, preferred_element_type=jnp.float32)
    back_rows = jnp.einsum("sd,ad->sa", shard_piece, w_outer, preferred_element_type=jnp.float32)
    grad_outer = weight_sum
    back_attended = back_rows[:, :head_cols].astype(jnp.bfloat16).reshape(split_shape)
    delta_all = jnp.sum(
        back_attended.astype(jnp.float32) * attended_full.reshape(split_shape), axis=2
    ).T

    def key_pass(key_index, grads_all):
        grad_query, grad_key, grad_value = grads_all
        key_start = key_index * block_rows
        key_block = take_rows(keys_all, key_start, block_rows)
        value_block = take_rows(values_all, key_start, block_rows)

        def query_pass(query_index, inner_state):
            grad_query, key_total, value_total = inner_state
            query_start = query_index * block_rows
            query_block = take_rows(queries, query_start, block_rows)
            back_block = take_rows(back_attended, query_start, block_rows)
            delta_block = lax.dynamic_slice_in_dim(delta_all, query_start, block_rows, 1)
            scores = block_scores(query_block, key_block, query_start, key_start)
            probability = (
                jnp.exp(scores - row_maxes[query_index][:, :, None])
                / row_sums[query_index][:, :, None]
            )
            grad_prob = jnp.einsum(
                "qhe,khe->hqk", back_block, value_block, preferred_element_type=jnp.float32
            )
            grad_scores = (probability * (grad_prob - delta_block[:, :, None])).astype(jnp.bfloat16)
            value_total = value_total + jnp.einsum(
                "hqk,qhe->khe",
                probability.astype(jnp.bfloat16),
                back_block,
                preferred_element_type=jnp.float32,
            )
            key_total = key_total + jnp.einsum(
                "hqk,qhe->khe", grad_scores, query_block, preferred_element_type=jnp.float32
            )
            query_rows = take_rows(grad_query, query_start, block_rows) + jnp.einsum(
                "hqk,khe->qhe", grad_scores, key_block, preferred_element_type=jnp.float32
            )
            grad_query = lax.dynamic_update_slice_in_dim(grad_query, query_rows, query_start, 0)
            return (grad_query, key_total, value_total)

        empty_block = jnp.zeros((block_rows, heads_here, HEAD_DIM), jnp.float32)
        grad_query, key_total, value_total = lax.fori_loop(
            key_index, block_count, query_pass, (grad_query, empty_block, empty_block)
        )
        grad_key = lax.dynamic_update_slice_in_dim(grad_key, key_total, key_start, 0)
        grad_value = lax.dynamic_update_slice_in_dim(grad_value, value_total, key_start, 0)
        return (grad_query, grad_key, grad_value)

    empty_all = jnp.zeros(split_shape, jnp.float32)
    grad_query, grad_key, grad_value = lax.fori_loop(
        0, block_count, key_pass, (empty_all, empty_all, empty_all)
    )
    grad_query = rotate(grad_query * scale_factor, cosine_part, -sine_part)
    grad_key = rotate(grad_key * scale_factor, cosine_part, -sine_part)
    _, gelu_back = jax.vjp(functools.partial(jax.nn.gelu, approximate=True), up_proj)
    grad_up = gelu_back(back_rows[:, head_cols:])[0]
    grad_inner_rows = jnp.concatenate(
        [
            grad_query.reshape(length, head_cols),
            grad_key.reshape(length, head_cols),
            grad_value.reshape(length, head_cols),
            grad_up,
        ],
        axis=1,
    ).astype(jnp.bfloat16)
    grad_normed = lax.psum_scatter(
        jnp.einsum(
            "sa,da->sd",
            take_rows(grad_inner_rows, jnp.int32(0), lax.axis_size("shard") * tok_rows),
            w_inner,
            preferred_element_type=jnp.float32,
        ).astype(jnp.bfloat16),
        "shard",
        scatter_dimension=0,
        tiled=True,
    ).astype(jnp.float32)
    grad_local, grad_gain, grad_shift = norm_back(grad_normed)
    grad_tokens = (cotangent.astype(jnp.float32) + grad_local).astype(jnp.bfloat16)
    bias_inner = jnp.sum(grad_inner_rows, axis=0, dtype=jnp.float32)
    grad_inner = jnp.einsum(
        "sd,sa->da", gathered, grad_inner_rows, preferred_element_type=jnp.float32
    )
    grad_gain, grad_shift, bias_out = lax.psum(
        (grad_gain, grad_shift, jnp.sum(cotangent, axis=0, dtype=jnp.float32)), ("shard", "replica")
    )
    grad_inner, bias_inner, grad_outer = (
        lax.psum(grad_inner.astype(jnp.bfloat16), "replica").astype(jnp.float32),
        lax.psum(bias_inner.astype(jnp.bfloat16), "replica").astype(jnp.float32),
        lax.psum(grad_outer.astype(jnp.bfloat16), "replica").astype(jnp.float32),
    )
    return (
        mixed_out[None],
        grad_tokens[None],
        grad_gain,
        grad_shift,
        grad_inner[:, :qkv_cols].reshape(model_width, 3, head_cols),
        bias_inner[:qkv_cols].reshape(3, head_cols),
        grad_inner[:, qkv_cols:],
        bias_inner[qkv_cols:],
        grad_outer[:head_cols],
        bias_out,
        grad_outer[head_cols:],
        bias_out,
    )


SEQ = 1024
TILE = 256
BF = jnp.bfloat16
F32 = jnp.float32
SUM = jnp.bfloat16
MESH = pl.DeviceIdType.MESH
NN = (((1,), (0,)), ((), ()))
NT = (((1,), (1,)), ((), ()))
TN = (((0,), (0,)), ((), ()))
CHUNKS = 48
RING = 3
LAG_INNER = 1
LAG_OUTER = 3
TICKS = CHUNKS + LAG_OUTER


def dot(left, right, dims):
    return lax.dot_general(left, right, dims, preferred_element_type=F32)


def span(index, size):
    return pl.ds(pl.multiple_of(index * size, size), size)


def fused(
    tok,
    gloc,
    gain,
    bias,
    wqkv_h,
    bqkv,
    wup_h,
    bup,
    wout_h,
    bout,
    wdown_h,
    bdown,
    seg_row,
    pos_row,
    freq,
    mixed_o,
    gtok_o,
    small_o,
    down_o,
    up_o,
    out_o,
    qkv_o,
    zown,
    nf,
    gf,
    act,
    gp,
    qkv,
    att,
    dout,
    dqkv,
    dk_acc,
    dv_acc,
    q_acc,
    o_acc,
    wqkv,
    wup,
    wout,
    wdown,
    cos_t,
    sin_t,
    seg_col,
    stage,
    near_b,
    far_b,
    own_b,
    send_n,
    send_f,
    tot_b,
    small,
    small_in,
    small_z,
    gat_send,
    gat_recv,
    w_sem,
    stage_sem,
    load_sem,
    nsend_sem,
    fsend_sem,
    tot_sem,
    near_sem,
    far_sem,
    rs_send,
    rs_recv,
    sm_send,
    sm_recv,
    smz_send,
    smz_recv,
    ready,
    credit,
):
    T, D = nf.shape
    R = tok.shape[0]
    FF = act.shape[1]
    half = R // 2
    s = lax.axis_index("shard")
    r = lax.axis_index("replica")
    core = lax.rem(s, 2)
    xb = lax.rem(s // 2, 2)
    yb = s // 4
    inner = (r == 1) | (r == 2)
    outer = (r == 0) | (r == 3)

    def other(mx, my, mc):
        cc = core + mc - 2 * core * mc
        xx = xb + mx - 2 * xb * mx
        yy = yb + my - 2 * yb * my
        return yy * 4 + xx * 2 + cc

    sib = other(0, 0, 1)
    xn = other(1, 0, 0)
    yn = other(0, 1, 0)
    diag = other(1, 1, 0)
    far_r = jnp.where(r == 0, 1, jnp.where(r == 1, 2, jnp.where(r == 2, 1, 2)))
    near_r = jnp.where(r == 1, 0, jnp.where(r == 2, 3, r))

    def to(shard_id):
        return {"shard": shard_id, "replica": r}

    def to_rep(rep_id):
        return {"shard": s, "replica": rep_id}

    scope = contextlib.ExitStack()

    def part(name):
        scope.close()
        scope.enter_context(jax.named_scope(name))

    part("norm")
    barrier = pltpu.get_barrier_semaphore()
    for peer in (sib, xn, yn):
        pl.semaphore_signal(barrier, inc=1, device_id=to(peer), device_id_type=MESH)
    for step in (1, 2, 3):
        pl.semaphore_signal(
            barrier, inc=1, device_id=to_rep(lax.rem(r + step, 4)), device_id_type=MESH
        )

    loads = [
        pltpu.make_async_copy(wup_h, wup, w_sem.at[0]),
        pltpu.make_async_copy(gloc, gf.at[span(s, R), :], w_sem.at[1]),
        pltpu.make_async_copy(wqkv_h, wqkv, w_sem.at[2]),
        pltpu.make_async_copy(wdown_h, wdown, w_sem.at[3]),
        pltpu.make_async_copy(wout_h, wout, w_sem.at[4]),
    ]
    for item in loads:
        item.start()

    LN_ROWS = 32

    def norm_rows(i):
        x = tok[span(i, LN_ROWS), :].astype(F32)
        centered = x - jnp.mean(x, axis=1, keepdims=True)
        inv = lax.rsqrt(jnp.mean(centered * centered, axis=1, keepdims=True) + EPSILON)
        return centered * inv, inv

    @pl.loop(0, R // LN_ROWS)
    def _(i):
        scaled, _ = norm_rows(i)
        rows = pl.ds(pl.multiple_of(s * R + i * LN_ROWS, LN_ROWS), LN_ROWS)
        nf[rows, :] = (scaled * gain[...] + bias[...]).astype(BF)

    pl.semaphore_wait(barrier, 6)

    def piece(buf, owner, h, cols):
        if h is None:
            return buf.at[span(owner, R), cols]
        rows = pl.ds(pl.multiple_of(owner * R + h * half, half), half)
        return buf.at[rows, cols]

    GATHER = {
        0: (lambda: s, 0, lambda: xn),
        1: (lambda: s, 1, lambda: xn),
        2: (lambda: yn, 1, lambda: xn),
        3: (lambda: s, 1, lambda: yn),
        4: (lambda: s, 0, lambda: yn),
        5: (lambda: xn, 0, lambda: yn),
        6: (lambda: s, None, lambda: sib),
        7: (lambda: xn, 0, lambda: sib),
        8: (lambda: yn, 1, lambda: sib),
        9: (lambda: xn, 1, lambda: sib),
        10: (lambda: yn, 0, lambda: sib),
        11: (lambda: diag, 0, lambda: sib),
        12: (lambda: diag, 1, lambda: sib),
    }

    def gcopy(buf, kind, slot, cols):
        owner, h, target = GATHER[kind]
        ref = piece(buf, owner(), h, cols)
        return pltpu.make_async_remote_copy(
            src_ref=ref,
            dst_ref=ref,
            send_sem=gat_send.at[slot, kind],
            recv_sem=gat_recv.at[slot, kind],
            device_id=to(target()),
            device_id_type=MESH,
        )

    every = pl.ds(0, D)

    def n_start(*kinds):
        for kind in kinds:
            gcopy(nf, kind, 8, every).start()

    def n_wait(*kinds):
        for kind in kinds:
            gcopy(nf, kind, 8, every).wait_recv()

    def g_start(j, *kinds):
        for kind in kinds:
            gcopy(gf, kind, j, span(j, TILE)).start()

    def g_wait(j, *kinds):
        for kind in kinds:
            gcopy(gf, kind, j, span(j, TILE)).wait_recv()

    OWN = (0, 3, 6, 1, 4)
    part("gather_rows")
    n_start(*OWN)

    C0 = math.sqrt(2.0 / math.pi)
    C1 = 0.044715

    def up_block(owner):
        rows = span(owner, R)

        @pl.loop(0, FF // TILE)
        def _(n):
            cols = span(n, TILE)
            u = dot(nf[rows, :], wup[:, cols], NN) + bup[:, cols]
            sq = u * u
            t = jnp.tanh(C0 * (u + C1 * (sq * u)))
            cdf = 0.5 + 0.5 * t
            act[rows, cols] = (u * cdf).astype(BF)
            gp[rows, cols] = (
                cdf + (0.5 * C0) * u * (1.0 - t * t) * (1.0 + (3.0 * C1) * sq)
            ).astype(BF)

    def rope(z, rows, sign):
        parts = []
        for p in range(2):
            zp = z[:, p * 128 : (p + 1) * 128]
            c = cos_t[rows, :]
            sn = sin_t[rows, :]
            turned = pltpu.roll(zp, 112, 1) * sn - pltpu.roll(zp * sn, 16, 1)
            parts.append(zp * c + sign * turned)
        return jnp.concatenate(parts, axis=1)

    def qkv_block(owner):
        rows = span(owner, R)
        for t in range(3):
            z = dot(nf[rows, :], wqkv[t], NN) + bqkv[t : t + 1, :]
            if t < 2:
                z = rope(z, rows, 1.0)
            z = z.astype(BF)
            if t == 0:
                z = (z.astype(F32) * (HEAD_DIM**-0.5)).astype(BF)
            qkv[t, rows, :] = z

    part("up_own")
    loads[0].wait()
    loads[1].wait()
    up_block(s)
    n_wait(6)
    up_block(sib)

    lane = lax.rem(lax.broadcasted_iota(jnp.int32, (128, 128), 1), HEAD_DIM)
    first = jnp.where(lane < ROT // 2, -1.0, 0.0)

    @pl.loop(0, T // 128)
    def _(i):
        rows = span(i, 128)
        line = seg_row[:, rows].astype(F32)
        seg_col[rows, :] = jnp.transpose(jnp.broadcast_to(line, (128, 128)))
        line = pos_row[:, rows].astype(F32)
        phase = jnp.transpose(jnp.broadcast_to(line, (128, 128))) * freq[...]
        cos_t[rows, :] = jnp.cos(phase)
        sin_t[rows, :] = jnp.sin(phase) * first

    g_start(0, *OWN)
    part("relay")
    n_wait(0)
    n_start(5, 7)
    n_wait(3)
    n_start(2, 8)
    n_wait(1)
    n_start(9)
    n_wait(4)
    n_start(10)
    g_wait(0, 0)
    g_start(0, 5, 7)
    g_wait(0, 3)
    g_start(0, 2, 8)
    g_start(1, *OWN)
    n_wait(7, 8, 9, 10)

    part("up_next")

    @pl.loop(0, 2)
    def _(mc):
        up_block(other(1, 0, mc))
        up_block(other(0, 1, mc))

    part("relay_far")
    n_wait(5)
    n_start(11)
    n_wait(2)
    n_start(12)
    g_wait(0, 1)
    g_start(0, 9)
    g_wait(0, 4)
    g_start(0, 10)
    n_wait(11, 12)

    part("up_far")

    @pl.loop(0, 2)
    def _(mc):
        up_block(other(1, 1, mc))

    for item in loads[2:]:
        item.wait()

    def near_send(c):
        return pltpu.make_async_remote_copy(
            src_ref=zown.at[c],
            dst_ref=near_b.at[lax.rem(c, RING)],
            send_sem=nsend_sem.at[lax.rem(c, RING)],
            recv_sem=near_sem.at[c],
            device_id=to_rep(far_r),
            device_id_type=MESH,
        )

    def mid_send(c):
        return pltpu.make_async_remote_copy(
            src_ref=send_n.at[lax.rem(c, RING)],
            dst_ref=far_b.at[lax.rem(c, RING)],
            send_sem=nsend_sem.at[lax.rem(c, RING)],
            recv_sem=far_sem.at[c],
            device_id=to_rep(far_r),
            device_id_type=MESH,
        )

    def back_send(c):
        return pltpu.make_async_remote_copy(
            src_ref=send_f.at[lax.rem(c, 2)],
            dst_ref=far_b.at[lax.rem(c, RING)],
            send_sem=fsend_sem.at[lax.rem(c, 2)],
            recv_sem=far_sem.at[c],
            device_id=to_rep(near_r),
            device_id_type=MESH,
        )

    def own_load(c):
        slot = lax.rem(c, RING)
        return pltpu.make_async_copy(zown.at[c], own_b.at[slot], load_sem.at[slot])

    def give(which, rep_id):
        pl.semaphore_signal(
            credit.at[which], inc=1, device_id=to_rep(rep_id), device_id_type=MESH
        )

    def tot_block(c, b, dst):
        slot = lax.rem(c, 2)
        return pltpu.make_async_copy(tot_b.at[slot, b], dst, tot_sem.at[slot, b])

    def tot_start(c):
        def down(b):
            return down_o.at[span(2 * lax.rem(c, 2) + b, TILE), span(c // 2, TILE)]

        def up(b):
            at = c - 16
            return up_o.at[span(at // 2, TILE), span(2 * lax.rem(at, 2) + b, TILE)]

        def out(b):
            return out_o.at[:, span(2 * (c - 32) + b, TILE)]

        def qkv(b):
            at = c - 36
            return qkv_o.at[at // 4, span(2 * lax.rem(at, 4) + b, TILE), :]

        for low, high, place in ((0, 16, down), (16, 32, up), (32, 36, out), (36, 48, qkv)):

            @pl.when((c >= low) & (c < high))
            def _():
                for b in range(2):
                    tot_block(c, b, place(b)).start()

    def tot_wait(c):
        for b in range(2):
            tot_block(c, b, down_o.at[0:TILE, 0:TILE]).wait()

    def add_blocks(outs, ins):
        @pl.loop(0, 8)
        def _(i):
            rows = pl.ds(pl.multiple_of(lax.rem(i, 4) * 64, 64), 64)
            b = i // 4
            vals = [x[b, rows, :].astype(F32) for x in ins]
            for ref, which in outs:
                total = vals[which[0]]
                for w in which[1:]:
                    total = total + vals[w]
                ref[b, rows, :] = total.astype(ref.dtype)

    def within(c):
        return (c >= 0) & (c < CHUNKS)

    def chain_begin():
        own_load(0).start()

        @pl.when(outer)
        def _():
            near_send(0).start()

    def near_tick(k):
        @pl.when(outer & within(k + 1))
        def _():
            @pl.when(k + 1 >= RING)
            def _():
                near_send(k + 1 - RING).wait_send()
                pl.semaphore_wait(credit.at[2], 1)

            near_send(k + 1).start()

        @pl.when(inner & within(k))
        def _():
            slot = lax.rem(k, RING)
            own_load(k).wait()

            @pl.when(k + 1 < CHUNKS)
            def _():
                own_load(k + 1).start()

            @pl.when(k >= RING)
            def _():
                mid_send(k - RING).wait_send()
                pl.semaphore_wait(credit.at[0], 1)

            near_send(k).wait_recv()
            add_blocks([(send_n.at[slot], (0, 1))], [near_b.at[slot], own_b.at[slot]])
            mid_send(k).start()

            @pl.when(k < CHUNKS - RING)
            def _():
                give(2, near_r)

    def far_tick(k):
        ci = k - LAG_INNER

        @pl.when(inner & within(ci))
        def _():
            slot = lax.rem(ci, RING)
            two = lax.rem(ci, 2)

            @pl.when(ci >= 2)
            def _():
                back_send(ci - 2).wait_send()
                tot_wait(ci - 2)

            @pl.when(ci >= RING)
            def _():
                pl.semaphore_wait(credit.at[1], 1)

            mid_send(ci).wait_recv()
            add_blocks(
                [(send_f.at[two], (0, 1)), (tot_b.at[two], (0, 2))],
                [far_b.at[slot], own_b.at[slot], send_n.at[slot]],
            )
            back_send(ci).start()
            tot_start(ci)

            @pl.when(ci < CHUNKS - RING)
            def _():
                give(0, far_r)

        co = k - LAG_OUTER

        @pl.when(outer & within(co))
        def _():
            slot = lax.rem(co, RING)
            own_load(co).wait()

            @pl.when(co + 1 < CHUNKS)
            def _():
                own_load(co + 1).start()

            @pl.when(co >= 2)
            def _():
                tot_wait(co - 2)

            back_send(co).wait_recv()
            add_blocks([(tot_b.at[lax.rem(co, 2)], (0, 1))], [far_b.at[slot], own_b.at[slot]])
            tot_start(co)

            @pl.when(co < CHUNKS - RING)
            def _():
                give(1, far_r)

    def keep(slot, c):
        return pltpu.make_async_copy(stage.at[slot], zown.at[c], stage_sem.at[slot])

    part("grad_w_down")
    small[...] = jnp.zeros_like(small)

    @pl.loop(0, D // TILE)
    def _(j):
        @pl.when(j + 2 < D // TILE)
        def _():
            g_start(j + 2, *OWN)

        @pl.when(j + 1 < D // TILE)
        def _():
            g_wait(j + 1, 0)
            g_start(j + 1, 5, 7)
            g_wait(j + 1, 3)
            g_start(j + 1, 2, 8)
            g_wait(j + 1, 1)
            g_start(j + 1, 9)
            g_wait(j + 1, 4)
            g_start(j + 1, 10)

        g_wait(j, 5)
        g_start(j, 11)
        g_wait(j, 2)
        g_start(j, 12)
        g_wait(j, 6, 7, 8, 9, 10, 11, 12)

        for h in range(FF // 512):
            product = dot(act[:, h * 512 : (h + 1) * 512], gf[:, span(j, TILE)], TN)
            stage[h, 0] = product[:TILE].astype(BF)
            stage[h, 1] = product[TILE:].astype(BF)
            keep(h, 2 * j + h).start()
            if h == 0:

                @pl.when(j == 0)
                def _():
                    keep(0, 0).wait()
                    chain_begin()

        @pl.when(j > 0)
        def _():
            keep(0, 2 * j).wait()

        keep(1, 2 * j + 1).wait()
        near_tick(j)
        qkv_block(j)
        far_tick(j)

    tick0 = D // TILE

    part("grad_up")
    @pl.loop(0, T // 512)
    def _(i):
        rows = span(i, 512)

        near_tick(tick0 + i)

        @pl.loop(0, FF // TILE)
        def _(n):
            @pl.when(n == FF // TILE // 2)
            def _():
                far_tick(tick0 + i)

            cols = span(n, TILE)
            ga = dot(gf[rows, :], wdown[cols, :], NT)
            gu = (ga * gp[rows, cols].astype(F32)).astype(BF)
            gp[rows, cols] = gu
            at = pl.ds(pl.multiple_of(3 * TILE + n * TILE, TILE), TILE)
            small[3:4, at] += jnp.sum(gu.astype(F32), axis=0, keepdims=True)

    tick0 += T // 512

    part("grad_w_up")
    @pl.loop(0, D // 512)
    def _(i):
        near_tick(tick0 + i)

        @pl.loop(0, 2)
        def _(b):
            @pl.when(b == 1)
            def _():
                far_tick(tick0 + i)

            at = 2 * i + b
            product = dot(nf[:, span(at, TILE)], gp[...], TN)
            for q in range(4):
                stage[2 * b + q // 2, q % 2] = product[:, q * TILE : (q + 1) * TILE].astype(BF)
            keep(2 * b, 16 + 2 * at).start()
            keep(2 * b + 1, 17 + 2 * at).start()

        for q in range(4):
            keep(q, 16 + 4 * i + q).wait()

    tick0 += D // 512

    part("grad_attended")
    near_tick(tick0)

    @pl.loop(0, T // 512)
    def _(i):
        rows = span(i, 512)
        dout[rows, :] = dot(gf[rows, :], wout[...], NT).astype(BF)

    far_tick(tick0)
    tick0 += 1

    HC = qkv.shape[2]
    heads = HC // HEAD_DIM
    blocks = SEQ // TILE

    def attend(seq, qb, h):
        base = seq * SEQ
        kmax = (qb + 1) * TILE
        qrows = pl.ds(pl.multiple_of(base + qb * TILE, TILE), TILE)
        krows = pl.ds(pl.multiple_of(base, SEQ), kmax)
        keep_lane = jnp.where(
            lax.broadcasted_iota(jnp.int32, (TILE, HC), 1) // HEAD_DIM == h, 1.0, 0.0
        )
        qh = (qkv[0, qrows, :].astype(F32) * keep_lane).astype(BF)
        doh32 = dout[qrows, :].astype(F32) * keep_lane
        doh = doh32.astype(BF)
        keys = qkv[1, krows, :]
        vals = qkv[2, krows, :]
        scores = dot(qh, keys, NT)
        allowed = (seg_col[qrows, 0:1] == seg_row[:, krows].astype(F32)) & (
            lax.broadcasted_iota(jnp.int32, (TILE, kmax), 1)
            <= lax.broadcasted_iota(jnp.int32, (TILE, kmax), 0) + qb * TILE
        )
        scores = jnp.where(allowed, scores, NEGATIVE)
        weights = jnp.exp(scores - jnp.max(scores, axis=1, keepdims=True))
        probs = weights * (1.0 / jnp.sum(weights, axis=1, keepdims=True))
        probs_low = probs.astype(BF)
        out = dot(probs_low, vals, NN) * keep_lane
        o_acc[...] += out
        delta = jnp.sum(doh32 * out, axis=1, keepdims=True)
        dprobs = dot(doh, vals, NT)
        ds = (probs * (dprobs - delta)).astype(BF)
        q_acc[...] += dot(ds, keys, NN) * keep_lane
        dk_acc[0:kmax, :] += dot(ds, qh, TN)
        dv_acc[0:kmax, :] += dot(probs_low, doh, TN)

    part("attention")
    TICKS_OF = (1, 1, 2, 2)
    per_seq = sum(TICKS_OF)

    @pl.loop(0, T // SEQ)
    def _(seq):
        dk_acc[...] = jnp.zeros_like(dk_acc)
        dv_acc[...] = jnp.zeros_like(dv_acc)
        passed = 0
        for qb in range(blocks):
            n = TICKS_OF[qb]
            q_acc[...] = jnp.zeros_like(q_acc)
            o_acc[...] = jnp.zeros_like(o_acc)

            @pl.loop(0, heads)
            def _(h):
                k = tick0 + seq * per_seq + passed + h // (heads // n)
                at = lax.rem(h, heads // n)

                @pl.when(at == 0)
                def _():
                    near_tick(k)

                @pl.when(at == heads // n // 2)
                def _():
                    far_tick(k)

                attend(seq, qb, h)

            passed += n
            qrows = pl.ds(pl.multiple_of(seq * SEQ + qb * TILE, TILE), TILE)
            att[qrows, :] = o_acc[...].astype(BF)
            dq = rope(q_acc[...] * (HEAD_DIM**-0.5), qrows, -1.0).astype(BF)
            dqkv[0, qrows, :] = dq
            small[3:4, 0:TILE] += jnp.sum(dq.astype(F32), axis=0, keepdims=True)

        @pl.loop(0, blocks)
        def _(b):
            rows = pl.ds(pl.multiple_of(seq * SEQ + b * TILE, TILE), TILE)
            dk = rope(dk_acc[span(b, TILE), :], rows, -1.0).astype(BF)
            dv = dv_acc[span(b, TILE), :].astype(BF)
            dqkv[1, rows, :] = dk
            dqkv[2, rows, :] = dv
            small[3:4, TILE : 2 * TILE] += jnp.sum(dk.astype(F32), axis=0, keepdims=True)
            small[3:4, 2 * TILE : 3 * TILE] += jnp.sum(
                dv.astype(F32), axis=0, keepdims=True
            )

    tick0 += (T // SEQ) * per_seq

    part("grad_w_attention")
    near_tick(tick0)

    @pl.loop(0, 4)
    def _(i):
        product = dot(att[...], gf[:, span(i, 512)], TN)
        stage[i, 0] = product[:, :TILE].astype(BF)
        stage[i, 1] = product[:, TILE:].astype(BF)
        keep(i, 32 + i).start()

    far_tick(tick0)
    for q in range(4):
        keep(q, 32 + q).wait()
    tick0 += 1

    @pl.loop(0, D // TILE)
    def _(j):
        for kind in range(13):
            gcopy(gf, kind, j, span(j, TILE)).wait_send()

    def announce(which):
        for peer in (sib, xn, yn):
            pl.semaphore_signal(
                ready.at[which], inc=1, device_id=to(peer), device_id_type=MESH
            )

    announce(0)

    def qkv_chunk(i):
        slot = lax.rem(i, 4)
        product = dot(nf[:, span(lax.rem(i, 4), 512)], dqkv[i // 4], TN)
        stage[slot, 0] = product[:TILE].astype(BF)
        stage[slot, 1] = product[TILE:].astype(BF)
        keep(slot, 36 + i).start()

    near_tick(tick0)

    @pl.loop(0, 4)
    def _(i):
        qkv_chunk(i)

    far_tick(tick0)
    for q in range(4):
        keep(q, 36 + q).wait()
    tick0 += 1
    part("ready")
    pl.semaphore_wait(ready.at[0], 3)

    CHIPS = ((1, 1), (1, 0), (0, 1), (0, 0))

    def reduce_rows(which, product, buf, between):
        stages = (buf.at[0:R, :], mixed_o)

        def blk(b, h=None):
            if h is None:
                return buf.at[b * R : (b + 1) * R, :]
            return buf.at[b * R + h * half : b * R + (h + 1) * half, :]

        def send(kind, src, dst, target):
            return pltpu.make_async_remote_copy(
                src_ref=src,
                dst_ref=dst,
                send_sem=rs_send.at[which, kind],
                recv_sem=rs_recv.at[which, kind],
                device_id=to(target),
                device_id_type=MESH,
            )

        def to_sib(i):
            return send(i, stages[i % 2], blk(1 + i), sib)

        steps = {
            4: lambda: send(4, blk(1, 0), blk(5, 0), xn),
            5: lambda: send(5, blk(1, 1), blk(5, 1), yn),
            6: lambda: send(6, blk(2, 0), blk(6, 0), xn),
            7: lambda: send(7, blk(3, 1), blk(6, 1), yn),
            8: lambda: send(8, blk(3, 0), blk(7, 0), yn),
            9: lambda: send(9, blk(2, 1), blk(7, 1), xn),
        }

        def sib_part(i):
            if i >= 2:
                to_sib(i - 2).wait_send()
            mx, my = CHIPS[i]
            rows = span(other(mx, my, 1), R)
            ref = stages[i % 2]

            @pl.loop(0, D // TILE)
            def _(n):
                ref[:, span(n, TILE)] = product(rows, n).astype(BF)

            to_sib(i).start()

        def own_part(i):
            mx, my = CHIPS[i]
            rows = span(other(mx, my, 0), R)
            to_sib(i).wait_recv()

            @pl.loop(0, D // TILE)
            def _(n):
                cols = span(n, TILE)
                total = product(rows, n) + buf[(1 + i) * R : (2 + i) * R, cols].astype(F32)
                buf[(1 + i) * R : (2 + i) * R, cols] = total.astype(BF)

        def add_half(dst, src):
            (db, dh), (sb, sh) = dst, src

            @pl.loop(0, half // 32)
            def _(i):
                a = pl.ds(pl.multiple_of(db * R + dh * half + i * 32, 32), 32)
                b = pl.ds(pl.multiple_of(sb * R + sh * half + i * 32, 32), 32)
                buf[a, :] = (buf[a, :].astype(F32) + buf[b, :].astype(F32)).astype(BF)

        sib_part(0)
        between(0)
        sib_part(1)
        between(1)
        own_part(0)
        steps[4]().start()
        steps[5]().start()
        between(2)
        sib_part(2)
        between(3)
        own_part(1)
        steps[6]().start()
        between(4)
        sib_part(3)
        between(5)
        own_part(2)
        steps[7]().start()
        steps[4]().wait_recv()
        add_half((3, 0), (5, 0))
        steps[8]().start()
        steps[5]().wait_recv()
        add_half((2, 1), (5, 1))
        steps[9]().start()
        between(6)
        own_part(3)
        between(7)
        for i in (2, 3):
            to_sib(i).wait_send()

        def finish():
            for kind in (6, 7, 8, 9):
                steps[kind]().wait_recv()

        def drain():
            for kind in range(4, 10):
                steps[kind]().wait_send()

        def total_rows(i):
            at = [
                pl.ds(pl.multiple_of(b * R + i * LN_ROWS, LN_ROWS), LN_ROWS) for b in (4, 6, 7)
            ]
            return sum(buf[a, :].astype(F32) for a in at)

        return finish, drain, total_rows

    def inner_product(rows, n):
        cols = span(n, TILE)
        total = dot(gp[rows, :], wup[cols, :], NT)
        for t in range(3):
            total = total + dot(dqkv[t, rows, :], wqkv[t, cols, :], NT)
        return total

    def outer_product(rows, n):
        cols = span(n, TILE)
        return dot(act[rows, :], wdown[:, cols], NN) + dot(att[rows, :], wout[:, cols], NN)

    part("scatter_inner")
    def between_inner(i):
        near_tick(tick0 + i)
        qkv_chunk(4 + i)
        far_tick(tick0 + i)
        keep(i % 4, 40 + i).wait()

    finish2, drain2, rows2 = reduce_rows(0, inner_product, gf, between_inner)
    tick0 += 8

    for kind in range(13):
        gcopy(nf, kind, 8, every).wait_send()
    announce(1)
    pl.semaphore_wait(ready.at[1], 3)
    part("scatter_outer")

    def between_outer(i):
        if i % 2 == 0:
            near_tick(tick0 + i // 2)
        else:
            far_tick(tick0 + i // 2)

    finish1, drain1, rows1 = reduce_rows(1, outer_product, nf, between_outer)
    tick0 += 4

    part("norm_backward")
    near_tick(tick0)
    finish2()
    cot_load = pltpu.make_async_copy(gloc, mixed_o, w_sem.at[1])
    cot_load.start()
    cot_load.wait()

    @pl.loop(0, R // LN_ROWS)
    def _(i):
        rows = span(i, LN_ROWS)
        scaled, inv = norm_rows(i)
        gn = rows2(i)
        cot = mixed_o[rows, :].astype(F32)
        g = gn * gain[...]
        back = g - jnp.mean(g, axis=1, keepdims=True)
        back = back - scaled * jnp.mean(g * scaled, axis=1, keepdims=True)
        gtok_o[rows, :] = (cot + back * inv).astype(BF)
        small[0:1, :] += jnp.sum(gn * scaled, axis=0, keepdims=True)
        small[1:2, :] += jnp.sum(gn, axis=0, keepdims=True)
        small[2:3, :] += jnp.sum(cot, axis=0, keepdims=True)

    far_tick(tick0)
    tick0 += 1

    part("small_sums")
    for step, peer in enumerate((sib, xn, yn)):
        copy = pltpu.make_async_remote_copy(
            src_ref=small,
            dst_ref=small_in.at[step],
            send_sem=sm_send.at[step],
            recv_sem=sm_recv.at[step],
            device_id=to(peer),
            device_id_type=MESH,
        )
        copy.start()
        near_tick(tick0 + step)
        copy.wait()
        small[0:3, :] += small_in[step, 0:3, :]
        far_tick(tick0 + step)

    tick0 += 3
    for step in (1, 2, 3):
        pltpu.make_async_remote_copy(
            src_ref=small,
            dst_ref=small_z.at[step - 1],
            send_sem=smz_send.at[step - 1],
            recv_sem=smz_recv.at[step - 1],
            device_id=to_rep(lax.rem(r + step, 4)),
            device_id_type=MESH,
        ).start()

    part("output")
    finish1()

    @pl.loop(0, R // LN_ROWS)
    def _(i):
        rows = span(i, LN_ROWS)
        total = tok[rows, :].astype(F32) + rows1(i) + bout[...] + bdown[...]
        mixed_o[rows, :] = total.astype(BF)

    drain2()
    drain1()

    for step in (1, 2, 3):
        pltpu.make_async_remote_copy(
            src_ref=small,
            dst_ref=small_z.at[step - 1],
            send_sem=smz_send.at[step - 1],
            recv_sem=smz_recv.at[step - 1],
            device_id=to_rep(lax.rem(r + step, 4)),
            device_id_type=MESH,
        ).wait()
    small_o[...] = small[...] + small_z[0] + small_z[1] + small_z[2]

    part("rest")

    @pl.loop(tick0, TICKS)
    def _(k):
        near_tick(k)
        far_tick(k)

    part("last")
    for c in range(CHUNKS - RING, CHUNKS):

        @pl.when(outer)
        def _():
            near_send(c).wait_send()

        @pl.when(inner)
        def _():
            mid_send(c).wait_send()

    for c in (CHUNKS - 2, CHUNKS - 1):
        tot_wait(c)

        @pl.when(inner)
        def _():
            back_send(c).wait_send()

    scope.close()


def frequencies():
    lane = np.arange(128) % HEAD_DIM
    frequency = np.exp(-(lane % (ROT // 2)) * (2.0 * math.log(10000.0) / ROT))
    return np.where(lane < ROT, frequency, 0.0).astype(np.float32)[None]


def fused_body(
    tokens,
    segments,
    positions,
    ln_gain,
    ln_bias,
    w_qkv,
    b_qkv,
    w_up,
    b_up,
    w_out,
    b_out,
    w_down,
    b_down,
    grad_out,
):
    _, R, D = tokens.shape
    T = R * lax.axis_size("shard")
    HC = w_qkv.shape[2]
    FF = w_up.shape[1]
    vmem = pl.BlockSpec(memory_space=pltpu.VMEM)
    hbm = pl.BlockSpec(memory_space=pl.ANY)
    block = (CHUNKS, 2, TILE, TILE)
    piece = (2, TILE, TILE)
    out_shape = (
        jax.ShapeDtypeStruct((R, D), BF),
        jax.ShapeDtypeStruct((R, D), BF),
        jax.ShapeDtypeStruct((8, D), F32),
        jax.ShapeDtypeStruct((FF, D), SUM),
        jax.ShapeDtypeStruct((D, FF), SUM),
        jax.ShapeDtypeStruct((HC, D), SUM),
        jax.ShapeDtypeStruct((3, D, HC), SUM),
        jax.ShapeDtypeStruct(block, BF),
    )
    dma = pltpu.SemaphoreType.DMA
    scratch = [
        pltpu.VMEM((T, D), BF),
        pltpu.VMEM((T, D), BF),
        pltpu.VMEM((T, FF), BF),
        pltpu.VMEM((T, FF), BF),
        pltpu.VMEM((3, T, HC), BF),
        pltpu.VMEM((T, HC), BF),
        pltpu.VMEM((T, HC), BF),
        pltpu.VMEM((3, T, HC), BF),
        pltpu.VMEM((SEQ, HC), F32),
        pltpu.VMEM((SEQ, HC), F32),
        pltpu.VMEM((TILE, HC), F32),
        pltpu.VMEM((TILE, HC), F32),
        pltpu.VMEM((3, D, HC), BF),
        pltpu.VMEM((D, FF), BF),
        pltpu.VMEM((HC, D), BF),
        pltpu.VMEM((FF, D), BF),
        pltpu.VMEM((T, 128), F32),
        pltpu.VMEM((T, 128), F32),
        pltpu.VMEM((T, 128), F32),
        pltpu.VMEM((4,) + piece, BF),
        pltpu.VMEM((RING,) + piece, BF),
        pltpu.VMEM((RING,) + piece, BF),
        pltpu.VMEM((RING,) + piece, BF),
        pltpu.VMEM((RING,) + piece, BF),
        pltpu.VMEM((2,) + piece, BF),
        pltpu.VMEM((2,) + piece, SUM),
        pltpu.VMEM((8, D), F32),
        pltpu.VMEM((3, 8, D), F32),
        pltpu.VMEM((3, 8, D), F32),
        dma((9, 13)),
        dma((9, 13)),
        dma((5,)),
        dma((4,)),
        dma((RING,)),
        dma((RING,)),
        dma((2,)),
        dma((2, 2)),
        dma((CHUNKS,)),
        dma((CHUNKS,)),
        dma((2, 10)),
        dma((2, 10)),
        dma((3,)),
        dma((3,)),
        dma((3,)),
        dma((3,)),
        pltpu.SemaphoreType.REGULAR((2,)),
        pltpu.SemaphoreType.REGULAR((3,)),
    ]
    mixed, gtok, small, g_down, g_up, g_out, g_qkv, _ = pl.pallas_call(
        fused,
        out_shape=out_shape,
        in_specs=[vmem, hbm, vmem, vmem, hbm, vmem, hbm, vmem, hbm, vmem, hbm] + [vmem] * 4,
        out_specs=(vmem, vmem, vmem, hbm, hbm, hbm, hbm, hbm),
        scratch_shapes=scratch,
        name="layer",
        compiler_params=pltpu.CompilerParams(
            collective_id=0, has_side_effects=True, vmem_limit_bytes=VMEM_BYTES
        ),
    )(
        tokens[0],
        grad_out[0],
        ln_gain[None],
        ln_bias[None],
        jnp.transpose(w_qkv, (1, 0, 2)),
        b_qkv,
        w_up,
        b_up[None],
        w_out,
        b_out[None],
        w_down,
        b_down[None],
        segments,
        positions,
        frequencies(),
    )
    bias_inner = small[3]
    return (
        mixed[None],
        gtok[None],
        small[0],
        small[1],
        jnp.transpose(g_qkv, (1, 0, 2)).astype(F32),
        bias_inner[: 3 * HC].reshape(3, HC),
        g_up.astype(F32),
        bias_inner[3 * HC : 3 * HC + FF],
        g_out.astype(F32),
        small[2],
        g_down.astype(F32),
        small[2],
    )


def fits_fused(mesh):
    return dict(mesh.shape) == {"shard": 8, "replica": 4}


def solution(mesh):
    placed = (
        P("replica", "shard", None),
        P("replica", None),
        P("replica", None),
        P(),
        P(),
        P(None, None, "shard"),
        P(None, "shard"),
        P(None, "shard"),
        P("shard"),
        P("shard", None),
        P(),
        P("shard", None),
        P(),
        P("replica", "shard", None),
    )
    return jax.shard_map(
        fused_body if fits_fused(mesh) else body,
        mesh=mesh,
        in_specs=placed,
        out_specs=(
            P("replica", "shard", None),
            P("replica", "shard", None),
            P(),
            P(),
            P(None, None, "shard"),
            P(None, "shard"),
            P(None, "shard"),
            P("shard"),
            P("shard", None),
            P(),
            P("shard", None),
            P(),
        ),
        check_vma=False,
    )
```

```python
import contextlib
import functools
import math

import jax
import jax.numpy as jnp
import numpy as np
from jax import lax
from jax.experimental import pallas as pl
from jax.experimental.pallas import tpu as pltpu
from jax.sharding import PartitionSpec as P

HEAD_DIM = 64
ROT = 32


EPSILON = 1e-05
NEGATIVE = -1e30
VMEM_BYTES = 64 * 1024 * 1024


def angles(positions):
    frequency = jnp.exp(jnp.arange(ROT // 2, dtype=jnp.float32) * (-2.0 * math.log(10000.0) / ROT))
    phase_angle = positions.astype(jnp.float32)[:, None] * frequency[None, :]
    return (jnp.cos(phase_angle), jnp.sin(phase_angle))


def rotate(heads_in, cosine_part, sine_part):
    half_rot = ROT // 2
    first_part = heads_in[..., :half_rot]
    second_part = heads_in[..., half_rot:ROT]
    cosine_rows = cosine_part[:, None, :]
    sine_rows = sine_part[:, None, :]
    return jnp.concatenate(
        [
            first_part * cosine_rows - second_part * sine_rows,
            second_part * cosine_rows + first_part * sine_rows,
            heads_in[..., ROT:],
        ],
        axis=-1,
    )


def layer_norm(token_rows, gain_vector, bias_vector):
    centered = token_rows - jnp.mean(token_rows, axis=1, keepdims=True)
    scaled = centered * lax.rsqrt(jnp.mean(centered * centered, axis=1, keepdims=True) + EPSILON)
    return scaled * gain_vector + bias_vector


def take_rows(array_in, row_start, row_count):
    return lax.dynamic_slice_in_dim(array_in, row_start, row_count, 0)


def body(
    tokens,
    segments,
    positions,
    ln_gain,
    ln_bias,
    w_qkv,
    b_qkv,
    w_up,
    b_up,
    w_out,
    b_out,
    w_down,
    b_down,
    grad_out,
):
    local_rows = tokens[0].astype(jnp.float32)
    tok_rows, model_width = local_rows.shape
    length = tok_rows * lax.axis_size("shard")
    head_cols = w_qkv.shape[2]
    heads_here = head_cols // HEAD_DIM
    qkv_cols = 3 * head_cols
    split_shape = (length, heads_here, HEAD_DIM)
    scale_factor = HEAD_DIM ** (-0.5)
    cosine_part, sine_part = angles(positions[0])
    seq_segments = segments[0]
    normed_full, norm_back = jax.vjp(layer_norm, local_rows, ln_gain, ln_bias)
    normed = normed_full.astype(jnp.bfloat16)
    w_inner = jnp.concatenate([w_qkv.reshape(model_width, qkv_cols), w_up], axis=1)
    b_inner = jnp.concatenate([b_qkv.reshape(qkv_cols), b_up])
    gathered = lax.all_gather(normed, "shard", axis=0, tiled=True)
    inner_proj = jnp.dot(gathered, w_inner, preferred_element_type=jnp.float32)
    inner_proj = inner_proj + b_inner
    queries = rotate(inner_proj[:, :head_cols].reshape(split_shape), cosine_part, sine_part).astype(
        jnp.bfloat16
    )
    keys_all = rotate(
        inner_proj[:, head_cols : 2 * head_cols].reshape(split_shape), cosine_part, sine_part
    ).astype(jnp.bfloat16)
    values_all = inner_proj[:, 2 * head_cols : qkv_cols].reshape(split_shape).astype(jnp.bfloat16)
    up_proj = inner_proj[:, qkv_cols:]
    activation = jax.nn.gelu(up_proj, approximate=True).astype(jnp.bfloat16)
    block_rows = math.gcd(length, 512)
    block_count = length // block_rows
    offsets_block = jnp.arange(block_rows, dtype=jnp.int32)

    def block_scores(query_block, key_block, query_start, key_start):
        scores = (
            jnp.einsum("qhe,khe->hqk", query_block, key_block, preferred_element_type=jnp.float32)
            * scale_factor
        )
        query_ids = query_start + offsets_block
        key_ids = key_start + offsets_block
        query_segs = take_rows(seq_segments, query_start, block_rows)
        key_segs = take_rows(seq_segments, key_start, block_rows)
        allowed = (query_ids[:, None] >= key_ids[None, :]) & (
            query_segs[:, None] == key_segs[None, :]
        )
        return jnp.where(allowed[None], scores, NEGATIVE)

    def attend(query_index):
        query_start = query_index * block_rows
        query_block = take_rows(queries, query_start, block_rows)

        def first_pass(key_index, row_stats):
            row_max, row_sum = row_stats
            key_start = key_index * block_rows
            scores = block_scores(
                query_block, take_rows(keys_all, key_start, block_rows), query_start, key_start
            )
            new_max = jnp.maximum(row_max, jnp.max(scores, axis=2))
            row_sum = row_sum * jnp.exp(row_max - new_max) + jnp.sum(
                jnp.exp(scores - new_max[:, :, None]), axis=2
            )
            return (new_max, row_sum)

        row_max, row_sum = lax.fori_loop(
            0,
            query_index + 1,
            first_pass,
            (
                jnp.full((heads_here, block_rows), NEGATIVE, jnp.float32),
                jnp.zeros((heads_here, block_rows), jnp.float32),
            ),
        )

        def second_pass(key_index, total_out):
            key_start = key_index * block_rows
            scores = block_scores(
                query_block, take_rows(keys_all, key_start, block_rows), query_start, key_start
            )
            probability = (jnp.exp(scores - row_max[:, :, None]) / row_sum[:, :, None]).astype(
                jnp.bfloat16
            )
            return total_out + jnp.einsum(
                "hqk,khe->qhe",
                probability,
                take_rows(values_all, key_start, block_rows),
                preferred_element_type=jnp.float32,
            )

        attended_block = lax.fori_loop(
            0,
            query_index + 1,
            second_pass,
            jnp.zeros((block_rows, heads_here, HEAD_DIM), jnp.float32),
        )
        return (attended_block, row_max, row_sum)

    attended_full, row_maxes, row_sums = lax.map(attend, jnp.arange(block_count, dtype=jnp.int32))
    attended_full = attended_full.reshape(length, head_cols)
    attended = attended_full.astype(jnp.bfloat16)
    outer_act = jnp.concatenate([attended, activation], axis=1)
    w_outer = jnp.concatenate([w_out, w_down], axis=0)
    branches = lax.psum_scatter(
        jnp.dot(
            take_rows(outer_act, jnp.int32(0), lax.axis_size("shard") * tok_rows),
            w_outer,
            preferred_element_type=jnp.float32,
        ).astype(jnp.bfloat16),
        "shard",
        scatter_dimension=0,
        tiled=True,
    ).astype(jnp.float32)
    mixed_out = (local_rows + branches + b_out + b_down).astype(jnp.bfloat16)
    cotangent = grad_out[0]
    shard_piece = lax.all_gather(cotangent, "shard", axis=0, tiled=True)
    act_rows = take_rows(outer_act, jnp.int32(0), shard_piece.shape[0])
    weight_sum = jnp.einsum("sa,sd->ad", act_rows, shard_piece, preferred_element_type=jnp.float32)
    back_rows = jnp.einsum("sd,ad->sa", shard_piece, w_outer, preferred_element_type=jnp.float32)
    grad_outer = weight_sum
    back_attended = back_rows[:, :head_cols].astype(jnp.bfloat16).reshape(split_shape)
    delta_all = jnp.sum(
        back_attended.astype(jnp.float32) * attended_full.reshape(split_shape), axis=2
    ).T

    def key_pass(key_index, grads_all):
        grad_query, grad_key, grad_value = grads_all
        key_start = key_index * block_rows
        key_block = take_rows(keys_all, key_start, block_rows)
        value_block = take_rows(values_all, key_start, block_rows)

        def query_pass(query_index, inner_state):
            grad_query, key_total, value_total = inner_state
            query_start = query_index * block_rows
            query_block = take_rows(queries, query_start, block_rows)
            back_block = take_rows(back_attended, query_start, block_rows)
            delta_block = lax.dynamic_slice_in_dim(delta_all, query_start, block_rows, 1)
            scores = block_scores(query_block, key_block, query_start, key_start)
            probability = (
                jnp.exp(scores - row_maxes[query_index][:, :, None])
                / row_sums[query_index][:, :, None]
            )
            grad_prob = jnp.einsum(
                "qhe,khe->hqk", back_block, value_block, preferred_element_type=jnp.float32
            )
            grad_scores = (probability * (grad_prob - delta_block[:, :, None])).astype(jnp.bfloat16)
            value_total = value_total + jnp.einsum(
                "hqk,qhe->khe",
                probability.astype(jnp.bfloat16),
                back_block,
                preferred_element_type=jnp.float32,
            )
            key_total = key_total + jnp.einsum(
                "hqk,qhe->khe", grad_scores, query_block, preferred_element_type=jnp.float32
            )
            query_rows = take_rows(grad_query, query_start, block_rows) + jnp.einsum(
                "hqk,khe->qhe", grad_scores, key_block, preferred_element_type=jnp.float32
            )
            grad_query = lax.dynamic_update_slice_in_dim(grad_query, query_rows, query_start, 0)
            return (grad_query, key_total, value_total)

        empty_block = jnp.zeros((block_rows, heads_here, HEAD_DIM), jnp.float32)
        grad_query, key_total, value_total = lax.fori_loop(
            key_index, block_count, query_pass, (grad_query, empty_block, empty_block)
        )
        grad_key = lax.dynamic_update_slice_in_dim(grad_key, key_total, key_start, 0)
        grad_value = lax.dynamic_update_slice_in_dim(grad_value, value_total, key_start, 0)
        return (grad_query, grad_key, grad_value)

    empty_all = jnp.zeros(split_shape, jnp.float32)
    grad_query, grad_key, grad_value = lax.fori_loop(
        0, block_count, key_pass, (empty_all, empty_all, empty_all)
    )
    grad_query = rotate(grad_query * scale_factor, cosine_part, -sine_part)
    grad_key = rotate(grad_key * scale_factor, cosine_part, -sine_part)
    _, gelu_back = jax.vjp(functools.partial(jax.nn.gelu, approximate=True), up_proj)
    grad_up = gelu_back(back_rows[:, head_cols:])[0]
    grad_inner_rows = jnp.concatenate(
        [
            grad_query.reshape(length, head_cols),
            grad_key.reshape(length, head_cols),
            grad_value.reshape(length, head_cols),
            grad_up,
        ],
        axis=1,
    ).astype(jnp.bfloat16)
    grad_normed = lax.psum_scatter(
        jnp.einsum(
            "sa,da->sd",
            take_rows(grad_inner_rows, jnp.int32(0), lax.axis_size("shard") * tok_rows),
            w_inner,
            preferred_element_type=jnp.float32,
        ).astype(jnp.bfloat16),
        "shard",
        scatter_dimension=0,
        tiled=True,
    ).astype(jnp.float32)
    grad_local, grad_gain, grad_shift = norm_back(grad_normed)
    grad_tokens = (cotangent.astype(jnp.float32) + grad_local).astype(jnp.bfloat16)
    bias_inner = jnp.sum(grad_inner_rows, axis=0, dtype=jnp.float32)
    grad_inner = jnp.einsum(
        "sd,sa->da", gathered, grad_inner_rows, preferred_element_type=jnp.float32
    )
    grad_gain, grad_shift, bias_out = lax.psum(
        (grad_gain, grad_shift, jnp.sum(cotangent, axis=0, dtype=jnp.float32)), ("shard", "replica")
    )
    grad_inner, bias_inner, grad_outer = (
        lax.psum(grad_inner.astype(jnp.bfloat16), "replica").astype(jnp.float32),
        lax.psum(bias_inner.astype(jnp.bfloat16), "replica").astype(jnp.float32),
        lax.psum(grad_outer.astype(jnp.bfloat16), "replica").astype(jnp.float32),
    )
    return (
        mixed_out[None],
        grad_tokens[None],
        grad_gain,
        grad_shift,
        grad_inner[:, :qkv_cols].reshape(model_width, 3, head_cols),
        bias_inner[:qkv_cols].reshape(3, head_cols),
        grad_inner[:, qkv_cols:],
        bias_inner[qkv_cols:],
        grad_outer[:head_cols],
        bias_out,
        grad_outer[head_cols:],
        bias_out,
    )


SEQ = 1024
TILE = 256
WIDE = 512
BF = jnp.bfloat16
F32 = jnp.float32
SUM = jnp.bfloat16
MESH = pl.DeviceIdType.MESH
NN = (((1,), (0,)), ((), ()))
NT = (((1,), (1,)), ((), ()))
TN = (((0,), (0,)), ((), ()))
CHUNKS = 48
RING = 3
LAG_INNER = 1
LAG_OUTER = 3
TICKS = CHUNKS + LAG_OUTER


def dot(left, right, dims):
    return lax.dot_general(left, right, dims, preferred_element_type=F32)


def span(index, size):
    return pl.ds(pl.multiple_of(index * size, size), size)


def fused(
    tok,
    gloc,
    gain,
    bias,
    wqkv_h,
    bqkv,
    wup_h,
    bup,
    wout_h,
    bout,
    wdown_h,
    bdown,
    seg_row,
    pos_row,
    freq,
    mixed_o,
    gtok_o,
    small_o,
    down_o,
    up_o,
    out_o,
    qkv_o,
    zown,
    nf,
    gf,
    act,
    gp,
    qkv,
    att,
    dout,
    dqkv,
    dk_acc,
    dv_acc,
    q_acc,
    o_acc,
    wqkv,
    wup,
    wout,
    wdown,
    cos_t,
    sin_t,
    seg_col,
    stage,
    near_b,
    far_b,
    own_b,
    send_n,
    send_f,
    tot_b,
    small,
    small_in,
    small_z,
    gat_send,
    gat_recv,
    w_sem,
    stage_sem,
    load_sem,
    nsend_sem,
    fsend_sem,
    tot_sem,
    near_sem,
    far_sem,
    rs_send,
    rs_recv,
    sm_send,
    sm_recv,
    smz_send,
    smz_recv,
    ready,
    credit,
):
    T, D = nf.shape
    R = tok.shape[0]
    FF = act.shape[1]
    half = R // 2
    s = lax.axis_index("shard")
    r = lax.axis_index("replica")
    core = lax.rem(s, 2)
    xb = lax.rem(s // 2, 2)
    yb = s // 4
    inner = (r == 1) | (r == 2)
    outer = (r == 0) | (r == 3)

    def other(mx, my, mc):
        cc = core + mc - 2 * core * mc
        xx = xb + mx - 2 * xb * mx
        yy = yb + my - 2 * yb * my
        return yy * 4 + xx * 2 + cc

    sib = other(0, 0, 1)
    xn = other(1, 0, 0)
    yn = other(0, 1, 0)
    diag = other(1, 1, 0)
    far_r = jnp.where(r == 0, 1, jnp.where(r == 1, 2, jnp.where(r == 2, 1, 2)))
    near_r = jnp.where(r == 1, 0, jnp.where(r == 2, 3, r))

    def to(shard_id):
        return {"shard": shard_id, "replica": r}

    def to_rep(rep_id):
        return {"shard": s, "replica": rep_id}

    scope = contextlib.ExitStack()

    def part(name):
        scope.close()
        scope.enter_context(jax.named_scope(name))

    part("norm")
    barrier = pltpu.get_barrier_semaphore()
    for peer in (sib, xn, yn):
        pl.semaphore_signal(barrier, inc=1, device_id=to(peer), device_id_type=MESH)
    for step in (1, 2, 3):
        pl.semaphore_signal(
            barrier, inc=1, device_id=to_rep(lax.rem(r + step, 4)), device_id_type=MESH
        )

    loads = [
        pltpu.make_async_copy(wup_h, wup, w_sem.at[0]),
        pltpu.make_async_copy(gloc, gf.at[span(s, R), :], w_sem.at[1]),
        pltpu.make_async_copy(wdown_h, wdown, w_sem.at[2]),
        pltpu.make_async_copy(wout_h, wout, w_sem.at[3]),
    ]
    HC = qkv.shape[2]
    for t in range(3):
        loads.append(
            pltpu.make_async_copy(
                wqkv_h.at[t], wqkv.at[:, t * HC : (t + 1) * HC], w_sem.at[4 + t]
            )
        )
    for item in loads:
        item.start()

    LN_ROWS = 32

    def norm_rows(i):
        x = tok[span(i, LN_ROWS), :].astype(F32)
        centered = x - jnp.mean(x, axis=1, keepdims=True)
        inv = lax.rsqrt(jnp.mean(centered * centered, axis=1, keepdims=True) + EPSILON)
        return centered * inv, inv

    @pl.loop(0, R // LN_ROWS)
    def _(i):
        scaled, _ = norm_rows(i)
        rows = pl.ds(pl.multiple_of(s * R + i * LN_ROWS, LN_ROWS), LN_ROWS)
        nf[rows, :] = (scaled * gain[...] + bias[...]).astype(BF)

    pl.semaphore_wait(barrier, 6)

    def piece(buf, owner, h, cols):
        if h is None:
            return buf.at[span(owner, R), cols]
        rows = pl.ds(pl.multiple_of(owner * R + h * half, half), half)
        return buf.at[rows, cols]

    GATHER = {
        0: (lambda: s, 0, lambda: xn),
        1: (lambda: s, 1, lambda: xn),
        2: (lambda: yn, 1, lambda: xn),
        3: (lambda: s, 1, lambda: yn),
        4: (lambda: s, 0, lambda: yn),
        5: (lambda: xn, 0, lambda: yn),
        6: (lambda: s, None, lambda: sib),
        7: (lambda: xn, 0, lambda: sib),
        8: (lambda: yn, 1, lambda: sib),
        9: (lambda: xn, 1, lambda: sib),
        10: (lambda: yn, 0, lambda: sib),
        11: (lambda: diag, 0, lambda: sib),
        12: (lambda: diag, 1, lambda: sib),
    }

    def gcopy(buf, kind, slot, cols):
        owner, h, target = GATHER[kind]
        ref = piece(buf, owner(), h, cols)
        return pltpu.make_async_remote_copy(
            src_ref=ref,
            dst_ref=ref,
            send_sem=gat_send.at[slot, kind],
            recv_sem=gat_recv.at[slot, kind],
            device_id=to(target()),
            device_id_type=MESH,
        )

    every = pl.ds(0, D)

    def n_start(*kinds):
        for kind in kinds:
            gcopy(nf, kind, 8, every).start()

    def n_wait(*kinds):
        for kind in kinds:
            gcopy(nf, kind, 8, every).wait_recv()

    def g_start(j, *kinds):
        for kind in kinds:
            gcopy(gf, kind, j, span(j, TILE)).start()

    def g_wait(j, *kinds):
        for kind in kinds:
            gcopy(gf, kind, j, span(j, TILE)).wait_recv()

    OWN = (0, 3, 6, 1, 4)
    part("gather_rows")
    n_start(*OWN)

    C0 = math.sqrt(2.0 / math.pi)
    C1 = 0.044715

    def up_block(owner):
        rows = span(owner, R)

        @pl.loop(0, FF // WIDE)
        def _(n):
            cols = span(n, WIDE)
            u = dot(nf[rows, :], wup[:, cols], NN) + bup[:, cols]
            sq = u * u
            t = jnp.tanh(C0 * (u + C1 * (sq * u)))
            cdf = 0.5 + 0.5 * t
            act[rows, cols] = (u * cdf).astype(BF)
            gp[rows, cols] = (
                cdf + (0.5 * C0) * u * (1.0 - t * t) * (1.0 + (3.0 * C1) * sq)
            ).astype(BF)

    def rope(z, rows, sign):
        parts = []
        for p in range(2):
            zp = z[:, p * 128 : (p + 1) * 128]
            c = cos_t[rows, :]
            sn = sin_t[rows, :]
            turned = pltpu.roll(zp, 112, 1) * sn - pltpu.roll(zp * sn, 16, 1)
            parts.append(zp * c + sign * turned)
        return jnp.concatenate(parts, axis=1)

    def qkv_block(owner):
        rows = span(owner, R)
        every_z = dot(nf[rows, :], wqkv[...], NN)
        for t in range(3):
            z = every_z[:, t * HC : (t + 1) * HC] + bqkv[t : t + 1, :]
            if t < 2:
                z = rope(z, rows, 1.0)
            z = z.astype(BF)
            if t == 0:
                z = (z.astype(F32) * (HEAD_DIM**-0.5)).astype(BF)
            qkv[t, rows, :] = z

    part("up_own")
    loads[0].wait()
    loads[1].wait()
    up_block(s)
    n_wait(6)
    up_block(sib)

    lane = lax.rem(lax.broadcasted_iota(jnp.int32, (128, 128), 1), HEAD_DIM)
    first = jnp.where(lane < ROT // 2, -1.0, 0.0)

    @pl.loop(0, T // 128)
    def _(i):
        rows = span(i, 128)
        line = seg_row[:, rows].astype(F32)
        seg_col[rows, :] = jnp.transpose(jnp.broadcast_to(line, (128, 128))).astype(BF)
        line = pos_row[:, rows].astype(F32)
        phase = jnp.transpose(jnp.broadcast_to(line, (128, 128))) * freq[...]
        cos_t[rows, :] = jnp.cos(phase)
        sin_t[rows, :] = jnp.sin(phase) * first

    part("relay")
    n_wait(0)
    n_start(5, 7)
    n_wait(3)
    n_start(2, 8)
    g_start(0, *OWN)
    n_wait(1)
    n_start(9)
    n_wait(4)
    n_start(10)
    n_wait(7, 8, 9, 10)

    part("up_next")

    @pl.loop(0, 2)
    def _(mc):
        up_block(other(1, 0, mc))
        up_block(other(0, 1, mc))

    part("relay_far")
    n_wait(5)
    n_start(11)
    n_wait(2)
    n_start(12)
    up_block(diag)
    g_wait(0, 0)
    g_start(0, 5, 7)
    g_wait(0, 3)
    g_start(0, 2, 8)
    g_start(1, *OWN)
    g_wait(0, 1)
    g_start(0, 9)
    g_wait(0, 4)
    g_start(0, 10)
    n_wait(11, 12)
    up_block(other(1, 1, 1))

    for item in loads[2:]:
        item.wait()

    def near_send(c):
        return pltpu.make_async_remote_copy(
            src_ref=zown.at[c],
            dst_ref=near_b.at[lax.rem(c, RING)],
            send_sem=nsend_sem.at[lax.rem(c, RING)],
            recv_sem=near_sem.at[c],
            device_id=to_rep(far_r),
            device_id_type=MESH,
        )

    def mid_send(c):
        return pltpu.make_async_remote_copy(
            src_ref=send_n.at[lax.rem(c, RING)],
            dst_ref=far_b.at[lax.rem(c, RING)],
            send_sem=nsend_sem.at[lax.rem(c, RING)],
            recv_sem=far_sem.at[c],
            device_id=to_rep(far_r),
            device_id_type=MESH,
        )

    def back_send(c):
        return pltpu.make_async_remote_copy(
            src_ref=send_f.at[lax.rem(c, 2)],
            dst_ref=far_b.at[lax.rem(c, RING)],
            send_sem=fsend_sem.at[lax.rem(c, 2)],
            recv_sem=far_sem.at[c],
            device_id=to_rep(near_r),
            device_id_type=MESH,
        )

    def own_load(c):
        slot = lax.rem(c, RING)
        return pltpu.make_async_copy(zown.at[c], own_b.at[slot], load_sem.at[slot])

    def give(which, rep_id):
        pl.semaphore_signal(
            credit.at[which], inc=1, device_id=to_rep(rep_id), device_id_type=MESH
        )

    def tot_block(c, b, dst):
        slot = lax.rem(c, 2)
        return pltpu.make_async_copy(tot_b.at[slot, b], dst, tot_sem.at[slot, b])

    def tot_start(c):
        def down(b):
            return down_o.at[span(2 * lax.rem(c, 2) + b, TILE), span(c // 2, TILE)]

        def up(b):
            at = c - 16
            return up_o.at[span(at // 2, TILE), span(2 * lax.rem(at, 2) + b, TILE)]

        def out(b):
            return out_o.at[:, span(2 * (c - 32) + b, TILE)]

        def qkv(b):
            at = c - 36
            return qkv_o.at[lax.rem(at, 3), span(2 * (at // 3) + b, TILE), :]

        for low, high, place in ((0, 16, down), (16, 32, up), (32, 36, out), (36, 48, qkv)):

            @pl.when((c >= low) & (c < high))
            def _():
                for b in range(2):
                    tot_block(c, b, place(b)).start()

    def tot_wait(c):
        for b in range(2):
            tot_block(c, b, down_o.at[0:TILE, 0:TILE]).wait()

    def add_blocks(outs, ins):
        @pl.loop(0, 8)
        def _(i):
            rows = pl.ds(pl.multiple_of(lax.rem(i, 4) * 64, 64), 64)
            b = i // 4
            vals = [x[b, rows, :].astype(F32) for x in ins]
            for ref, which in outs:
                total = vals[which[0]]
                for w in which[1:]:
                    total = total + vals[w]
                ref[b, rows, :] = total.astype(ref.dtype)

    def within(c):
        return (c >= 0) & (c < CHUNKS)

    def chain_begin():
        own_load(0).start()

        @pl.when(outer)
        def _():
            near_send(0).start()

    def near_tick(k):
        @pl.when(outer & within(k + 1))
        def _():
            @pl.when(k + 1 >= RING)
            def _():
                near_send(k + 1 - RING).wait_send()
                pl.semaphore_wait(credit.at[2], 1)

            near_send(k + 1).start()

        @pl.when(inner & within(k))
        def _():
            slot = lax.rem(k, RING)
            own_load(k).wait()

            @pl.when(k + 1 < CHUNKS)
            def _():
                own_load(k + 1).start()

            @pl.when(k >= RING)
            def _():
                mid_send(k - RING).wait_send()
                pl.semaphore_wait(credit.at[0], 1)

            near_send(k).wait_recv()
            add_blocks([(send_n.at[slot], (0, 1))], [near_b.at[slot], own_b.at[slot]])
            mid_send(k).start()

            @pl.when(k < CHUNKS - RING)
            def _():
                give(2, near_r)

    def far_tick(k):
        ci = k - LAG_INNER

        @pl.when(inner & within(ci))
        def _():
            slot = lax.rem(ci, RING)
            two = lax.rem(ci, 2)

            @pl.when(ci >= 2)
            def _():
                back_send(ci - 2).wait_send()
                tot_wait(ci - 2)

            @pl.when(ci >= RING)
            def _():
                pl.semaphore_wait(credit.at[1], 1)

            mid_send(ci).wait_recv()
            add_blocks(
                [(send_f.at[two], (0, 1)), (tot_b.at[two], (0, 2))],
                [far_b.at[slot], own_b.at[slot], send_n.at[slot]],
            )
            back_send(ci).start()
            tot_start(ci)

            @pl.when(ci < CHUNKS - RING)
            def _():
                give(0, far_r)

        co = k - LAG_OUTER

        @pl.when(outer & within(co))
        def _():
            slot = lax.rem(co, RING)
            own_load(co).wait()

            @pl.when(co + 1 < CHUNKS)
            def _():
                own_load(co + 1).start()

            @pl.when(co >= 2)
            def _():
                tot_wait(co - 2)

            back_send(co).wait_recv()
            add_blocks([(tot_b.at[lax.rem(co, 2)], (0, 1))], [far_b.at[slot], own_b.at[slot]])
            tot_start(co)

            @pl.when(co < CHUNKS - RING)
            def _():
                give(1, far_r)

    def keep(slot, c):
        return pltpu.make_async_copy(stage.at[slot], zown.at[c], stage_sem.at[slot])

    part("grad_w_down")
    small[...] = jnp.zeros_like(small)

    def next_columns(j):
        @pl.when(j + 1 < D // TILE)
        def _():
            g_wait(j + 1, 0)
            g_start(j + 1, 5, 7)
            g_wait(j + 1, 3)
            g_start(j + 1, 2, 8)
            g_wait(j + 1, 1)
            g_start(j + 1, 9)
            g_wait(j + 1, 4)
            g_start(j + 1, 10)

        @pl.when(j + 2 < D // TILE)
        def _():
            g_start(j + 2, *OWN)

    @pl.loop(0, D // TILE)
    def _(j):
        @pl.when(j > 0)
        def _():
            next_columns(j)

        g_wait(j, 5)
        g_start(j, 11)
        g_wait(j, 2)
        g_start(j, 12)
        g_wait(j, 6, 7, 8, 9, 10, 11, 12)

        for h in range(FF // 512):
            product = dot(act[:, h * 512 : (h + 1) * 512], gf[:, span(j, TILE)], TN)
            stage[h, 0] = product[:TILE].astype(BF)
            stage[h, 1] = product[TILE:].astype(BF)
            keep(h, 2 * j + h).start()
            if h == 0:

                @pl.when(j == 0)
                def _():
                    keep(0, 0).wait()
                    chain_begin()

        @pl.when(j > 0)
        def _():
            keep(0, 2 * j).wait()

        keep(1, 2 * j + 1).wait()
        @pl.when(j == 0)
        def _():
            next_columns(0)

        near_tick(j)
        qkv_block(j)
        far_tick(j)

    tick0 = D // TILE

    def spread(unit, units, ticks, far_at):
        group = (unit * ticks) // units
        at = unit - (group * units + ticks - 1) // ticks

        @pl.when(at == 0)
        def _():
            near_tick(tick0 + group)

        @pl.when(at == far_at)
        def _():
            far_tick(tick0 + group)

    part("grad_up")
    ups = (T // 512) * (FF // TILE)
    rows_of = T // 512

    @pl.loop(0, ups + rows_of)
    def _(u):
        spread(u, ups + rows_of, 4, 2)

        @pl.when(u < ups)
        def _():
            rows = span(u // (FF // TILE), 512)
            n = lax.rem(u, FF // TILE)
            cols = span(n, TILE)
            ga = dot(gf[rows, :], wdown[cols, :], NT)
            gu = (ga * gp[rows, cols].astype(F32)).astype(BF)
            gp[rows, cols] = gu
            at = pl.ds(pl.multiple_of(3 * TILE + n * TILE, TILE), TILE)
            small[3:4, at] += jnp.sum(gu.astype(F32), axis=0, keepdims=True)

        @pl.when(u >= ups)
        def _():
            rows = span(u - ups, 512)
            dout[rows, :] = dot(gf[rows, :], wout[...], NT).astype(BF)

    tick0 += 4

    part("grad_w_up")

    def up_chunk(i):
        slot = lax.rem(i, 4)

        @pl.when(i >= 4)
        def _():
            keep(slot, 12 + i).wait()

        cols = span(lax.rem(i, 2), 2 * TILE)
        product = dot(nf[:, span(i // 2, TILE)], gp[:, cols], TN)
        stage[slot, 0] = product[:, :TILE].astype(BF)
        stage[slot, 1] = product[:, TILE:].astype(BF)
        keep(slot, 16 + i).start()

    near_tick(tick0)
    up_chunk(0)
    far_tick(tick0)

    @pl.loop(1, 4)
    def _(i):
        up_chunk(i)

    tick0 += 1

    heads = HC // HEAD_DIM
    blocks = SEQ // TILE

    def attend(seq, qb, pair):
        base = seq * SEQ
        kmax = (qb + 1) * TILE
        qrows = pl.ds(pl.multiple_of(base + qb * TILE, TILE), TILE)
        krows = pl.ds(pl.multiple_of(base, SEQ), kmax)
        two = range(2)
        lane_head = lax.broadcasted_iota(jnp.int32, (TILE, HC), 1) // HEAD_DIM
        keep_lane = [jnp.where(lane_head == 2 * pair + i, 1.0, 0.0) for i in two]
        q_all = qkv[0, qrows, :].astype(F32)
        do_all = dout[qrows, :].astype(F32)
        qh = [(q_all * keep_lane[i]).astype(BF) for i in two]
        doh32 = [do_all * keep_lane[i] for i in two]
        doh = [doh32[i].astype(BF) for i in two]
        keys = qkv[1, krows, :]
        vals = qkv[2, krows, :]
        allowed = (seg_col[qrows, 0:1].astype(F32) == seg_row[:, krows].astype(F32)) & (
            lax.broadcasted_iota(jnp.int32, (TILE, kmax), 1)
            <= lax.broadcasted_iota(jnp.int32, (TILE, kmax), 0) + qb * TILE
        )
        scores = [jnp.where(allowed, dot(qh[i], keys, NT), NEGATIVE) for i in two]
        dprobs = [dot(doh[i], vals, NT) for i in two]
        weights = [jnp.exp(x - jnp.max(x, axis=1, keepdims=True)) for x in scores]
        probs = [x * (1.0 / jnp.sum(x, axis=1, keepdims=True)) for x in weights]
        low = [x.astype(BF) for x in probs]
        out = [dot(low[i], vals, NN) * keep_lane[i] for i in two]
        o_acc[...] += out[0] + out[1]
        delta = [jnp.sum(doh32[i] * out[i], axis=1, keepdims=True) for i in two]
        ds = [(probs[i] * (dprobs[i] - delta[i])).astype(BF) for i in two]
        dq = [dot(ds[i], keys, NN) * keep_lane[i] for i in two]
        q_acc[...] += dq[0] + dq[1]
        dk_acc[0:kmax, :] += dot(ds[0], qh[0], TN) + dot(ds[1], qh[1], TN)
        dv_acc[0:kmax, :] += dot(low[0], doh[0], TN) + dot(low[1], doh[1], TN)

    part("attention")
    TICKS_OF = (1, 1, 2, 2)
    per_seq = sum(TICKS_OF)

    @pl.loop(0, T // SEQ)
    def _(seq):
        dk_acc[...] = jnp.zeros_like(dk_acc)
        dv_acc[...] = jnp.zeros_like(dv_acc)
        passed = 0
        for qb in range(blocks):
            n = TICKS_OF[qb]
            q_acc[...] = jnp.zeros_like(q_acc)
            o_acc[...] = jnp.zeros_like(o_acc)

            @pl.loop(0, heads // 2)
            def _(pair):
                i = seq * per_seq + passed + (pair * n) // (heads // 2)

                @pl.when(lax.rem(pair, heads // 2 // n) == 0)
                def _():
                    near_tick(tick0 + i)
                    up_chunk(4 + i)
                    far_tick(tick0 + i)

                attend(seq, qb, pair)

            passed += n
            qrows = pl.ds(pl.multiple_of(seq * SEQ + qb * TILE, TILE), TILE)
            att[qrows, :] = o_acc[...].astype(BF)
            dq = rope(q_acc[...] * (HEAD_DIM**-0.5), qrows, -1.0).astype(BF)
            dqkv[qrows, 0:HC] = dq
            small[3:4, 0:TILE] += jnp.sum(dq.astype(F32), axis=0, keepdims=True)

        @pl.loop(0, blocks)
        def _(b):
            rows = pl.ds(pl.multiple_of(seq * SEQ + b * TILE, TILE), TILE)
            dk = rope(dk_acc[span(b, TILE), :], rows, -1.0).astype(BF)
            dv = dv_acc[span(b, TILE), :].astype(BF)
            dqkv[rows, HC : 2 * HC] = dk
            dqkv[rows, 2 * HC : 3 * HC] = dv
            small[3:4, TILE : 2 * TILE] += jnp.sum(dk.astype(F32), axis=0, keepdims=True)
            small[3:4, 2 * TILE : 3 * TILE] += jnp.sum(
                dv.astype(F32), axis=0, keepdims=True
            )

    tick0 += (T // SEQ) * per_seq
    for q in range(4):
        keep(q, 28 + q).wait()

    part("grad_w_attention")
    near_tick(tick0)

    @pl.loop(0, 2)
    def _(i):
        product = dot(att[...], gf[:, span(i, 1024)], TN)
        for q in range(4):
            stage[2 * i + q // 2, q % 2] = product[:, q * TILE : (q + 1) * TILE].astype(BF)
        keep(2 * i, 32 + 2 * i).start()
        keep(2 * i + 1, 33 + 2 * i).start()

    far_tick(tick0)
    for q in range(4):
        keep(q, 32 + q).wait()
    tick0 += 1

    @pl.loop(0, D // TILE)
    def _(j):
        for kind in range(13):
            gcopy(gf, kind, j, span(j, TILE)).wait_send()

    def announce(which):
        for peer in (sib, xn, yn):
            pl.semaphore_signal(
                ready.at[which], inc=1, device_id=to(peer), device_id_type=MESH
            )

    announce(0)

    def qkv_rows(u):
        product = dot(nf[:, span(u, TILE)], dqkv[...], TN)
        for t in range(3):
            stage[t, lax.rem(u, 2)] = product[:, t * HC : (t + 1) * HC].astype(BF)

    def qkv_keep(u):
        return [keep(t, 36 + 3 * (u // 2) + t) for t in range(3)]

    near_tick(tick0)
    qkv_rows(0)
    far_tick(tick0)
    qkv_rows(1)
    for item in qkv_keep(1):
        item.start()
    for item in qkv_keep(1):
        item.wait()
    tick0 += 1
    part("ready")
    pl.semaphore_wait(ready.at[0], 3)

    CHIPS = ((1, 1), (1, 0), (0, 1), (0, 0))

    def reduce_rows(which, product, buf, tick0, extra):
        stages = (buf.at[0:R, :], mixed_o)

        def blk(b, h=None):
            if h is None:
                return buf.at[b * R : (b + 1) * R, :]
            return buf.at[b * R + h * half : b * R + (h + 1) * half, :]

        def send(kind, src, dst, target):
            return pltpu.make_async_remote_copy(
                src_ref=src,
                dst_ref=dst,
                send_sem=rs_send.at[which, kind],
                recv_sem=rs_recv.at[which, kind],
                device_id=to(target),
                device_id_type=MESH,
            )

        def to_sib(i):
            return send(i, stages[i % 2], blk(1 + i), sib)

        steps = {
            4: lambda: send(4, blk(1, 0), blk(5, 0), xn),
            5: lambda: send(5, blk(1, 1), blk(5, 1), yn),
            6: lambda: send(6, blk(2, 0), blk(6, 0), xn),
            7: lambda: send(7, blk(3, 1), blk(6, 1), yn),
            8: lambda: send(8, blk(3, 0), blk(7, 0), yn),
            9: lambda: send(9, blk(2, 1), blk(7, 1), xn),
        }

        def in_halves(step, tiles):
            near_tick(tick0 + step)
            pl.loop(0, D // WIDE // 2)(tiles)
            far_tick(tick0 + step)
            pl.loop(D // WIDE // 2, D // WIDE)(tiles)
            extra(step)

        def sib_part(i, step):
            if i >= 2:
                to_sib(i - 2).wait_send()
            mx, my = CHIPS[i]
            rows = span(other(mx, my, 1), R)
            ref = stages[i % 2]

            def tiles(n):
                ref[:, span(n, WIDE)] = product(rows, n).astype(BF)

            in_halves(step, tiles)
            to_sib(i).start()

        def own_part(i, step):
            mx, my = CHIPS[i]
            rows = span(other(mx, my, 0), R)
            to_sib(i).wait_recv()

            def tiles(n):
                cols = span(n, WIDE)
                total = product(rows, n) + buf[(1 + i) * R : (2 + i) * R, cols].astype(F32)
                buf[(1 + i) * R : (2 + i) * R, cols] = total.astype(BF)

            in_halves(step, tiles)

        def add_half(dst, src):
            (db, dh), (sb, sh) = dst, src

            @pl.loop(0, half // 32)
            def _(i):
                a = pl.ds(pl.multiple_of(db * R + dh * half + i * 32, 32), 32)
                b = pl.ds(pl.multiple_of(sb * R + sh * half + i * 32, 32), 32)
                buf[a, :] = (buf[a, :].astype(F32) + buf[b, :].astype(F32)).astype(BF)

        sib_part(0, 0)
        sib_part(1, 1)
        own_part(0, 2)
        steps[4]().start()
        steps[5]().start()
        sib_part(2, 3)
        own_part(1, 4)
        steps[6]().start()
        sib_part(3, 5)
        own_part(2, 6)
        steps[7]().start()
        own_part(3, 7)
        for i in (2, 3):
            to_sib(i).wait_send()

        def relay():
            steps[4]().wait_recv()
            add_half((3, 0), (5, 0))
            steps[8]().start()
            steps[5]().wait_recv()
            add_half((2, 1), (5, 1))
            steps[9]().start()

        def finish():
            for kind in (6, 7, 8, 9):
                steps[kind]().wait_recv()

        def drain():
            for kind in range(4, 10):
                steps[kind]().wait_send()

        def total_rows(i):
            at = [
                pl.ds(pl.multiple_of(b * R + i * LN_ROWS, LN_ROWS), LN_ROWS) for b in (4, 6, 7)
            ]
            return sum(buf[a, :].astype(F32) for a in at)

        return relay, finish, drain, total_rows

    def inner_product(rows, n):
        cols = span(n, WIDE)
        return dot(gp[rows, :], wup[cols, :], NT) + dot(dqkv[rows, :], wqkv[cols, :], NT)

    def outer_product(rows, n):
        cols = span(n, WIDE)
        return dot(act[rows, :], wdown[:, cols], NN) + dot(att[rows, :], wout[:, cols], NN)

    def more_qkv(i):
        if i < 6:
            if i % 2 == 0 and i > 0:
                for item in qkv_keep(1 + i):
                    item.wait()
            qkv_rows(2 + i)
            if i % 2 == 1:
                for item in qkv_keep(2 + i):
                    item.start()
        if i == 6:
            for item in qkv_keep(7):
                item.wait()

    relay2, finish2, drain2, rows2 = reduce_rows(0, inner_product, gf, tick0, more_qkv)
    relay2()
    tick0 += 8

    for kind in range(13):
        gcopy(nf, kind, 8, every).wait_send()
    announce(1)
    pl.semaphore_wait(ready.at[1], 3)
    part("scatter_outer")

    relay1, finish1, drain1, rows1 = reduce_rows(1, outer_product, nf, tick0, lambda i: None)
    tick0 += 8

    part("norm_backward")
    cot_load = pltpu.make_async_copy(gloc, mixed_o, w_sem.at[1])
    cot_load.start()
    near_tick(tick0)
    finish2()
    cot_load.wait()

    def norm_back(i):
        rows = span(i, LN_ROWS)
        scaled, inv = norm_rows(i)
        gn = rows2(i)
        cot = mixed_o[rows, :].astype(F32)
        g = gn * gain[...]
        back = g - jnp.mean(g, axis=1, keepdims=True)
        back = back - scaled * jnp.mean(g * scaled, axis=1, keepdims=True)
        mixed_o[rows, :] = (cot + back * inv).astype(BF)
        small[0:1, :] += jnp.sum(gn * scaled, axis=0, keepdims=True)
        small[1:2, :] += jnp.sum(gn, axis=0, keepdims=True)
        small[2:3, :] += jnp.sum(cot, axis=0, keepdims=True)

    pl.loop(0, 2)(norm_back)
    far_tick(tick0)
    pl.loop(2, R // LN_ROWS)(norm_back)
    gtok_store = pltpu.make_async_copy(mixed_o, gtok_o, w_sem.at[2])
    gtok_store.start()
    tick0 += 1

    part("small_sums")
    for step, peer in enumerate((sib, xn, yn)):
        copy = pltpu.make_async_remote_copy(
            src_ref=small,
            dst_ref=small_in.at[step],
            send_sem=sm_send.at[step],
            recv_sem=sm_recv.at[step],
            device_id=to(peer),
            device_id_type=MESH,
        )
        copy.start()
        near_tick(tick0 + step)
        if step == 0:
            relay1()
        copy.wait()
        small[0:3, :] += small_in[step, 0:3, :]
        far_tick(tick0 + step)

    tick0 += 3
    for step in (1, 2, 3):
        pltpu.make_async_remote_copy(
            src_ref=small,
            dst_ref=small_z.at[step - 1],
            send_sem=smz_send.at[step - 1],
            recv_sem=smz_recv.at[step - 1],
            device_id=to_rep(lax.rem(r + step, 4)),
            device_id_type=MESH,
        ).start()

    part("rest")

    @pl.loop(tick0, TICKS - 2)
    def _(k):
        near_tick(k)
        far_tick(k)

    part("output")
    finish1()
    gtok_store.wait()

    @pl.loop(0, R // LN_ROWS)
    def _(i):
        rows = span(i, LN_ROWS)
        total = tok[rows, :].astype(F32) + rows1(i) + bout[...] + bdown[...]
        mixed_o[rows, :] = total.astype(BF)

    drain2()
    drain1()

    for step in (1, 2, 3):
        pltpu.make_async_remote_copy(
            src_ref=small,
            dst_ref=small_z.at[step - 1],
            send_sem=smz_send.at[step - 1],
            recv_sem=smz_recv.at[step - 1],
            device_id=to_rep(lax.rem(r + step, 4)),
            device_id_type=MESH,
        ).wait()
    small_o[...] = small[...] + small_z[0] + small_z[1] + small_z[2]

    @pl.loop(TICKS - 2, TICKS)
    def _(k):
        near_tick(k)
        far_tick(k)

    part("last")
    for c in range(CHUNKS - RING, CHUNKS):

        @pl.when(outer)
        def _():
            near_send(c).wait_send()

        @pl.when(inner)
        def _():
            mid_send(c).wait_send()

    for c in (CHUNKS - 2, CHUNKS - 1):
        tot_wait(c)

        @pl.when(inner)
        def _():
            back_send(c).wait_send()

    scope.close()


PIECE_ROWS = 256


def widen(down_b, up_b, out_b, qkv_b, mixed_b, gtok_b, small, *refs):
    mixed_o, gtok_o, gain_o, shift_o, qkv_o, bqkv_o, up_o, bup_o, out_o, bout_o, down_o, bdown_o = refs[:12]
    scratch, load_sem, store_sem, pass_sem = refs[12:-3], *refs[-3:]
    D, FF = up_o.shape
    HC = out_o.shape[0]
    rows_b = scratch[8]
    passed = []
    for i, (src, dst) in enumerate(((mixed_b, mixed_o), (gtok_b, gtok_o))):
        load = pltpu.make_async_copy(src, rows_b.at[i], pass_sem.at[i])
        store = pltpu.make_async_copy(rows_b.at[i], dst, pass_sem.at[i])
        passed.append((load, store))
    work = []
    arrays = [(down_b, down_o), (up_b, up_o), (out_b, out_o)]
    arrays += [(qkv_b.at[t], qkv_o.at[t]) for t in range(3)]
    spaces = scratch[0:2], scratch[2:4], scratch[4:6]
    spaces += tuple(tuple(x.at[t] for x in scratch[6:8]) for t in range(3))
    for (src, dst), (low, wide) in zip(arrays, spaces):
        for row in range(0, src.shape[0], PIECE_ROWS):
            rows = pl.ds(row, PIECE_ROWS)
            n = len(work)
            load = pltpu.make_async_copy(src.at[rows, :], low.at[rows, :], load_sem.at[n])
            store = pltpu.make_async_copy(wide.at[rows, :], dst.at[rows, :], store_sem.at[n])
            work.append((load, store, low, wide, row))
    for load, *_ in work:
        load.start()
    for load, _ in passed:
        load.start()
    gain_o[...] = small[0, :]
    shift_o[...] = small[1, :]
    bout_o[...] = small[2, :]
    bdown_o[...] = small[2, :]
    for t in range(3):
        bqkv_o[t, :] = small[3, t * HC : (t + 1) * HC]
    bup_o[...] = small[3, 3 * HC : 3 * HC + FF]
    for load, store in passed:
        load.wait()
        store.start()
    for load, store, low, wide, row in work:
        load.wait()

        @pl.loop(0, PIECE_ROWS // 16)
        def _(i):
            at = pl.ds(pl.multiple_of(row + i * 16, 16), 16)
            wide[at, :] = low[at, :].astype(F32)

        store.start()
    for _, store, *_ in work:
        store.wait()
    for _, store in passed:
        store.wait()


def frequencies():
    lane = np.arange(128) % HEAD_DIM
    frequency = np.exp(-(lane % (ROT // 2)) * (2.0 * math.log(10000.0) / ROT))
    return np.where(lane < ROT, frequency, 0.0).astype(np.float32)[None]


def fused_body(
    tokens,
    segments,
    positions,
    ln_gain,
    ln_bias,
    w_qkv,
    b_qkv,
    w_up,
    b_up,
    w_out,
    b_out,
    w_down,
    b_down,
    grad_out,
):
    _, R, D = tokens.shape
    T = R * lax.axis_size("shard")
    HC = w_qkv.shape[2]
    FF = w_up.shape[1]
    vmem = pl.BlockSpec(memory_space=pltpu.VMEM)
    hbm = pl.BlockSpec(memory_space=pl.ANY)
    block = (CHUNKS, 2, TILE, TILE)
    piece = (2, TILE, TILE)
    out_shape = (
        jax.ShapeDtypeStruct((R, D), BF),
        jax.ShapeDtypeStruct((R, D), BF),
        jax.ShapeDtypeStruct((8, D), F32),
        jax.ShapeDtypeStruct((FF, D), SUM),
        jax.ShapeDtypeStruct((D, FF), SUM),
        jax.ShapeDtypeStruct((HC, D), SUM),
        jax.ShapeDtypeStruct((3, D, HC), SUM),
        jax.ShapeDtypeStruct(block, BF),
    )
    dma = pltpu.SemaphoreType.DMA
    scratch = [
        pltpu.VMEM((T, D), BF),
        pltpu.VMEM((T, D), BF),
        pltpu.VMEM((T, FF), BF),
        pltpu.VMEM((T, FF), BF),
        pltpu.VMEM((3, T, HC), BF),
        pltpu.VMEM((T, HC), BF),
        pltpu.VMEM((T, HC), BF),
        pltpu.VMEM((T, 3 * HC), BF),
        pltpu.VMEM((SEQ, HC), F32),
        pltpu.VMEM((SEQ, HC), F32),
        pltpu.VMEM((TILE, HC), F32),
        pltpu.VMEM((TILE, HC), F32),
        pltpu.VMEM((D, 3 * HC), BF),
        pltpu.VMEM((D, FF), BF),
        pltpu.VMEM((HC, D), BF),
        pltpu.VMEM((FF, D), BF),
        pltpu.VMEM((T, 128), F32),
        pltpu.VMEM((T, 128), F32),
        pltpu.VMEM((T, 128), BF),
        pltpu.VMEM((4,) + piece, BF),
        pltpu.VMEM((RING,) + piece, BF),
        pltpu.VMEM((RING,) + piece, BF),
        pltpu.VMEM((RING,) + piece, BF),
        pltpu.VMEM((RING,) + piece, BF),
        pltpu.VMEM((2,) + piece, BF),
        pltpu.VMEM((2,) + piece, SUM),
        pltpu.VMEM((8, D), F32),
        pltpu.VMEM((3, 8, D), F32),
        pltpu.VMEM((3, 8, D), F32),
        dma((9, 13)),
        dma((9, 13)),
        dma((7,)),
        dma((4,)),
        dma((RING,)),
        dma((RING,)),
        dma((2,)),
        dma((2, 2)),
        dma((CHUNKS,)),
        dma((CHUNKS,)),
        dma((2, 10)),
        dma((2, 10)),
        dma((3,)),
        dma((3,)),
        dma((3,)),
        dma((3,)),
        pltpu.SemaphoreType.REGULAR((2,)),
        pltpu.SemaphoreType.REGULAR((3,)),
    ]
    mixed, gtok, small, g_down, g_up, g_out, g_qkv, _ = pl.pallas_call(
        fused,
        out_shape=out_shape,
        in_specs=[vmem, hbm, vmem, vmem, hbm, vmem, hbm, vmem, hbm, vmem, hbm] + [vmem] * 4,
        out_specs=(vmem, hbm, vmem, hbm, hbm, hbm, hbm, hbm),
        scratch_shapes=scratch,
        name="layer",
        compiler_params=pltpu.CompilerParams(
            collective_id=0, has_side_effects=True, vmem_limit_bytes=VMEM_BYTES
        ),
    )(
        tokens[0],
        grad_out[0],
        ln_gain[None],
        ln_bias[None],
        jnp.transpose(w_qkv, (1, 0, 2)),
        b_qkv,
        w_up,
        b_up[None],
        w_out,
        b_out[None],
        w_down,
        b_down[None],
        segments,
        positions,
        frequencies(),
    )
    pieces = (FF + D + HC + 3 * D) // PIECE_ROWS
    row = jax.ShapeDtypeStruct((D,), F32)
    outs = pl.pallas_call(
        widen,
        out_shape=(
            jax.ShapeDtypeStruct((R, D), BF),
            jax.ShapeDtypeStruct((R, D), BF),
            row,
            row,
            jax.ShapeDtypeStruct((3, D, HC), F32),
            jax.ShapeDtypeStruct((3, HC), F32),
            jax.ShapeDtypeStruct((D, FF), F32),
            jax.ShapeDtypeStruct((FF,), F32),
            jax.ShapeDtypeStruct((HC, D), F32),
            row,
            jax.ShapeDtypeStruct((FF, D), F32),
            row,
        ),
        in_specs=[hbm] * 6 + [vmem],
        out_specs=(hbm, hbm, vmem, vmem, hbm, vmem, hbm, vmem, hbm, vmem, hbm, vmem),
        scratch_shapes=[
            pltpu.VMEM((FF, D), BF),
            pltpu.VMEM((FF, D), F32),
            pltpu.VMEM((D, FF), BF),
            pltpu.VMEM((D, FF), F32),
            pltpu.VMEM((HC, D), BF),
            pltpu.VMEM((HC, D), F32),
            pltpu.VMEM((3, D, HC), BF),
            pltpu.VMEM((3, D, HC), F32),
            pltpu.VMEM((2, R, D), BF),
            dma((pieces,)),
            dma((pieces,)),
            dma((2,)),
        ],
        name="widen",
        compiler_params=pltpu.CompilerParams(vmem_limit_bytes=VMEM_BYTES),
    )(g_down, g_up, g_out, g_qkv, mixed, gtok, small)
    mixed, gtok, gain, shift, g_qkv, bqkv, g_up, bup, g_out, bout, g_down, bdown = outs
    return (
        mixed[None],
        gtok[None],
        gain,
        shift,
        jnp.transpose(g_qkv, (1, 0, 2)),
        bqkv,
        g_up,
        bup,
        g_out,
        bout,
        g_down,
        bdown,
    )


def fits_fused(mesh):
    return dict(mesh.shape) == {"shard": 8, "replica": 4}


def solution(mesh):
    placed = (
        P("replica", "shard", None),
        P("replica", None),
        P("replica", None),
        P(),
        P(),
        P(None, None, "shard"),
        P(None, "shard"),
        P(None, "shard"),
        P("shard"),
        P("shard", None),
        P(),
        P("shard", None),
        P(),
        P("replica", "shard", None),
    )
    return jax.shard_map(
        fused_body if fits_fused(mesh) else body,
        mesh=mesh,
        in_specs=placed,
        out_specs=(
            P("replica", "shard", None),
            P("replica", "shard", None),
            P(),
            P(),
            P(None, None, "shard"),
            P(None, "shard"),
            P(None, "shard"),
            P("shard"),
            P("shard", None),
            P(),
            P("shard", None),
            P(),
        ),
        check_vma=False,
    )
```

```python
import contextlib
import functools
import math

import jax
import jax.numpy as jnp
import numpy as np
from jax import lax
from jax.experimental import pallas as pl
from jax.experimental.pallas import tpu as pltpu
from jax.sharding import PartitionSpec as P

HEAD_DIM = 64
ROT = 32


EPSILON = 1e-05
NEGATIVE = -1e30
VMEM_BYTES = 64 * 1024 * 1024


def angles(positions):
    frequency = jnp.exp(jnp.arange(ROT // 2, dtype=jnp.float32) * (-2.0 * math.log(10000.0) / ROT))
    phase_angle = positions.astype(jnp.float32)[:, None] * frequency[None, :]
    return (jnp.cos(phase_angle), jnp.sin(phase_angle))


def rotate(heads_in, cosine_part, sine_part):
    half_rot = ROT // 2
    first_part = heads_in[..., :half_rot]
    second_part = heads_in[..., half_rot:ROT]
    cosine_rows = cosine_part[:, None, :]
    sine_rows = sine_part[:, None, :]
    return jnp.concatenate(
        [
            first_part * cosine_rows - second_part * sine_rows,
            second_part * cosine_rows + first_part * sine_rows,
            heads_in[..., ROT:],
        ],
        axis=-1,
    )


def layer_norm(token_rows, gain_vector, bias_vector):
    centered = token_rows - jnp.mean(token_rows, axis=1, keepdims=True)
    scaled = centered * lax.rsqrt(jnp.mean(centered * centered, axis=1, keepdims=True) + EPSILON)
    return scaled * gain_vector + bias_vector


def take_rows(array_in, row_start, row_count):
    return lax.dynamic_slice_in_dim(array_in, row_start, row_count, 0)


def body(
    tokens,
    segments,
    positions,
    ln_gain,
    ln_bias,
    w_qkv,
    b_qkv,
    w_up,
    b_up,
    w_out,
    b_out,
    w_down,
    b_down,
    grad_out,
):
    local_rows = tokens[0].astype(jnp.float32)
    tok_rows, model_width = local_rows.shape
    length = tok_rows * lax.axis_size("shard")
    head_cols = w_qkv.shape[2]
    heads_here = head_cols // HEAD_DIM
    qkv_cols = 3 * head_cols
    split_shape = (length, heads_here, HEAD_DIM)
    scale_factor = HEAD_DIM ** (-0.5)
    cosine_part, sine_part = angles(positions[0])
    seq_segments = segments[0]
    normed_full, norm_back = jax.vjp(layer_norm, local_rows, ln_gain, ln_bias)
    normed = normed_full.astype(jnp.bfloat16)
    w_inner = jnp.concatenate([w_qkv.reshape(model_width, qkv_cols), w_up], axis=1)
    b_inner = jnp.concatenate([b_qkv.reshape(qkv_cols), b_up])
    gathered = lax.all_gather(normed, "shard", axis=0, tiled=True)
    inner_proj = jnp.dot(gathered, w_inner, preferred_element_type=jnp.float32)
    inner_proj = inner_proj + b_inner
    queries = rotate(inner_proj[:, :head_cols].reshape(split_shape), cosine_part, sine_part).astype(
        jnp.bfloat16
    )
    keys_all = rotate(
        inner_proj[:, head_cols : 2 * head_cols].reshape(split_shape), cosine_part, sine_part
    ).astype(jnp.bfloat16)
    values_all = inner_proj[:, 2 * head_cols : qkv_cols].reshape(split_shape).astype(jnp.bfloat16)
    up_proj = inner_proj[:, qkv_cols:]
    activation = jax.nn.gelu(up_proj, approximate=True).astype(jnp.bfloat16)
    block_rows = math.gcd(length, 512)
    block_count = length // block_rows
    offsets_block = jnp.arange(block_rows, dtype=jnp.int32)

    def block_scores(query_block, key_block, query_start, key_start):
        scores = (
            jnp.einsum("qhe,khe->hqk", query_block, key_block, preferred_element_type=jnp.float32)
            * scale_factor
        )
        query_ids = query_start + offsets_block
        key_ids = key_start + offsets_block
        query_segs = take_rows(seq_segments, query_start, block_rows)
        key_segs = take_rows(seq_segments, key_start, block_rows)
        allowed = (query_ids[:, None] >= key_ids[None, :]) & (
            query_segs[:, None] == key_segs[None, :]
        )
        return jnp.where(allowed[None], scores, NEGATIVE)

    def attend(query_index):
        query_start = query_index * block_rows
        query_block = take_rows(queries, query_start, block_rows)

        def first_pass(key_index, row_stats):
            row_max, row_sum = row_stats
            key_start = key_index * block_rows
            scores = block_scores(
                query_block, take_rows(keys_all, key_start, block_rows), query_start, key_start
            )
            new_max = jnp.maximum(row_max, jnp.max(scores, axis=2))
            row_sum = row_sum * jnp.exp(row_max - new_max) + jnp.sum(
                jnp.exp(scores - new_max[:, :, None]), axis=2
            )
            return (new_max, row_sum)

        row_max, row_sum = lax.fori_loop(
            0,
            query_index + 1,
            first_pass,
            (
                jnp.full((heads_here, block_rows), NEGATIVE, jnp.float32),
                jnp.zeros((heads_here, block_rows), jnp.float32),
            ),
        )

        def second_pass(key_index, total_out):
            key_start = key_index * block_rows
            scores = block_scores(
                query_block, take_rows(keys_all, key_start, block_rows), query_start, key_start
            )
            probability = (jnp.exp(scores - row_max[:, :, None]) / row_sum[:, :, None]).astype(
                jnp.bfloat16
            )
            return total_out + jnp.einsum(
                "hqk,khe->qhe",
                probability,
                take_rows(values_all, key_start, block_rows),
                preferred_element_type=jnp.float32,
            )

        attended_block = lax.fori_loop(
            0,
            query_index + 1,
            second_pass,
            jnp.zeros((block_rows, heads_here, HEAD_DIM), jnp.float32),
        )
        return (attended_block, row_max, row_sum)

    attended_full, row_maxes, row_sums = lax.map(attend, jnp.arange(block_count, dtype=jnp.int32))
    attended_full = attended_full.reshape(length, head_cols)
    attended = attended_full.astype(jnp.bfloat16)
    outer_act = jnp.concatenate([attended, activation], axis=1)
    w_outer = jnp.concatenate([w_out, w_down], axis=0)
    branches = lax.psum_scatter(
        jnp.dot(
            take_rows(outer_act, jnp.int32(0), lax.axis_size("shard") * tok_rows),
            w_outer,
            preferred_element_type=jnp.float32,
        ).astype(jnp.bfloat16),
        "shard",
        scatter_dimension=0,
        tiled=True,
    ).astype(jnp.float32)
    mixed_out = (local_rows + branches + b_out + b_down).astype(jnp.bfloat16)
    cotangent = grad_out[0]
    shard_piece = lax.all_gather(cotangent, "shard", axis=0, tiled=True)
    act_rows = take_rows(outer_act, jnp.int32(0), shard_piece.shape[0])
    weight_sum = jnp.einsum("sa,sd->ad", act_rows, shard_piece, preferred_element_type=jnp.float32)
    back_rows = jnp.einsum("sd,ad->sa", shard_piece, w_outer, preferred_element_type=jnp.float32)
    grad_outer = weight_sum
    back_attended = back_rows[:, :head_cols].astype(jnp.bfloat16).reshape(split_shape)
    delta_all = jnp.sum(
        back_attended.astype(jnp.float32) * attended_full.reshape(split_shape), axis=2
    ).T

    def key_pass(key_index, grads_all):
        grad_query, grad_key, grad_value = grads_all
        key_start = key_index * block_rows
        key_block = take_rows(keys_all, key_start, block_rows)
        value_block = take_rows(values_all, key_start, block_rows)

        def query_pass(query_index, inner_state):
            grad_query, key_total, value_total = inner_state
            query_start = query_index * block_rows
            query_block = take_rows(queries, query_start, block_rows)
            back_block = take_rows(back_attended, query_start, block_rows)
            delta_block = lax.dynamic_slice_in_dim(delta_all, query_start, block_rows, 1)
            scores = block_scores(query_block, key_block, query_start, key_start)
            probability = (
                jnp.exp(scores - row_maxes[query_index][:, :, None])
                / row_sums[query_index][:, :, None]
            )
            grad_prob = jnp.einsum(
                "qhe,khe->hqk", back_block, value_block, preferred_element_type=jnp.float32
            )
            grad_scores = (probability * (grad_prob - delta_block[:, :, None])).astype(jnp.bfloat16)
            value_total = value_total + jnp.einsum(
                "hqk,qhe->khe",
                probability.astype(jnp.bfloat16),
                back_block,
                preferred_element_type=jnp.float32,
            )
            key_total = key_total + jnp.einsum(
                "hqk,qhe->khe", grad_scores, query_block, preferred_element_type=jnp.float32
            )
            query_rows = take_rows(grad_query, query_start, block_rows) + jnp.einsum(
                "hqk,khe->qhe", grad_scores, key_block, preferred_element_type=jnp.float32
            )
            grad_query = lax.dynamic_update_slice_in_dim(grad_query, query_rows, query_start, 0)
            return (grad_query, key_total, value_total)

        empty_block = jnp.zeros((block_rows, heads_here, HEAD_DIM), jnp.float32)
        grad_query, key_total, value_total = lax.fori_loop(
            key_index, block_count, query_pass, (grad_query, empty_block, empty_block)
        )
        grad_key = lax.dynamic_update_slice_in_dim(grad_key, key_total, key_start, 0)
        grad_value = lax.dynamic_update_slice_in_dim(grad_value, value_total, key_start, 0)
        return (grad_query, grad_key, grad_value)

    empty_all = jnp.zeros(split_shape, jnp.float32)
    grad_query, grad_key, grad_value = lax.fori_loop(
        0, block_count, key_pass, (empty_all, empty_all, empty_all)
    )
    grad_query = rotate(grad_query * scale_factor, cosine_part, -sine_part)
    grad_key = rotate(grad_key * scale_factor, cosine_part, -sine_part)
    _, gelu_back = jax.vjp(functools.partial(jax.nn.gelu, approximate=True), up_proj)
    grad_up = gelu_back(back_rows[:, head_cols:])[0]
    grad_inner_rows = jnp.concatenate(
        [
            grad_query.reshape(length, head_cols),
            grad_key.reshape(length, head_cols),
            grad_value.reshape(length, head_cols),
            grad_up,
        ],
        axis=1,
    ).astype(jnp.bfloat16)
    grad_normed = lax.psum_scatter(
        jnp.einsum(
            "sa,da->sd",
            take_rows(grad_inner_rows, jnp.int32(0), lax.axis_size("shard") * tok_rows),
            w_inner,
            preferred_element_type=jnp.float32,
        ).astype(jnp.bfloat16),
        "shard",
        scatter_dimension=0,
        tiled=True,
    ).astype(jnp.float32)
    grad_local, grad_gain, grad_shift = norm_back(grad_normed)
    grad_tokens = (cotangent.astype(jnp.float32) + grad_local).astype(jnp.bfloat16)
    bias_inner = jnp.sum(grad_inner_rows, axis=0, dtype=jnp.float32)
    grad_inner = jnp.einsum(
        "sd,sa->da", gathered, grad_inner_rows, preferred_element_type=jnp.float32
    )
    grad_gain, grad_shift, bias_out = lax.psum(
        (grad_gain, grad_shift, jnp.sum(cotangent, axis=0, dtype=jnp.float32)), ("shard", "replica")
    )
    grad_inner, bias_inner, grad_outer = (
        lax.psum(grad_inner.astype(jnp.bfloat16), "replica").astype(jnp.float32),
        lax.psum(bias_inner.astype(jnp.bfloat16), "replica").astype(jnp.float32),
        lax.psum(grad_outer.astype(jnp.bfloat16), "replica").astype(jnp.float32),
    )
    return (
        mixed_out[None],
        grad_tokens[None],
        grad_gain,
        grad_shift,
        grad_inner[:, :qkv_cols].reshape(model_width, 3, head_cols),
        bias_inner[:qkv_cols].reshape(3, head_cols),
        grad_inner[:, qkv_cols:],
        bias_inner[qkv_cols:],
        grad_outer[:head_cols],
        bias_out,
        grad_outer[head_cols:],
        bias_out,
    )


SEQ = 1024
TILE = 256
WIDE = 512
BF = jnp.bfloat16
F32 = jnp.float32
SUM = jnp.bfloat16
MESH = pl.DeviceIdType.MESH
NN = (((1,), (0,)), ((), ()))
NT = (((1,), (1,)), ((), ()))
TN = (((0,), (0,)), ((), ()))
CHUNKS = 48
RING = 3
LAG_INNER = 1
LAG_OUTER = 3
TICKS = CHUNKS + LAG_OUTER


def dot(left, right, dims):
    return lax.dot_general(left, right, dims, preferred_element_type=F32)


def span(index, size):
    return pl.ds(pl.multiple_of(index * size, size), size)


def fused(
    tok,
    gloc,
    gain,
    bias,
    wqkv_h,
    bqkv,
    wup_h,
    bup,
    wout_h,
    bout,
    wdown_h,
    bdown,
    seg_row,
    pos_row,
    freq,
    mixed_o,
    gtok_o,
    small_o,
    down_o,
    up_o,
    out_o,
    qkv_o,
    zown,
    nf,
    gf,
    act,
    gp,
    qkv,
    att,
    dout,
    dqkv,
    dk_acc,
    dv_acc,
    q_acc,
    o_acc,
    wqkv,
    wup,
    wout,
    wdown,
    cos_t,
    sin_t,
    seg_col,
    stage,
    near_b,
    far_b,
    own_b,
    send_n,
    send_f,
    tot_b,
    small,
    small_in,
    small_z,
    gat_send,
    gat_recv,
    w_sem,
    stage_sem,
    load_sem,
    nsend_sem,
    fsend_sem,
    tot_sem,
    near_sem,
    far_sem,
    rs_send,
    rs_recv,
    sm_send,
    sm_recv,
    smz_send,
    smz_recv,
    ready,
    credit,
):
    T, D = nf.shape
    R = tok.shape[0]
    FF = act.shape[1]
    half = R // 2
    s = lax.axis_index("shard")
    r = lax.axis_index("replica")
    core = lax.rem(s, 2)
    xb = lax.rem(s // 2, 2)
    yb = s // 4
    inner = (r == 1) | (r == 2)
    outer = (r == 0) | (r == 3)

    def other(mx, my, mc):
        cc = core + mc - 2 * core * mc
        xx = xb + mx - 2 * xb * mx
        yy = yb + my - 2 * yb * my
        return yy * 4 + xx * 2 + cc

    sib = other(0, 0, 1)
    xn = other(1, 0, 0)
    yn = other(0, 1, 0)
    diag = other(1, 1, 0)
    far_r = jnp.where(r == 0, 1, jnp.where(r == 1, 2, jnp.where(r == 2, 1, 2)))
    near_r = jnp.where(r == 1, 0, jnp.where(r == 2, 3, r))

    def to(shard_id):
        return {"shard": shard_id, "replica": r}

    def to_rep(rep_id):
        return {"shard": s, "replica": rep_id}

    scope = contextlib.ExitStack()

    def part(name):
        scope.close()
        scope.enter_context(jax.named_scope(name))

    part("norm")
    barrier = pltpu.get_barrier_semaphore()
    for peer in (sib, xn, yn):
        pl.semaphore_signal(barrier, inc=1, device_id=to(peer), device_id_type=MESH)
    for step in (1, 2, 3):
        pl.semaphore_signal(
            barrier, inc=1, device_id=to_rep(lax.rem(r + step, 4)), device_id_type=MESH
        )

    loads = [
        pltpu.make_async_copy(wup_h, wup, w_sem.at[0]),
        pltpu.make_async_copy(gloc, gf.at[span(s, R), :], w_sem.at[1]),
        pltpu.make_async_copy(wdown_h, wdown, w_sem.at[2]),
        pltpu.make_async_copy(wout_h, wout, w_sem.at[3]),
    ]
    HC = qkv.shape[2]
    for t in range(3):
        loads.append(
            pltpu.make_async_copy(
                wqkv_h.at[t], wqkv.at[:, t * HC : (t + 1) * HC], w_sem.at[4 + t]
            )
        )
    for item in loads:
        item.start()

    LN_ROWS = 32

    def norm_rows(i):
        x = tok[span(i, LN_ROWS), :].astype(F32)
        centered = x - jnp.mean(x, axis=1, keepdims=True)
        inv = lax.rsqrt(jnp.mean(centered * centered, axis=1, keepdims=True) + EPSILON)
        return centered * inv, inv

    @pl.loop(0, R // LN_ROWS)
    def _(i):
        scaled, _ = norm_rows(i)
        rows = pl.ds(pl.multiple_of(s * R + i * LN_ROWS, LN_ROWS), LN_ROWS)
        nf[rows, :] = (scaled * gain[...] + bias[...]).astype(BF)

    pl.semaphore_wait(barrier, 6)

    def piece(buf, owner, h, cols):
        if h is None:
            return buf.at[span(owner, R), cols]
        rows = pl.ds(pl.multiple_of(owner * R + h * half, half), half)
        return buf.at[rows, cols]

    GATHER = {
        0: (lambda: s, 0, lambda: xn),
        1: (lambda: s, 1, lambda: xn),
        2: (lambda: yn, 1, lambda: xn),
        3: (lambda: s, 1, lambda: yn),
        4: (lambda: s, 0, lambda: yn),
        5: (lambda: xn, 0, lambda: yn),
        6: (lambda: s, None, lambda: sib),
        7: (lambda: xn, 0, lambda: sib),
        8: (lambda: yn, 1, lambda: sib),
        9: (lambda: xn, 1, lambda: sib),
        10: (lambda: yn, 0, lambda: sib),
        11: (lambda: diag, 0, lambda: sib),
        12: (lambda: diag, 1, lambda: sib),
    }

    def gcopy(buf, kind, slot, cols):
        owner, h, target = GATHER[kind]
        ref = piece(buf, owner(), h, cols)
        return pltpu.make_async_remote_copy(
            src_ref=ref,
            dst_ref=ref,
            send_sem=gat_send.at[slot, kind],
            recv_sem=gat_recv.at[slot, kind],
            device_id=to(target()),
            device_id_type=MESH,
        )

    every = pl.ds(0, D)

    def n_start(*kinds):
        for kind in kinds:
            gcopy(nf, kind, 8, every).start()

    def n_wait(*kinds):
        for kind in kinds:
            gcopy(nf, kind, 8, every).wait_recv()

    def g_start(j, *kinds):
        for kind in kinds:
            gcopy(gf, kind, j, span(j, TILE)).start()

    def g_wait(j, *kinds):
        for kind in kinds:
            gcopy(gf, kind, j, span(j, TILE)).wait_recv()

    OWN = (0, 3, 6, 1, 4)
    part("gather_rows")
    n_start(*OWN)

    C0 = math.sqrt(2.0 / math.pi)
    C1 = 0.044715

    def up_block(owner):
        rows = span(owner, R)

        @pl.loop(0, FF // WIDE)
        def _(n):
            cols = span(n, WIDE)
            u = dot(nf[rows, :], wup[:, cols], NN) + bup[:, cols]
            sq = u * u
            t = jnp.tanh(C0 * (u + C1 * (sq * u)))
            cdf = 0.5 + 0.5 * t
            act[rows, cols] = (u * cdf).astype(BF)
            gp[rows, cols] = (
                cdf + (0.5 * C0) * u * (1.0 - t * t) * (1.0 + (3.0 * C1) * sq)
            ).astype(BF)

    def rope(z, rows, sign):
        parts = []
        for p in range(2):
            zp = z[:, p * 128 : (p + 1) * 128]
            c = cos_t[rows, :]
            sn = sin_t[rows, :]
            turned = pltpu.roll(zp, 112, 1) * sn - pltpu.roll(zp * sn, 16, 1)
            parts.append(zp * c + sign * turned)
        return jnp.concatenate(parts, axis=1)

    def qkv_block(owner):
        rows = span(owner, R)
        every_z = dot(nf[rows, :], wqkv[...], NN)
        for t in range(3):
            z = every_z[:, t * HC : (t + 1) * HC] + bqkv[t : t + 1, :]
            if t < 2:
                z = rope(z, rows, 1.0)
            z = z.astype(BF)
            if t == 0:
                z = (z.astype(F32) * (HEAD_DIM**-0.5)).astype(BF)
            qkv[t, rows, :] = z

    part("up_own")
    loads[0].wait()
    loads[1].wait()
    up_block(s)
    n_wait(6)
    up_block(sib)

    lane = lax.rem(lax.broadcasted_iota(jnp.int32, (128, 128), 1), HEAD_DIM)
    first = jnp.where(lane < ROT // 2, -1.0, 0.0)

    @pl.loop(0, T // 128)
    def _(i):
        rows = span(i, 128)
        line = seg_row[:, rows].astype(F32)
        seg_col[rows, :] = jnp.transpose(jnp.broadcast_to(line, (128, 128))).astype(BF)
        line = pos_row[:, rows].astype(F32)
        phase = jnp.transpose(jnp.broadcast_to(line, (128, 128))) * freq[...]
        cos_t[rows, :] = jnp.cos(phase)
        sin_t[rows, :] = jnp.sin(phase) * first

    part("relay")
    n_wait(0)
    n_start(5, 7)
    n_wait(3)
    n_start(2, 8)
    g_start(0, *OWN)
    n_wait(1)
    n_start(9)
    n_wait(4)
    n_start(10)
    n_wait(7, 8, 9, 10)

    part("up_next")

    @pl.loop(0, 2)
    def _(mc):
        up_block(other(1, 0, mc))
        up_block(other(0, 1, mc))

    part("relay_far")
    n_wait(5)
    n_start(11)
    n_wait(2)
    n_start(12)
    up_block(diag)
    g_wait(0, 0)
    g_start(0, 5, 7)
    g_wait(0, 3)
    g_start(0, 2, 8)
    g_start(1, *OWN)
    g_wait(0, 1)
    g_start(0, 9)
    g_wait(0, 4)
    g_start(0, 10)
    n_wait(11, 12)
    up_block(other(1, 1, 1))

    for item in loads[2:]:
        item.wait()

    def near_send(c):
        return pltpu.make_async_remote_copy(
            src_ref=zown.at[c],
            dst_ref=near_b.at[lax.rem(c, RING)],
            send_sem=nsend_sem.at[lax.rem(c, RING)],
            recv_sem=near_sem.at[c],
            device_id=to_rep(far_r),
            device_id_type=MESH,
        )

    def mid_send(c):
        return pltpu.make_async_remote_copy(
            src_ref=send_n.at[lax.rem(c, RING)],
            dst_ref=far_b.at[lax.rem(c, RING)],
            send_sem=nsend_sem.at[lax.rem(c, RING)],
            recv_sem=far_sem.at[c],
            device_id=to_rep(far_r),
            device_id_type=MESH,
        )

    def back_send(c):
        return pltpu.make_async_remote_copy(
            src_ref=send_f.at[lax.rem(c, 2)],
            dst_ref=far_b.at[lax.rem(c, RING)],
            send_sem=fsend_sem.at[lax.rem(c, 2)],
            recv_sem=far_sem.at[c],
            device_id=to_rep(near_r),
            device_id_type=MESH,
        )

    def own_load(c):
        slot = lax.rem(c, RING)
        return pltpu.make_async_copy(zown.at[c], own_b.at[slot], load_sem.at[slot])

    def give(which, rep_id):
        pl.semaphore_signal(
            credit.at[which], inc=1, device_id=to_rep(rep_id), device_id_type=MESH
        )

    def tot_block(c, b, dst):
        slot = lax.rem(c, 2)
        return pltpu.make_async_copy(tot_b.at[slot, b], dst, tot_sem.at[slot, b])

    def tot_start(c):
        def down(b):
            return down_o.at[span(2 * lax.rem(c, 2) + b, TILE), span(c // 2, TILE)]

        def up(b):
            at = c - 16
            return up_o.at[span(at // 2, TILE), span(2 * lax.rem(at, 2) + b, TILE)]

        def out(b):
            return out_o.at[:, span(2 * (c - 32) + b, TILE)]

        def qkv(b):
            at = c - 36
            return qkv_o.at[lax.rem(at, 3), span(2 * (at // 3) + b, TILE), :]

        for low, high, place in ((0, 16, down), (16, 32, up), (32, 36, out), (36, 48, qkv)):

            @pl.when((c >= low) & (c < high))
            def _():
                for b in range(2):
                    tot_block(c, b, place(b)).start()

    def tot_wait(c):
        for b in range(2):
            tot_block(c, b, down_o.at[0:TILE, 0:TILE]).wait()

    def add_blocks(outs, ins):
        @pl.loop(0, 8)
        def _(i):
            rows = pl.ds(pl.multiple_of(lax.rem(i, 4) * 64, 64), 64)
            b = i // 4
            vals = [x[b, rows, :].astype(F32) for x in ins]
            for ref, which in outs:
                total = vals[which[0]]
                for w in which[1:]:
                    total = total + vals[w]
                ref[b, rows, :] = total.astype(ref.dtype)

    def within(c):
        return (c >= 0) & (c < CHUNKS)

    def chain_begin():
        own_load(0).start()

        @pl.when(outer)
        def _():
            near_send(0).start()

    def near_tick(k):
        @pl.when(outer & within(k + 1))
        def _():
            @pl.when(k + 1 >= RING)
            def _():
                near_send(k + 1 - RING).wait_send()
                pl.semaphore_wait(credit.at[2], 1)

            near_send(k + 1).start()

        @pl.when(inner & within(k))
        def _():
            slot = lax.rem(k, RING)
            own_load(k).wait()

            @pl.when(k + 1 < CHUNKS)
            def _():
                own_load(k + 1).start()

            @pl.when(k >= RING)
            def _():
                mid_send(k - RING).wait_send()
                pl.semaphore_wait(credit.at[0], 1)

            near_send(k).wait_recv()
            add_blocks([(send_n.at[slot], (0, 1))], [near_b.at[slot], own_b.at[slot]])
            mid_send(k).start()

            @pl.when(k < CHUNKS - RING)
            def _():
                give(2, near_r)

    def far_tick(k):
        ci = k - LAG_INNER

        @pl.when(inner & within(ci))
        def _():
            slot = lax.rem(ci, RING)
            two = lax.rem(ci, 2)

            @pl.when(ci >= 2)
            def _():
                back_send(ci - 2).wait_send()
                tot_wait(ci - 2)

            @pl.when(ci >= RING)
            def _():
                pl.semaphore_wait(credit.at[1], 1)

            mid_send(ci).wait_recv()
            add_blocks(
                [(send_f.at[two], (0, 1)), (tot_b.at[two], (0, 2))],
                [far_b.at[slot], own_b.at[slot], send_n.at[slot]],
            )
            back_send(ci).start()
            tot_start(ci)

            @pl.when(ci < CHUNKS - RING)
            def _():
                give(0, far_r)

        co = k - LAG_OUTER

        @pl.when(outer & within(co))
        def _():
            slot = lax.rem(co, RING)
            own_load(co).wait()

            @pl.when(co + 1 < CHUNKS)
            def _():
                own_load(co + 1).start()

            @pl.when(co >= 2)
            def _():
                tot_wait(co - 2)

            back_send(co).wait_recv()
            add_blocks([(tot_b.at[lax.rem(co, 2)], (0, 1))], [far_b.at[slot], own_b.at[slot]])
            tot_start(co)

            @pl.when(co < CHUNKS - RING)
            def _():
                give(1, far_r)

    def keep(slot, c):
        return pltpu.make_async_copy(stage.at[slot], zown.at[c], stage_sem.at[slot])

    part("grad_w_down")
    small[...] = jnp.zeros_like(small)

    def next_columns(j):
        @pl.when(j + 1 < D // TILE)
        def _():
            g_wait(j + 1, 0)
            g_start(j + 1, 5, 7)
            g_wait(j + 1, 3)
            g_start(j + 1, 2, 8)
            g_wait(j + 1, 1)
            g_start(j + 1, 9)
            g_wait(j + 1, 4)
            g_start(j + 1, 10)

        @pl.when(j + 2 < D // TILE)
        def _():
            g_start(j + 2, *OWN)

    @pl.loop(0, D // TILE)
    def _(j):
        @pl.when(j > 0)
        def _():
            next_columns(j)

        g_wait(j, 5)
        g_start(j, 11)
        g_wait(j, 2)
        g_start(j, 12)
        g_wait(j, 6, 7, 8, 9, 10, 11, 12)

        for h in range(FF // 512):
            product = dot(act[:, h * 512 : (h + 1) * 512], gf[:, span(j, TILE)], TN)
            stage[h, 0] = product[:TILE].astype(BF)
            stage[h, 1] = product[TILE:].astype(BF)
            keep(h, 2 * j + h).start()
            if h == 0:

                @pl.when(j == 0)
                def _():
                    keep(0, 0).wait()
                    chain_begin()

        @pl.when(j > 0)
        def _():
            keep(0, 2 * j).wait()

        keep(1, 2 * j + 1).wait()
        @pl.when(j == 0)
        def _():
            next_columns(0)

        near_tick(j)
        qkv_block(j)
        far_tick(j)

    tick0 = D // TILE

    def spread(unit, units, ticks, far_at):
        group = (unit * ticks) // units
        at = unit - (group * units + ticks - 1) // ticks

        @pl.when(at == 0)
        def _():
            near_tick(tick0 + group)

        @pl.when(at == far_at)
        def _():
            far_tick(tick0 + group)

    part("grad_up")
    ups = (T // 512) * (FF // TILE)
    rows_of = T // 512

    @pl.loop(0, ups + rows_of)
    def _(u):
        spread(u, ups + rows_of, 4, 2)

        @pl.when(u < ups)
        def _():
            rows = span(u // (FF // TILE), 512)
            n = lax.rem(u, FF // TILE)
            cols = span(n, TILE)
            ga = dot(gf[rows, :], wdown[cols, :], NT)
            gu = (ga * gp[rows, cols].astype(F32)).astype(BF)
            gp[rows, cols] = gu
            at = pl.ds(pl.multiple_of(3 * TILE + n * TILE, TILE), TILE)
            small[3:4, at] += jnp.sum(gu.astype(F32), axis=0, keepdims=True)

        @pl.when(u >= ups)
        def _():
            rows = span(u - ups, 512)
            dout[rows, :] = dot(gf[rows, :], wout[...], NT).astype(BF)

    tick0 += 4

    part("grad_w_up")

    def up_chunk(i):
        slot = lax.rem(i, 4)

        @pl.when(i >= 4)
        def _():
            keep(slot, 12 + i).wait()

        cols = span(lax.rem(i, 2), 2 * TILE)
        product = dot(nf[:, span(i // 2, TILE)], gp[:, cols], TN)
        stage[slot, 0] = product[:, :TILE].astype(BF)
        stage[slot, 1] = product[:, TILE:].astype(BF)
        keep(slot, 16 + i).start()

    near_tick(tick0)
    up_chunk(0)
    far_tick(tick0)

    @pl.loop(1, 4)
    def _(i):
        up_chunk(i)

    tick0 += 1

    heads = HC // HEAD_DIM
    blocks = SEQ // TILE

    def attend(seq, qb, pair):
        base = seq * SEQ
        kmax = (qb + 1) * TILE
        qrows = pl.ds(pl.multiple_of(base + qb * TILE, TILE), TILE)
        krows = pl.ds(pl.multiple_of(base, SEQ), kmax)
        two = range(2)
        lane_head = lax.broadcasted_iota(jnp.int32, (TILE, HC), 1) // HEAD_DIM
        keep_lane = [jnp.where(lane_head == 2 * pair + i, 1.0, 0.0) for i in two]
        q_all = qkv[0, qrows, :].astype(F32)
        do_all = dout[qrows, :].astype(F32)
        qh = [(q_all * keep_lane[i]).astype(BF) for i in two]
        doh32 = [do_all * keep_lane[i] for i in two]
        doh = [doh32[i].astype(BF) for i in two]
        keys = qkv[1, krows, :]
        vals = qkv[2, krows, :]
        allowed = (seg_col[qrows, 0:1].astype(F32) == seg_row[:, krows].astype(F32)) & (
            lax.broadcasted_iota(jnp.int32, (TILE, kmax), 1)
            <= lax.broadcasted_iota(jnp.int32, (TILE, kmax), 0) + qb * TILE
        )
        scores = [jnp.where(allowed, dot(qh[i], keys, NT), NEGATIVE) for i in two]
        dprobs = [dot(doh[i], vals, NT) for i in two]
        weights = [jnp.exp(x - jnp.max(x, axis=1, keepdims=True)) for x in scores]
        probs = [x * (1.0 / jnp.sum(x, axis=1, keepdims=True)) for x in weights]
        low = [x.astype(BF) for x in probs]
        out = [dot(low[i], vals, NN) * keep_lane[i] for i in two]
        o_acc[...] += out[0] + out[1]
        delta = [jnp.sum(doh32[i] * out[i], axis=1, keepdims=True) for i in two]
        ds = [(probs[i] * (dprobs[i] - delta[i])).astype(BF) for i in two]
        dq = [dot(ds[i], keys, NN) * keep_lane[i] for i in two]
        q_acc[...] += dq[0] + dq[1]
        dk_acc[0:kmax, :] += dot(ds[0], qh[0], TN) + dot(ds[1], qh[1], TN)
        dv_acc[0:kmax, :] += dot(low[0], doh[0], TN) + dot(low[1], doh[1], TN)

    part("attention")
    TICKS_OF = (1, 1, 2, 2)
    per_seq = sum(TICKS_OF)

    @pl.loop(0, T // SEQ)
    def _(seq):
        dk_acc[...] = jnp.zeros_like(dk_acc)
        dv_acc[...] = jnp.zeros_like(dv_acc)
        passed = 0
        for qb in range(blocks):
            n = TICKS_OF[qb]
            q_acc[...] = jnp.zeros_like(q_acc)
            o_acc[...] = jnp.zeros_like(o_acc)

            @pl.loop(0, heads // 2)
            def _(pair):
                i = seq * per_seq + passed + (pair * n) // (heads // 2)

                @pl.when(lax.rem(pair, heads // 2 // n) == 0)
                def _():
                    near_tick(tick0 + i)
                    up_chunk(4 + i)
                    far_tick(tick0 + i)

                attend(seq, qb, pair)

            passed += n
            qrows = pl.ds(pl.multiple_of(seq * SEQ + qb * TILE, TILE), TILE)
            att[qrows, :] = o_acc[...].astype(BF)
            dq = rope(q_acc[...] * (HEAD_DIM**-0.5), qrows, -1.0).astype(BF)
            dqkv[qrows, 0:HC] = dq
            small[3:4, 0:TILE] += jnp.sum(dq.astype(F32), axis=0, keepdims=True)

        @pl.loop(0, blocks)
        def _(b):
            rows = pl.ds(pl.multiple_of(seq * SEQ + b * TILE, TILE), TILE)
            dk = rope(dk_acc[span(b, TILE), :], rows, -1.0).astype(BF)
            dv = dv_acc[span(b, TILE), :].astype(BF)
            dqkv[rows, HC : 2 * HC] = dk
            dqkv[rows, 2 * HC : 3 * HC] = dv
            small[3:4, TILE : 2 * TILE] += jnp.sum(dk.astype(F32), axis=0, keepdims=True)
            small[3:4, 2 * TILE : 3 * TILE] += jnp.sum(
                dv.astype(F32), axis=0, keepdims=True
            )

    tick0 += (T // SEQ) * per_seq
    for q in range(4):
        keep(q, 28 + q).wait()

    part("grad_w_attention")
    near_tick(tick0)

    @pl.loop(0, 2)
    def _(i):
        product = dot(att[...], gf[:, span(i, 1024)], TN)
        for q in range(4):
            stage[2 * i + q // 2, q % 2] = product[:, q * TILE : (q + 1) * TILE].astype(BF)
        keep(2 * i, 32 + 2 * i).start()
        keep(2 * i + 1, 33 + 2 * i).start()

    far_tick(tick0)
    for q in range(4):
        keep(q, 32 + q).wait()
    tick0 += 1

    @pl.loop(0, D // TILE)
    def _(j):
        for kind in range(13):
            gcopy(gf, kind, j, span(j, TILE)).wait_send()

    def announce(which):
        for peer in (sib, xn, yn):
            pl.semaphore_signal(
                ready.at[which], inc=1, device_id=to(peer), device_id_type=MESH
            )

    announce(0)

    def qkv_rows(u):
        product = dot(nf[:, span(u, TILE)], dqkv[...], TN)
        for t in range(3):
            stage[t, lax.rem(u, 2)] = product[:, t * HC : (t + 1) * HC].astype(BF)

    def qkv_keep(u):
        return [keep(t, 36 + 3 * (u // 2) + t) for t in range(3)]

    near_tick(tick0)
    qkv_rows(0)
    far_tick(tick0)
    qkv_rows(1)
    for item in qkv_keep(1):
        item.start()
    for item in qkv_keep(1):
        item.wait()
    tick0 += 1
    part("ready")
    pl.semaphore_wait(ready.at[0], 3)

    def reduce_rows(which, product, buf, tick0, extra):
        def blk(b, h=None):
            if h is None:
                return buf.at[span(b, R), :]
            return buf.at[span(2 * b + h, half), :]

        def send(kind, src, dst, target):
            return pltpu.make_async_remote_copy(
                src_ref=src,
                dst_ref=dst,
                send_sem=rs_send.at[which, kind],
                recv_sem=rs_recv.at[which, kind],
                device_id=to(target),
                device_id_type=MESH,
            )

        def to_sib(i):
            return send(i, blk(0), blk(1 + i), sib)

        steps = {
            4: lambda: send(4, blk(1, 0), blk(5, 0), xn),
            5: lambda: send(5, blk(1, 1), blk(5, 1), yn),
            6: lambda: send(6, blk(2, 0), blk(6, 0), xn),
            7: lambda: send(7, blk(3, 1), blk(6, 1), yn),
            8: lambda: send(8, blk(3, 0), blk(7, 0), yn),
            9: lambda: send(9, blk(2, 1), blk(7, 1), xn),
        }

        def tiles(step, put):
            near_tick(tick0 + step)

            @pl.loop(0, D // WIDE)
            def _(n):
                @pl.when(n == D // WIDE // 2)
                def _():
                    far_tick(tick0 + step)

                put(span(n, WIDE), n)

            extra(step)

        @pl.loop(0, 5)
        def _(i):
            @pl.when(i < 4)
            def _():
                @pl.when(i > 0)
                def _():
                    to_sib(i - 1).wait_send()

                rows = span(other(1 - i // 2, 1 - lax.rem(i, 2), 1), R)

                def put(cols, n):
                    buf[0:R, cols] = product(rows, n).astype(BF)

                tiles(jnp.where(i == 0, 0, 2 * i - 1), put)
                to_sib(i).start()

            @pl.when(i > 0)
            def _():
                o = i - 1
                to_sib(o).wait_recv()
                rows = span(other(1 - o // 2, 1 - lax.rem(o, 2), 0), R)

                def put(cols, n):
                    total = product(rows, n) + buf[span(i, R), cols].astype(F32)
                    buf[span(i, R), cols] = total.astype(BF)

                tiles(jnp.where(o == 3, 7, 2 * o + 2), put)
                for at, kinds in ((0, (4, 5)), (1, (6,)), (2, (7,))):

                    @pl.when(o == at)
                    def _():
                        for kind in kinds:
                            steps[kind]().start()

        to_sib(3).wait_send()

        def add_half(dst, src):
            (db, dh), (sb, sh) = dst, src

            @pl.loop(0, half // 32)
            def _(i):
                a = pl.ds(pl.multiple_of(db * R + dh * half + i * 32, 32), 32)
                b = pl.ds(pl.multiple_of(sb * R + sh * half + i * 32, 32), 32)
                buf[a, :] = (buf[a, :].astype(F32) + buf[b, :].astype(F32)).astype(BF)

        def relay():
            steps[4]().wait_recv()
            add_half((3, 0), (5, 0))
            steps[8]().start()
            steps[5]().wait_recv()
            add_half((2, 1), (5, 1))
            steps[9]().start()

        def finish():
            for kind in (6, 7, 8, 9):
                steps[kind]().wait_recv()

        def drain():
            for kind in range(4, 10):
                steps[kind]().wait_send()

        def total_rows(i):
            at = [
                pl.ds(pl.multiple_of(b * R + i * LN_ROWS, LN_ROWS), LN_ROWS) for b in (4, 6, 7)
            ]
            return sum(buf[a, :].astype(F32) for a in at)

        return relay, finish, drain, total_rows

    def inner_product(rows, n):
        cols = span(n, WIDE)
        return dot(gp[rows, :], wup[cols, :], NT) + dot(dqkv[rows, :], wqkv[cols, :], NT)

    def outer_product(rows, n):
        cols = span(n, WIDE)
        return dot(act[rows, :], wdown[:, cols], NN) + dot(att[rows, :], wout[:, cols], NN)

    def more_qkv(step):
        @pl.when(step < 6)
        def _():
            @pl.when((step > 0) & (lax.rem(step, 2) == 0))
            def _():
                for item in qkv_keep(1 + step):
                    item.wait()

            qkv_rows(2 + step)

            @pl.when(lax.rem(step, 2) == 1)
            def _():
                for item in qkv_keep(2 + step):
                    item.start()

        @pl.when(step == 6)
        def _():
            for item in qkv_keep(7):
                item.wait()

    relay2, finish2, drain2, rows2 = reduce_rows(0, inner_product, gf, tick0, more_qkv)
    relay2()
    tick0 += 8

    for kind in range(13):
        gcopy(nf, kind, 8, every).wait_send()
    announce(1)
    pl.semaphore_wait(ready.at[1], 3)
    part("scatter_outer")
    cot_load = pltpu.make_async_copy(gloc, mixed_o, w_sem.at[1])
    cot_load.start()

    relay1, finish1, drain1, rows1 = reduce_rows(1, outer_product, nf, tick0, lambda i: None)
    tick0 += 8

    part("norm_backward")
    near_tick(tick0)
    finish2()
    cot_load.wait()

    def norm_back(i):
        rows = span(i, LN_ROWS)
        scaled, inv = norm_rows(i)
        gn = rows2(i)
        cot = mixed_o[rows, :].astype(F32)
        g = gn * gain[...]
        back = g - jnp.mean(g, axis=1, keepdims=True)
        back = back - scaled * jnp.mean(g * scaled, axis=1, keepdims=True)
        mixed_o[rows, :] = (cot + back * inv).astype(BF)
        small[0:1, :] += jnp.sum(gn * scaled, axis=0, keepdims=True)
        small[1:2, :] += jnp.sum(gn, axis=0, keepdims=True)
        small[2:3, :] += jnp.sum(cot, axis=0, keepdims=True)

    pl.loop(0, 2)(norm_back)
    far_tick(tick0)
    pl.loop(2, R // LN_ROWS)(norm_back)
    gtok_store = pltpu.make_async_copy(mixed_o, gtok_o, w_sem.at[2])
    gtok_store.start()
    tick0 += 1

    part("small_sums")
    for step, peer in enumerate((sib, xn, yn)):
        copy = pltpu.make_async_remote_copy(
            src_ref=small,
            dst_ref=small_in.at[step],
            send_sem=sm_send.at[step],
            recv_sem=sm_recv.at[step],
            device_id=to(peer),
            device_id_type=MESH,
        )
        copy.start()
        near_tick(tick0 + step)
        far_tick(tick0 + step)
        if step == 0:
            relay1()
        copy.wait()
        small[0:3, :] += small_in[step, 0:3, :]

    tick0 += 3
    for step in (1, 2, 3):
        pltpu.make_async_remote_copy(
            src_ref=small,
            dst_ref=small_z.at[step - 1],
            send_sem=smz_send.at[step - 1],
            recv_sem=smz_recv.at[step - 1],
            device_id=to_rep(lax.rem(r + step, 4)),
            device_id_type=MESH,
        ).start()

    part("rest")

    @pl.loop(tick0, TICKS - 2)
    def _(k):
        near_tick(k)
        far_tick(k)

    part("output")
    finish1()
    gtok_store.wait()

    @pl.loop(0, R // LN_ROWS)
    def _(i):
        rows = span(i, LN_ROWS)
        total = tok[rows, :].astype(F32) + rows1(i) + bout[...] + bdown[...]
        mixed_o[rows, :] = total.astype(BF)

    drain2()
    drain1()

    for step in (1, 2, 3):
        pltpu.make_async_remote_copy(
            src_ref=small,
            dst_ref=small_z.at[step - 1],
            send_sem=smz_send.at[step - 1],
            recv_sem=smz_recv.at[step - 1],
            device_id=to_rep(lax.rem(r + step, 4)),
            device_id_type=MESH,
        ).wait()
    small_o[...] = small[...] + small_z[0] + small_z[1] + small_z[2]

    @pl.loop(TICKS - 2, TICKS)
    def _(k):
        near_tick(k)
        far_tick(k)

    part("last")
    for c in range(CHUNKS - RING, CHUNKS):

        @pl.when(outer)
        def _():
            near_send(c).wait_send()

        @pl.when(inner)
        def _():
            mid_send(c).wait_send()

    for c in (CHUNKS - 2, CHUNKS - 1):
        tot_wait(c)

        @pl.when(inner)
        def _():
            back_send(c).wait_send()

    scope.close()


PIECE_ROWS = 256


def widen(down_b, up_b, out_b, qkv_b, mixed_b, gtok_b, small, *refs):
    mixed_o, gtok_o, gain_o, shift_o, qkv_o, bqkv_o, up_o, bup_o, out_o, bout_o, down_o, bdown_o = refs[:12]
    scratch, load_sem, store_sem, pass_sem = refs[12:-3], *refs[-3:]
    D, FF = up_o.shape
    HC = out_o.shape[0]
    rows_b = scratch[8]
    passed = []
    for i, (src, dst) in enumerate(((mixed_b, mixed_o), (gtok_b, gtok_o))):
        load = pltpu.make_async_copy(src, rows_b.at[i], pass_sem.at[i])
        store = pltpu.make_async_copy(rows_b.at[i], dst, pass_sem.at[i])
        passed.append((load, store))
    work = []
    arrays = [(down_b, down_o), (up_b, up_o), (out_b, out_o)]
    arrays += [(qkv_b.at[t], qkv_o.at[t]) for t in range(3)]
    spaces = scratch[0:2], scratch[2:4], scratch[4:6]
    spaces += tuple(tuple(x.at[t] for x in scratch[6:8]) for t in range(3))
    for (src, dst), (low, wide) in zip(arrays, spaces):
        for row in range(0, src.shape[0], PIECE_ROWS):
            rows = pl.ds(row, PIECE_ROWS)
            n = len(work)
            load = pltpu.make_async_copy(src.at[rows, :], low.at[rows, :], load_sem.at[n])
            store = pltpu.make_async_copy(wide.at[rows, :], dst.at[rows, :], store_sem.at[n])
            work.append((load, store, low, wide, row))
    for load, _ in passed:
        load.start()
    for load, *_ in work:
        load.start()
    gain_o[...] = small[0, :]
    shift_o[...] = small[1, :]
    bout_o[...] = small[2, :]
    bdown_o[...] = small[2, :]
    for t in range(3):
        bqkv_o[t, :] = small[3, t * HC : (t + 1) * HC]
    bup_o[...] = small[3, 3 * HC : 3 * HC + FF]
    for load, store in passed:
        load.wait()
        store.start()
    for load, store, low, wide, row in work:
        load.wait()

        @pl.loop(0, PIECE_ROWS // 16)
        def _(i):
            at = pl.ds(pl.multiple_of(row + i * 16, 16), 16)
            wide[at, :] = low[at, :].astype(F32)

        store.start()
    for _, store, *_ in work:
        store.wait()
    for _, store in passed:
        store.wait()


def frequencies():
    lane = np.arange(128) % HEAD_DIM
    frequency = np.exp(-(lane % (ROT // 2)) * (2.0 * math.log(10000.0) / ROT))
    return np.where(lane < ROT, frequency, 0.0).astype(np.float32)[None]


def fused_body(
    tokens,
    segments,
    positions,
    ln_gain,
    ln_bias,
    w_qkv,
    b_qkv,
    w_up,
    b_up,
    w_out,
    b_out,
    w_down,
    b_down,
    grad_out,
):
    _, R, D = tokens.shape
    T = R * lax.axis_size("shard")
    HC = w_qkv.shape[2]
    FF = w_up.shape[1]
    vmem = pl.BlockSpec(memory_space=pltpu.VMEM)
    hbm = pl.BlockSpec(memory_space=pl.ANY)
    block = (CHUNKS, 2, TILE, TILE)
    piece = (2, TILE, TILE)
    out_shape = (
        jax.ShapeDtypeStruct((R, D), BF),
        jax.ShapeDtypeStruct((R, D), BF),
        jax.ShapeDtypeStruct((8, D), F32),
        jax.ShapeDtypeStruct((FF, D), SUM),
        jax.ShapeDtypeStruct((D, FF), SUM),
        jax.ShapeDtypeStruct((HC, D), SUM),
        jax.ShapeDtypeStruct((3, D, HC), SUM),
        jax.ShapeDtypeStruct(block, BF),
    )
    dma = pltpu.SemaphoreType.DMA
    scratch = [
        pltpu.VMEM((T, D), BF),
        pltpu.VMEM((T, D), BF),
        pltpu.VMEM((T, FF), BF),
        pltpu.VMEM((T, FF), BF),
        pltpu.VMEM((3, T, HC), BF),
        pltpu.VMEM((T, HC), BF),
        pltpu.VMEM((T, HC), BF),
        pltpu.VMEM((T, 3 * HC), BF),
        pltpu.VMEM((SEQ, HC), F32),
        pltpu.VMEM((SEQ, HC), F32),
        pltpu.VMEM((TILE, HC), F32),
        pltpu.VMEM((TILE, HC), F32),
        pltpu.VMEM((D, 3 * HC), BF),
        pltpu.VMEM((D, FF), BF),
        pltpu.VMEM((HC, D), BF),
        pltpu.VMEM((FF, D), BF),
        pltpu.VMEM((T, 128), F32),
        pltpu.VMEM((T, 128), F32),
        pltpu.VMEM((T, 128), BF),
        pltpu.VMEM((4,) + piece, BF),
        pltpu.VMEM((RING,) + piece, BF),
        pltpu.VMEM((RING,) + piece, BF),
        pltpu.VMEM((RING,) + piece, BF),
        pltpu.VMEM((RING,) + piece, BF),
        pltpu.VMEM((2,) + piece, BF),
        pltpu.VMEM((2,) + piece, SUM),
        pltpu.VMEM((8, D), F32),
        pltpu.VMEM((3, 8, D), F32),
        pltpu.VMEM((3, 8, D), F32),
        dma((9, 13)),
        dma((9, 13)),
        dma((7,)),
        dma((4,)),
        dma((RING,)),
        dma((RING,)),
        dma((2,)),
        dma((2, 2)),
        dma((CHUNKS,)),
        dma((CHUNKS,)),
        dma((2, 10)),
        dma((2, 10)),
        dma((3,)),
        dma((3,)),
        dma((3,)),
        dma((3,)),
        pltpu.SemaphoreType.REGULAR((2,)),
        pltpu.SemaphoreType.REGULAR((3,)),
    ]
    mixed, gtok, small, g_down, g_up, g_out, g_qkv, _ = pl.pallas_call(
        fused,
        out_shape=out_shape,
        in_specs=[vmem, hbm, vmem, vmem, hbm, vmem, hbm, vmem, hbm, vmem, hbm] + [vmem] * 4,
        out_specs=(vmem, hbm, vmem, hbm, hbm, hbm, hbm, hbm),
        scratch_shapes=scratch,
        name="layer",
        compiler_params=pltpu.CompilerParams(
            collective_id=0, has_side_effects=True, vmem_limit_bytes=VMEM_BYTES
        ),
    )(
        tokens[0],
        grad_out[0],
        ln_gain[None],
        ln_bias[None],
        jnp.transpose(w_qkv, (1, 0, 2)),
        b_qkv,
        w_up,
        b_up[None],
        w_out,
        b_out[None],
        w_down,
        b_down[None],
        segments,
        positions,
        frequencies(),
    )
    pieces = (FF + D + HC + 3 * D) // PIECE_ROWS
    row = jax.ShapeDtypeStruct((D,), F32)
    outs = pl.pallas_call(
        widen,
        out_shape=(
            jax.ShapeDtypeStruct((R, D), BF),
            jax.ShapeDtypeStruct((R, D), BF),
            row,
            row,
            jax.ShapeDtypeStruct((3, D, HC), F32),
            jax.ShapeDtypeStruct((3, HC), F32),
            jax.ShapeDtypeStruct((D, FF), F32),
            jax.ShapeDtypeStruct((FF,), F32),
            jax.ShapeDtypeStruct((HC, D), F32),
            row,
            jax.ShapeDtypeStruct((FF, D), F32),
            row,
        ),
        in_specs=[hbm] * 6 + [vmem],
        out_specs=(hbm, hbm, vmem, vmem, hbm, vmem, hbm, vmem, hbm, vmem, hbm, vmem),
        scratch_shapes=[
            pltpu.VMEM((FF, D), BF),
            pltpu.VMEM((FF, D), F32),
            pltpu.VMEM((D, FF), BF),
            pltpu.VMEM((D, FF), F32),
            pltpu.VMEM((HC, D), BF),
            pltpu.VMEM((HC, D), F32),
            pltpu.VMEM((3, D, HC), BF),
            pltpu.VMEM((3, D, HC), F32),
            pltpu.VMEM((2, R, D), BF),
            dma((pieces,)),
            dma((pieces,)),
            dma((2,)),
        ],
        name="widen",
        compiler_params=pltpu.CompilerParams(vmem_limit_bytes=VMEM_BYTES),
    )(g_down, g_up, g_out, g_qkv, mixed, gtok, small)
    mixed, gtok, gain, shift, g_qkv, bqkv, g_up, bup, g_out, bout, g_down, bdown = outs
    return (
        mixed[None],
        gtok[None],
        gain,
        shift,
        jnp.transpose(g_qkv, (1, 0, 2)),
        bqkv,
        g_up,
        bup,
        g_out,
        bout,
        g_down,
        bdown,
    )


def fits_fused(mesh):
    return dict(mesh.shape) == {"shard": 8, "replica": 4}


def solution(mesh):
    placed = (
        P("replica", "shard", None),
        P("replica", None),
        P("replica", None),
        P(),
        P(),
        P(None, None, "shard"),
        P(None, "shard"),
        P(None, "shard"),
        P("shard"),
        P("shard", None),
        P(),
        P("shard", None),
        P(),
        P("replica", "shard", None),
    )
    return jax.shard_map(
        fused_body if fits_fused(mesh) else body,
        mesh=mesh,
        in_specs=placed,
        out_specs=(
            P("replica", "shard", None),
            P("replica", "shard", None),
            P(),
            P(),
            P(None, None, "shard"),
            P(None, "shard"),
            P(None, "shard"),
            P("shard"),
            P("shard", None),
            P(),
            P("shard", None),
            P(),
        ),
        check_vma=False,
    )
```

```python
import contextlib
import functools
import math

import jax
import jax.numpy as jnp
import numpy as np
from jax import lax
from jax.experimental import pallas as pl
from jax.experimental.pallas import tpu as pltpu
from jax.sharding import PartitionSpec as P

HEAD_DIM = 64
ROT = 32


EPSILON = 1e-05
NEGATIVE = -1e30
VMEM_BYTES = 64 * 1024 * 1024


def angles(positions):
    frequency = jnp.exp(jnp.arange(ROT // 2, dtype=jnp.float32) * (-2.0 * math.log(10000.0) / ROT))
    phase_angle = positions.astype(jnp.float32)[:, None] * frequency[None, :]
    return (jnp.cos(phase_angle), jnp.sin(phase_angle))


def rotate(heads_in, cosine_part, sine_part):
    half_rot = ROT // 2
    first_part = heads_in[..., :half_rot]
    second_part = heads_in[..., half_rot:ROT]
    cosine_rows = cosine_part[:, None, :]
    sine_rows = sine_part[:, None, :]
    return jnp.concatenate(
        [
            first_part * cosine_rows - second_part * sine_rows,
            second_part * cosine_rows + first_part * sine_rows,
            heads_in[..., ROT:],
        ],
        axis=-1,
    )


def layer_norm(token_rows, gain_vector, bias_vector):
    centered = token_rows - jnp.mean(token_rows, axis=1, keepdims=True)
    scaled = centered * lax.rsqrt(jnp.mean(centered * centered, axis=1, keepdims=True) + EPSILON)
    return scaled * gain_vector + bias_vector


def take_rows(array_in, row_start, row_count):
    return lax.dynamic_slice_in_dim(array_in, row_start, row_count, 0)


def body(
    tokens,
    segments,
    positions,
    ln_gain,
    ln_bias,
    w_qkv,
    b_qkv,
    w_up,
    b_up,
    w_out,
    b_out,
    w_down,
    b_down,
    grad_out,
):
    local_rows = tokens[0].astype(jnp.float32)
    tok_rows, model_width = local_rows.shape
    length = tok_rows * lax.axis_size("shard")
    head_cols = w_qkv.shape[2]
    heads_here = head_cols // HEAD_DIM
    qkv_cols = 3 * head_cols
    split_shape = (length, heads_here, HEAD_DIM)
    scale_factor = HEAD_DIM ** (-0.5)
    cosine_part, sine_part = angles(positions[0])
    seq_segments = segments[0]
    normed_full, norm_back = jax.vjp(layer_norm, local_rows, ln_gain, ln_bias)
    normed = normed_full.astype(jnp.bfloat16)
    w_inner = jnp.concatenate([w_qkv.reshape(model_width, qkv_cols), w_up], axis=1)
    b_inner = jnp.concatenate([b_qkv.reshape(qkv_cols), b_up])
    gathered = lax.all_gather(normed, "shard", axis=0, tiled=True)
    inner_proj = jnp.dot(gathered, w_inner, preferred_element_type=jnp.float32)
    inner_proj = inner_proj + b_inner
    queries = rotate(inner_proj[:, :head_cols].reshape(split_shape), cosine_part, sine_part).astype(
        jnp.bfloat16
    )
    keys_all = rotate(
        inner_proj[:, head_cols : 2 * head_cols].reshape(split_shape), cosine_part, sine_part
    ).astype(jnp.bfloat16)
    values_all = inner_proj[:, 2 * head_cols : qkv_cols].reshape(split_shape).astype(jnp.bfloat16)
    up_proj = inner_proj[:, qkv_cols:]
    activation = jax.nn.gelu(up_proj, approximate=True).astype(jnp.bfloat16)
    block_rows = math.gcd(length, 512)
    block_count = length // block_rows
    offsets_block = jnp.arange(block_rows, dtype=jnp.int32)

    def block_scores(query_block, key_block, query_start, key_start):
        scores = (
            jnp.einsum("qhe,khe->hqk", query_block, key_block, preferred_element_type=jnp.float32)
            * scale_factor
        )
        query_ids = query_start + offsets_block
        key_ids = key_start + offsets_block
        query_segs = take_rows(seq_segments, query_start, block_rows)
        key_segs = take_rows(seq_segments, key_start, block_rows)
        allowed = (query_ids[:, None] >= key_ids[None, :]) & (
            query_segs[:, None] == key_segs[None, :]
        )
        return jnp.where(allowed[None], scores, NEGATIVE)

    def attend(query_index):
        query_start = query_index * block_rows
        query_block = take_rows(queries, query_start, block_rows)

        def first_pass(key_index, row_stats):
            row_max, row_sum = row_stats
            key_start = key_index * block_rows
            scores = block_scores(
                query_block, take_rows(keys_all, key_start, block_rows), query_start, key_start
            )
            new_max = jnp.maximum(row_max, jnp.max(scores, axis=2))
            row_sum = row_sum * jnp.exp(row_max - new_max) + jnp.sum(
                jnp.exp(scores - new_max[:, :, None]), axis=2
            )
            return (new_max, row_sum)

        row_max, row_sum = lax.fori_loop(
            0,
            query_index + 1,
            first_pass,
            (
                jnp.full((heads_here, block_rows), NEGATIVE, jnp.float32),
                jnp.zeros((heads_here, block_rows), jnp.float32),
            ),
        )

        def second_pass(key_index, total_out):
            key_start = key_index * block_rows
            scores = block_scores(
                query_block, take_rows(keys_all, key_start, block_rows), query_start, key_start
            )
            probability = (jnp.exp(scores - row_max[:, :, None]) / row_sum[:, :, None]).astype(
                jnp.bfloat16
            )
            return total_out + jnp.einsum(
                "hqk,khe->qhe",
                probability,
                take_rows(values_all, key_start, block_rows),
                preferred_element_type=jnp.float32,
            )

        attended_block = lax.fori_loop(
            0,
            query_index + 1,
            second_pass,
            jnp.zeros((block_rows, heads_here, HEAD_DIM), jnp.float32),
        )
        return (attended_block, row_max, row_sum)

    attended_full, row_maxes, row_sums = lax.map(attend, jnp.arange(block_count, dtype=jnp.int32))
    attended_full = attended_full.reshape(length, head_cols)
    attended = attended_full.astype(jnp.bfloat16)
    outer_act = jnp.concatenate([attended, activation], axis=1)
    w_outer = jnp.concatenate([w_out, w_down], axis=0)
    branches = lax.psum_scatter(
        jnp.dot(
            take_rows(outer_act, jnp.int32(0), lax.axis_size("shard") * tok_rows),
            w_outer,
            preferred_element_type=jnp.float32,
        ).astype(jnp.bfloat16),
        "shard",
        scatter_dimension=0,
        tiled=True,
    ).astype(jnp.float32)
    mixed_out = (local_rows + branches + b_out + b_down).astype(jnp.bfloat16)
    cotangent = grad_out[0]
    shard_piece = lax.all_gather(cotangent, "shard", axis=0, tiled=True)
    act_rows = take_rows(outer_act, jnp.int32(0), shard_piece.shape[0])
    weight_sum = jnp.einsum("sa,sd->ad", act_rows, shard_piece, preferred_element_type=jnp.float32)
    back_rows = jnp.einsum("sd,ad->sa", shard_piece, w_outer, preferred_element_type=jnp.float32)
    grad_outer = weight_sum
    back_attended = back_rows[:, :head_cols].astype(jnp.bfloat16).reshape(split_shape)
    delta_all = jnp.sum(
        back_attended.astype(jnp.float32) * attended_full.reshape(split_shape), axis=2
    ).T

    def key_pass(key_index, grads_all):
        grad_query, grad_key, grad_value = grads_all
        key_start = key_index * block_rows
        key_block = take_rows(keys_all, key_start, block_rows)
        value_block = take_rows(values_all, key_start, block_rows)

        def query_pass(query_index, inner_state):
            grad_query, key_total, value_total = inner_state
            query_start = query_index * block_rows
            query_block = take_rows(queries, query_start, block_rows)
            back_block = take_rows(back_attended, query_start, block_rows)
            delta_block = lax.dynamic_slice_in_dim(delta_all, query_start, block_rows, 1)
            scores = block_scores(query_block, key_block, query_start, key_start)
            probability = (
                jnp.exp(scores - row_maxes[query_index][:, :, None])
                / row_sums[query_index][:, :, None]
            )
            grad_prob = jnp.einsum(
                "qhe,khe->hqk", back_block, value_block, preferred_element_type=jnp.float32
            )
            grad_scores = (probability * (grad_prob - delta_block[:, :, None])).astype(jnp.bfloat16)
            value_total = value_total + jnp.einsum(
                "hqk,qhe->khe",
                probability.astype(jnp.bfloat16),
                back_block,
                preferred_element_type=jnp.float32,
            )
            key_total = key_total + jnp.einsum(
                "hqk,qhe->khe", grad_scores, query_block, preferred_element_type=jnp.float32
            )
            query_rows = take_rows(grad_query, query_start, block_rows) + jnp.einsum(
                "hqk,khe->qhe", grad_scores, key_block, preferred_element_type=jnp.float32
            )
            grad_query = lax.dynamic_update_slice_in_dim(grad_query, query_rows, query_start, 0)
            return (grad_query, key_total, value_total)

        empty_block = jnp.zeros((block_rows, heads_here, HEAD_DIM), jnp.float32)
        grad_query, key_total, value_total = lax.fori_loop(
            key_index, block_count, query_pass, (grad_query, empty_block, empty_block)
        )
        grad_key = lax.dynamic_update_slice_in_dim(grad_key, key_total, key_start, 0)
        grad_value = lax.dynamic_update_slice_in_dim(grad_value, value_total, key_start, 0)
        return (grad_query, grad_key, grad_value)

    empty_all = jnp.zeros(split_shape, jnp.float32)
    grad_query, grad_key, grad_value = lax.fori_loop(
        0, block_count, key_pass, (empty_all, empty_all, empty_all)
    )
    grad_query = rotate(grad_query * scale_factor, cosine_part, -sine_part)
    grad_key = rotate(grad_key * scale_factor, cosine_part, -sine_part)
    _, gelu_back = jax.vjp(functools.partial(jax.nn.gelu, approximate=True), up_proj)
    grad_up = gelu_back(back_rows[:, head_cols:])[0]
    grad_inner_rows = jnp.concatenate(
        [
            grad_query.reshape(length, head_cols),
            grad_key.reshape(length, head_cols),
            grad_value.reshape(length, head_cols),
            grad_up,
        ],
        axis=1,
    ).astype(jnp.bfloat16)
    grad_normed = lax.psum_scatter(
        jnp.einsum(
            "sa,da->sd",
            take_rows(grad_inner_rows, jnp.int32(0), lax.axis_size("shard") * tok_rows),
            w_inner,
            preferred_element_type=jnp.float32,
        ).astype(jnp.bfloat16),
        "shard",
        scatter_dimension=0,
        tiled=True,
    ).astype(jnp.float32)
    grad_local, grad_gain, grad_shift = norm_back(grad_normed)
    grad_tokens = (cotangent.astype(jnp.float32) + grad_local).astype(jnp.bfloat16)
    bias_inner = jnp.sum(grad_inner_rows, axis=0, dtype=jnp.float32)
    grad_inner = jnp.einsum(
        "sd,sa->da", gathered, grad_inner_rows, preferred_element_type=jnp.float32
    )
    grad_gain, grad_shift, bias_out = lax.psum(
        (grad_gain, grad_shift, jnp.sum(cotangent, axis=0, dtype=jnp.float32)), ("shard", "replica")
    )
    grad_inner, bias_inner, grad_outer = (
        lax.psum(grad_inner.astype(jnp.bfloat16), "replica").astype(jnp.float32),
        lax.psum(bias_inner.astype(jnp.bfloat16), "replica").astype(jnp.float32),
        lax.psum(grad_outer.astype(jnp.bfloat16), "replica").astype(jnp.float32),
    )
    return (
        mixed_out[None],
        grad_tokens[None],
        grad_gain,
        grad_shift,
        grad_inner[:, :qkv_cols].reshape(model_width, 3, head_cols),
        bias_inner[:qkv_cols].reshape(3, head_cols),
        grad_inner[:, qkv_cols:],
        bias_inner[qkv_cols:],
        grad_outer[:head_cols],
        bias_out,
        grad_outer[head_cols:],
        bias_out,
    )


SEQ = 1024
TILE = 256
WIDE = 512
BF = jnp.bfloat16
F32 = jnp.float32
SUM = jnp.bfloat16
MESH = pl.DeviceIdType.MESH
NN = (((1,), (0,)), ((), ()))
NT = (((1,), (1,)), ((), ()))
TN = (((0,), (0,)), ((), ()))
CHUNKS = 48
RING = 3
LAG_INNER = 1
LAG_OUTER = 3
TICKS = CHUNKS + LAG_OUTER


def dot(left, right, dims):
    return lax.dot_general(left, right, dims, preferred_element_type=F32)


def span(index, size):
    return pl.ds(pl.multiple_of(index * size, size), size)


def fused(
    tok_h,
    gloc,
    gain,
    bias,
    wqkv_h,
    bqkv,
    wup_h,
    bup,
    wout_h,
    bout,
    wdown_h,
    bdown,
    seg_row,
    pos_row,
    freq,
    mixed_o,
    gtok_o,
    small_o,
    down_o,
    up_o,
    out_o,
    qkv_o,
    zown,
    tok,
    rows_b,
    nf,
    gf,
    act,
    gp,
    qkv,
    att,
    dout,
    dqkv,
    dk_acc,
    dv_acc,
    q_acc,
    o_acc,
    wqkv,
    wup,
    wout,
    wdown,
    turns,
    seg_col,
    stage,
    near_b,
    far_b,
    own_b,
    send_n,
    send_f,
    tot_b,
    small,
    small_in,
    small_z,
    gat_send,
    gat_recv,
    w_sem,
    stage_sem,
    load_sem,
    nsend_sem,
    fsend_sem,
    tot_sem,
    near_sem,
    far_sem,
    rs_send,
    rs_recv,
    sm_send,
    sm_recv,
    smz_send,
    smz_recv,
    ready,
    credit,
):
    T, D = nf.shape
    R = tok.shape[0]
    FF = act.shape[1]
    half = R // 2
    s = lax.axis_index("shard")
    r = lax.axis_index("replica")
    core = lax.rem(s, 2)
    xb = lax.rem(s // 2, 2)
    yb = s // 4
    inner = (r == 1) | (r == 2)
    outer = (r == 0) | (r == 3)

    def other(mx, my, mc):
        cc = core + mc - 2 * core * mc
        xx = xb + mx - 2 * xb * mx
        yy = yb + my - 2 * yb * my
        return yy * 4 + xx * 2 + cc

    sib = other(0, 0, 1)
    xn = other(1, 0, 0)
    yn = other(0, 1, 0)
    diag = other(1, 1, 0)
    far_r = jnp.where(r == 0, 1, jnp.where(r == 1, 2, jnp.where(r == 2, 1, 2)))
    near_r = jnp.where(r == 1, 0, jnp.where(r == 2, 3, r))

    def to(shard_id):
        return {"shard": shard_id, "replica": r}

    def to_rep(rep_id):
        return {"shard": s, "replica": rep_id}

    scope = contextlib.ExitStack()

    def part(name):
        scope.close()
        scope.enter_context(jax.named_scope(name))

    part("norm")
    barrier = pltpu.get_barrier_semaphore()
    for peer in (sib, xn, yn):
        pl.semaphore_signal(barrier, inc=1, device_id=to(peer), device_id_type=MESH)
    for step in (1, 2, 3):
        pl.semaphore_signal(
            barrier, inc=1, device_id=to_rep(lax.rem(r + step, 4)), device_id_type=MESH
        )

    tok_loads = [
        pltpu.make_async_copy(
            tok_h.at[span(h, half), :], tok.at[span(h, half), :], w_sem.at[7 + h]
        )
        for h in range(2)
    ]
    for item in tok_loads:
        item.start()
    loads = [
        pltpu.make_async_copy(wup_h, wup, w_sem.at[0]),
        pltpu.make_async_copy(gloc, gf.at[span(s, R), :], w_sem.at[1]),
        pltpu.make_async_copy(wdown_h, wdown, w_sem.at[2]),
        pltpu.make_async_copy(wout_h, wout, w_sem.at[3]),
    ]
    HC = qkv.shape[2]
    for t in range(3):
        loads.append(
            pltpu.make_async_copy(
                wqkv_h.at[t], wqkv.at[:, t * HC : (t + 1) * HC], w_sem.at[4 + t]
            )
        )
    for item in loads:
        item.start()

    LN_ROWS = 32

    def norm_rows(i):
        x = tok[span(i, LN_ROWS), :].astype(F32)
        centered = x - jnp.mean(x, axis=1, keepdims=True)
        inv = lax.rsqrt(jnp.mean(centered * centered, axis=1, keepdims=True) + EPSILON)
        return centered * inv, inv

    def norm_half(h):
        tok_loads[h].wait()

        @pl.loop(h * half // LN_ROWS, (h + 1) * half // LN_ROWS)
        def _(i):
            scaled, _ = norm_rows(i)
            rows = pl.ds(pl.multiple_of(s * R + i * LN_ROWS, LN_ROWS), LN_ROWS)
            nf[rows, :] = (scaled * gain[...] + bias[...]).astype(BF)

    norm_half(0)
    pl.semaphore_wait(barrier, 6)

    def piece(buf, owner, h, cols):
        if h is None:
            return buf.at[span(owner, R), cols]
        rows = pl.ds(pl.multiple_of(owner * R + h * half, half), half)
        return buf.at[rows, cols]

    GATHER = {
        0: (lambda: s, 0, lambda: xn),
        1: (lambda: s, 1, lambda: xn),
        2: (lambda: yn, 1, lambda: xn),
        3: (lambda: s, 1, lambda: yn),
        4: (lambda: s, 0, lambda: yn),
        5: (lambda: xn, 0, lambda: yn),
        6: (lambda: s, None, lambda: sib),
        7: (lambda: xn, 0, lambda: sib),
        8: (lambda: yn, 1, lambda: sib),
        9: (lambda: xn, 1, lambda: sib),
        10: (lambda: yn, 0, lambda: sib),
        11: (lambda: diag, 0, lambda: sib),
        12: (lambda: diag, 1, lambda: sib),
    }

    def gcopy(buf, kind, slot, cols):
        owner, h, target = GATHER[kind]
        ref = piece(buf, owner(), h, cols)
        return pltpu.make_async_remote_copy(
            src_ref=ref,
            dst_ref=ref,
            send_sem=gat_send.at[slot, kind],
            recv_sem=gat_recv.at[slot, kind],
            device_id=to(target()),
            device_id_type=MESH,
        )

    every = pl.ds(0, D)

    def n_start(*kinds):
        for kind in kinds:
            gcopy(nf, kind, 8, every).start()

    def n_wait(*kinds):
        for kind in kinds:
            gcopy(nf, kind, 8, every).wait_recv()

    def g_start(j, *kinds):
        for kind in kinds:
            gcopy(gf, kind, j, span(j, TILE)).start()

    def g_wait(j, *kinds):
        for kind in kinds:
            gcopy(gf, kind, j, span(j, TILE)).wait_recv()

    OWN = (0, 3, 6, 1, 4)
    part("gather_rows")
    n_start(0, 4)
    norm_half(1)
    n_start(3, 1, 6)

    C0 = math.sqrt(2.0 / math.pi)
    C1 = 0.044715

    def up_block(owner):
        rows = span(owner, R)

        @pl.loop(0, FF // WIDE)
        def _(n):
            cols = span(n, WIDE)
            u = dot(nf[rows, :], wup[:, cols], NN) + bup[:, cols]
            sq = u * u
            t = jnp.tanh(C0 * (u + C1 * (sq * u)))
            cdf = 0.5 + 0.5 * t
            act[rows, cols] = (u * cdf).astype(BF)
            gp[rows, cols] = (
                cdf + (0.5 * C0) * u * (1.0 - t * t) * (1.0 + (3.0 * C1) * sq)
            ).astype(BF)

    def rope(z, rows, sign):
        table = turns[rows, :]
        at = lax.rem(lax.broadcasted_iota(jnp.int32, table.shape, 1), HEAD_DIM)
        c = jnp.where(at < ROT, table, 1.0)
        sn = jnp.where(at < ROT // 2, pltpu.roll(table, 128 - ROT, 1), 0.0)
        parts = []
        for p in range(2):
            zp = z[:, p * 128 : (p + 1) * 128]
            turned = pltpu.roll(zp, 112, 1) * sn - pltpu.roll(zp * sn, 16, 1)
            parts.append(zp * c + sign * turned)
        return jnp.concatenate(parts, axis=1)

    def qkv_block(owner):
        rows = span(owner, R)
        every_z = dot(nf[rows, :], wqkv[...], NN)
        for t in range(3):
            z = every_z[:, t * HC : (t + 1) * HC] + bqkv[t : t + 1, :]
            if t < 2:
                z = rope(z, rows, 1.0)
            z = z.astype(BF)
            if t == 0:
                z = (z.astype(F32) * (HEAD_DIM**-0.5)).astype(BF)
            qkv[t, rows, :] = z

    part("up_own")
    loads[0].wait()
    loads[1].wait()
    up_block(s)
    n_wait(6)
    up_block(sib)

    lane = lax.rem(lax.broadcasted_iota(jnp.int32, (128, 128), 1), HEAD_DIM)

    @pl.loop(0, T // 128)
    def _(i):
        rows = span(i, 128)
        line = seg_row[:, rows].astype(F32)
        seg_col[rows, :] = jnp.transpose(jnp.broadcast_to(line, (128, 128))).astype(BF)
        line = pos_row[:, rows].astype(F32)
        phase = jnp.transpose(jnp.broadcast_to(line, (128, 128))) * freq[...]
        turns[rows, :] = jnp.where(lane < ROT, jnp.cos(phase), -jnp.sin(phase))

    for item in loads[4:]:
        item.wait()

    @pl.loop(0, 2)
    def _(mc):
        qkv_block(other(0, 0, mc))

    part("relay")
    n_wait(0)
    n_start(5, 7)
    n_wait(3)
    n_start(2, 8)
    g_start(0, *OWN)
    n_wait(1)
    n_start(9)
    n_wait(4)
    n_start(10)
    n_wait(7, 8, 9, 10)

    part("up_next")

    @pl.loop(0, 2)
    def _(mc):
        up_block(other(1, 0, mc))
        up_block(other(0, 1, mc))
        qkv_block(other(1, 0, mc))

    part("relay_far")
    n_wait(5)
    n_start(11)
    n_wait(2)
    n_start(12)
    g_wait(0, 0)
    g_start(0, 5, 7)
    g_wait(0, 3)
    g_start(0, 2, 8)
    g_start(1, *OWN)
    up_block(diag)
    g_wait(0, 1)
    g_start(0, 9)
    g_wait(0, 4)
    g_start(0, 10)
    g_wait(0, 5)
    g_start(0, 11)
    g_wait(0, 2)
    g_start(0, 12)
    n_wait(11, 12)
    up_block(other(1, 1, 1))

    for item in loads[2:4]:
        item.wait()

    def near_send(c):
        return pltpu.make_async_remote_copy(
            src_ref=zown.at[c],
            dst_ref=near_b.at[lax.rem(c, RING)],
            send_sem=nsend_sem.at[lax.rem(c, RING)],
            recv_sem=near_sem.at[c],
            device_id=to_rep(far_r),
            device_id_type=MESH,
        )

    def mid_send(c):
        return pltpu.make_async_remote_copy(
            src_ref=send_n.at[lax.rem(c, RING)],
            dst_ref=far_b.at[lax.rem(c, RING)],
            send_sem=nsend_sem.at[lax.rem(c, RING)],
            recv_sem=far_sem.at[c],
            device_id=to_rep(far_r),
            device_id_type=MESH,
        )

    def back_send(c):
        return pltpu.make_async_remote_copy(
            src_ref=send_f.at[lax.rem(c, 2)],
            dst_ref=far_b.at[lax.rem(c, RING)],
            send_sem=fsend_sem.at[lax.rem(c, 2)],
            recv_sem=far_sem.at[c],
            device_id=to_rep(near_r),
            device_id_type=MESH,
        )

    def own_load(c):
        slot = lax.rem(c, RING)
        return pltpu.make_async_copy(zown.at[c], own_b.at[slot], load_sem.at[slot])

    def give(which, rep_id):
        pl.semaphore_signal(
            credit.at[which], inc=1, device_id=to_rep(rep_id), device_id_type=MESH
        )

    def tot_block(c, b, dst):
        slot = lax.rem(c, 2)
        return pltpu.make_async_copy(tot_b.at[slot, b], dst, tot_sem.at[slot, b])

    def tot_start(c):
        def down(b):
            return down_o.at[span(2 * lax.rem(c, 2) + b, TILE), span(c // 2, TILE)]

        def up(b):
            at = c - 16
            return up_o.at[span(at // 2, TILE), span(2 * lax.rem(at, 2) + b, TILE)]

        def out(b):
            return out_o.at[:, span(2 * (c - 32) + b, TILE)]

        def qkv(b):
            at = c - 36
            return qkv_o.at[lax.rem(at, 3), span(2 * (at // 3) + b, TILE), :]

        for low, high, place in ((0, 16, down), (16, 32, up), (32, 36, out), (36, 48, qkv)):

            @pl.when((c >= low) & (c < high))
            def _():
                for b in range(2):
                    tot_block(c, b, place(b)).start()

    def tot_wait(c):
        for b in range(2):
            tot_block(c, b, down_o.at[0:TILE, 0:TILE]).wait()

    def add_blocks(outs, ins):
        @pl.loop(0, 8)
        def _(i):
            rows = pl.ds(pl.multiple_of(lax.rem(i, 4) * 64, 64), 64)
            b = i // 4
            vals = [x[b, rows, :].astype(F32) for x in ins]
            for ref, which in outs:
                total = vals[which[0]]
                for w in which[1:]:
                    total = total + vals[w]
                ref[b, rows, :] = total.astype(ref.dtype)

    def within(c):
        return (c >= 0) & (c < CHUNKS)

    def chain_begin():
        own_load(0).start()

        @pl.when(outer)
        def _():
            near_send(0).start()

    def near_tick(k):
        @pl.when(outer & within(k + 1))
        def _():
            @pl.when(k + 1 >= RING)
            def _():
                near_send(k + 1 - RING).wait_send()
                pl.semaphore_wait(credit.at[2], 1)

            near_send(k + 1).start()

        @pl.when(inner & within(k))
        def _():
            slot = lax.rem(k, RING)
            own_load(k).wait()

            @pl.when(k + 1 < CHUNKS)
            def _():
                own_load(k + 1).start()

            @pl.when(k >= RING)
            def _():
                mid_send(k - RING).wait_send()
                pl.semaphore_wait(credit.at[0], 1)

            near_send(k).wait_recv()
            add_blocks([(send_n.at[slot], (0, 1))], [near_b.at[slot], own_b.at[slot]])
            mid_send(k).start()

            @pl.when(k < CHUNKS - RING)
            def _():
                give(2, near_r)

    def far_tick(k):
        ci = k - LAG_INNER

        @pl.when(inner & within(ci))
        def _():
            slot = lax.rem(ci, RING)
            two = lax.rem(ci, 2)

            @pl.when(ci >= 2)
            def _():
                back_send(ci - 2).wait_send()
                tot_wait(ci - 2)

            @pl.when(ci >= RING)
            def _():
                pl.semaphore_wait(credit.at[1], 1)

            mid_send(ci).wait_recv()
            add_blocks(
                [(send_f.at[two], (0, 1)), (tot_b.at[two], (0, 2))],
                [far_b.at[slot], own_b.at[slot], send_n.at[slot]],
            )
            back_send(ci).start()
            tot_start(ci)

            @pl.when(ci < CHUNKS - RING)
            def _():
                give(0, far_r)

        co = k - LAG_OUTER

        @pl.when(outer & within(co))
        def _():
            slot = lax.rem(co, RING)
            own_load(co).wait()

            @pl.when(co + 1 < CHUNKS)
            def _():
                own_load(co + 1).start()

            @pl.when(co >= 2)
            def _():
                tot_wait(co - 2)

            back_send(co).wait_recv()
            add_blocks([(tot_b.at[lax.rem(co, 2)], (0, 1))], [far_b.at[slot], own_b.at[slot]])
            tot_start(co)

            @pl.when(co < CHUNKS - RING)
            def _():
                give(1, far_r)

    def keep(slot, c):
        return pltpu.make_async_copy(stage.at[slot], zown.at[c], stage_sem.at[slot])

    part("grad_w_down")
    small[...] = jnp.zeros_like(small)

    def next_columns(j):
        @pl.when(j + 1 < D // TILE)
        def _():
            g_wait(j + 1, 0)
            g_start(j + 1, 5, 7)
            g_wait(j + 1, 3)
            g_start(j + 1, 2, 8)
            g_wait(j + 1, 1)
            g_start(j + 1, 9)
            g_wait(j + 1, 4)
            g_start(j + 1, 10)

        @pl.when(j == 0)
        def _():
            g_start(2, *OWN)

        @pl.when(j + 3 < D // TILE)
        def _():
            g_start(j + 3, *OWN)

    @pl.loop(0, D // TILE)
    def _(j):
        @pl.when(j > 0)
        def _():
            next_columns(j)
            g_wait(j, 5)
            g_start(j, 11)
            g_wait(j, 2)
            g_start(j, 12)

        g_wait(j, 6, 7, 8, 9, 10, 11, 12)

        for h in range(FF // 512):
            product = dot(act[:, h * 512 : (h + 1) * 512], gf[:, span(j, TILE)], TN)
            stage[h, 0] = product[:TILE].astype(BF)
            stage[h, 1] = product[TILE:].astype(BF)
            keep(h, 2 * j + h).start()
            if h == 0:

                @pl.when(j == 0)
                def _():
                    keep(0, 0).wait()
                    chain_begin()

        @pl.when(j > 0)
        def _():
            keep(0, 2 * j).wait()

        keep(1, 2 * j + 1).wait()
        @pl.when(j == 0)
        def _():
            next_columns(0)

        near_tick(j)

        @pl.when(j >= 4)
        def _():
            qkv_block(other(j // 2 - 2, 1, lax.rem(j, 2)))

        far_tick(j)

    tick0 = D // TILE

    def spread(unit, units, ticks, far_at):
        group = (unit * ticks) // units
        at = unit - (group * units + ticks - 1) // ticks

        @pl.when(at == 0)
        def _():
            near_tick(tick0 + group)

        @pl.when(at == far_at)
        def _():
            far_tick(tick0 + group)

    part("grad_up")
    ups = (T // 512) * (FF // TILE)
    rows_of = T // 512

    @pl.loop(0, ups + rows_of)
    def _(u):
        spread(u, ups + rows_of, 4, 2)

        @pl.when(u < ups)
        def _():
            rows = span(u // (FF // TILE), 512)
            n = lax.rem(u, FF // TILE)
            cols = span(n, TILE)
            ga = dot(gf[rows, :], wdown[cols, :], NT)
            gu = (ga * gp[rows, cols].astype(F32)).astype(BF)
            gp[rows, cols] = gu
            at = pl.ds(pl.multiple_of(3 * TILE + n * TILE, TILE), TILE)
            small[3:4, at] += jnp.sum(gu.astype(F32), axis=0, keepdims=True)

        @pl.when(u >= ups)
        def _():
            rows = span(u - ups, 512)
            dout[rows, :] = dot(gf[rows, :], wout[...], NT).astype(BF)

    tick0 += 4

    part("grad_w_up")

    def up_chunk(i):
        slot = lax.rem(i, 4)

        @pl.when(i >= 4)
        def _():
            keep(slot, 12 + i).wait()

        cols = span(lax.rem(i, 2), 2 * TILE)
        product = dot(nf[:, span(i // 2, TILE)], gp[:, cols], TN)
        stage[slot, 0] = product[:, :TILE].astype(BF)
        stage[slot, 1] = product[:, TILE:].astype(BF)
        keep(slot, 16 + i).start()

    near_tick(tick0)
    up_chunk(0)
    far_tick(tick0)

    @pl.loop(1, 4)
    def _(i):
        up_chunk(i)

    tick0 += 1

    heads = HC // HEAD_DIM
    blocks = SEQ // TILE

    def attend(seq, qb, pair):
        base = seq * SEQ
        kmax = (qb + 1) * TILE
        qrows = pl.ds(pl.multiple_of(base + qb * TILE, TILE), TILE)
        krows = pl.ds(pl.multiple_of(base, SEQ), kmax)
        two = range(2)
        lane_head = lax.broadcasted_iota(jnp.int32, (TILE, HC), 1) // HEAD_DIM
        keep_lane = [jnp.where(lane_head == 2 * pair + i, 1.0, 0.0) for i in two]
        q_all = qkv[0, qrows, :].astype(F32)
        do_all = dout[qrows, :].astype(F32)
        qh = [(q_all * keep_lane[i]).astype(BF) for i in two]
        doh32 = [do_all * keep_lane[i] for i in two]
        doh = [doh32[i].astype(BF) for i in two]
        keys = qkv[1, krows, :]
        vals = qkv[2, krows, :]
        allowed = (seg_col[qrows, 0:1].astype(F32) == seg_row[:, krows].astype(F32)) & (
            lax.broadcasted_iota(jnp.int32, (TILE, kmax), 1)
            <= lax.broadcasted_iota(jnp.int32, (TILE, kmax), 0) + qb * TILE
        )
        scores = [jnp.where(allowed, dot(qh[i], keys, NT), NEGATIVE) for i in two]
        dprobs = [dot(doh[i], vals, NT) for i in two]
        weights = [jnp.exp(x - jnp.max(x, axis=1, keepdims=True)) for x in scores]
        probs = [x * (1.0 / jnp.sum(x, axis=1, keepdims=True)) for x in weights]
        low = [x.astype(BF) for x in probs]
        out = [dot(low[i], vals, NN) * keep_lane[i] for i in two]
        o_acc[...] += out[0] + out[1]
        delta = [jnp.sum(doh32[i] * out[i], axis=1, keepdims=True) for i in two]
        ds = [(probs[i] * (dprobs[i] - delta[i])).astype(BF) for i in two]
        dq = [dot(ds[i], keys, NN) * keep_lane[i] for i in two]
        q_acc[...] += dq[0] + dq[1]
        dk_acc[0:kmax, :] += dot(ds[0], qh[0], TN) + dot(ds[1], qh[1], TN)
        dv_acc[0:kmax, :] += dot(low[0], doh[0], TN) + dot(low[1], doh[1], TN)

    part("attention")
    TICKS_OF = (1, 1, 2, 2)
    per_seq = sum(TICKS_OF)

    @pl.loop(0, T // SEQ)
    def _(seq):
        dk_acc[...] = jnp.zeros_like(dk_acc)
        dv_acc[...] = jnp.zeros_like(dv_acc)
        passed = 0
        for qb in range(blocks):
            n = TICKS_OF[qb]
            q_acc[...] = jnp.zeros_like(q_acc)
            o_acc[...] = jnp.zeros_like(o_acc)

            @pl.loop(0, heads // 2)
            def _(pair):
                i = seq * per_seq + passed + (pair * n) // (heads // 2)

                @pl.when(lax.rem(pair, heads // 2 // n) == 0)
                def _():
                    near_tick(tick0 + i)
                    up_chunk(4 + i)
                    far_tick(tick0 + i)

                attend(seq, qb, pair)

            passed += n
            qrows = pl.ds(pl.multiple_of(seq * SEQ + qb * TILE, TILE), TILE)
            att[qrows, :] = o_acc[...].astype(BF)
            dq = rope(q_acc[...] * (HEAD_DIM**-0.5), qrows, -1.0).astype(BF)
            dqkv[qrows, 0:HC] = dq
            small[3:4, 0:TILE] += jnp.sum(dq.astype(F32), axis=0, keepdims=True)

        @pl.loop(0, blocks)
        def _(b):
            rows = pl.ds(pl.multiple_of(seq * SEQ + b * TILE, TILE), TILE)
            dk = rope(dk_acc[span(b, TILE), :], rows, -1.0).astype(BF)
            dv = dv_acc[span(b, TILE), :].astype(BF)
            dqkv[rows, HC : 2 * HC] = dk
            dqkv[rows, 2 * HC : 3 * HC] = dv
            small[3:4, TILE : 2 * TILE] += jnp.sum(dk.astype(F32), axis=0, keepdims=True)
            small[3:4, 2 * TILE : 3 * TILE] += jnp.sum(
                dv.astype(F32), axis=0, keepdims=True
            )

    tick0 += (T // SEQ) * per_seq
    for q in range(4):
        keep(q, 28 + q).wait()

    part("grad_w_attention")
    near_tick(tick0)

    @pl.loop(0, 2)
    def _(i):
        product = dot(att[...], gf[:, span(i, 1024)], TN)
        for q in range(4):
            stage[2 * i + q // 2, q % 2] = product[:, q * TILE : (q + 1) * TILE].astype(BF)
        keep(2 * i, 32 + 2 * i).start()
        keep(2 * i + 1, 33 + 2 * i).start()

    far_tick(tick0)
    for q in range(4):
        keep(q, 32 + q).wait()
    tick0 += 1

    @pl.loop(0, D // TILE)
    def _(j):
        for kind in range(13):
            gcopy(gf, kind, j, span(j, TILE)).wait_send()

    def announce(which):
        for peer in (sib, xn, yn):
            pl.semaphore_signal(
                ready.at[which], inc=1, device_id=to(peer), device_id_type=MESH
            )

    announce(0)

    def qkv_rows(u):
        product = dot(nf[:, span(u, TILE)], dqkv[...], TN)
        for t in range(3):
            stage[t, lax.rem(u, 2)] = product[:, t * HC : (t + 1) * HC].astype(BF)

    def qkv_keep(u):
        return [keep(t, 36 + 3 * (u // 2) + t) for t in range(3)]

    near_tick(tick0)
    qkv_rows(0)
    far_tick(tick0)
    qkv_rows(1)
    for item in qkv_keep(1):
        item.start()
    for item in qkv_keep(1):
        item.wait()
    tick0 += 1
    part("ready")
    pl.semaphore_wait(ready.at[0], 3)

    def reduce_rows(which, product, buf, tick0, extra):
        def blk(b, h=None):
            if h is None:
                return buf.at[span(b, R), :]
            return buf.at[span(2 * b + h, half), :]

        def send(kind, src, dst, target):
            return pltpu.make_async_remote_copy(
                src_ref=src,
                dst_ref=dst,
                send_sem=rs_send.at[which, kind],
                recv_sem=rs_recv.at[which, kind],
                device_id=to(target),
                device_id_type=MESH,
            )

        def to_sib(i):
            return send(i, blk(0), blk(1 + i), sib)

        steps = {
            4: lambda: send(4, blk(1, 0), blk(5, 0), xn),
            5: lambda: send(5, blk(1, 1), blk(5, 1), yn),
            6: lambda: send(6, blk(2, 0), blk(6, 0), xn),
            7: lambda: send(7, blk(3, 1), blk(6, 1), yn),
            8: lambda: send(8, blk(3, 0), blk(7, 0), yn),
            9: lambda: send(9, blk(2, 1), blk(7, 1), xn),
        }

        def tiles(step, put):
            near_tick(tick0 + step)

            @pl.loop(0, D // WIDE)
            def _(n):
                @pl.when(n == D // WIDE // 2)
                def _():
                    far_tick(tick0 + step)

                put(span(n, WIDE), n)

            extra(step)

        @pl.loop(0, 5)
        def _(i):
            @pl.when(i < 4)
            def _():
                @pl.when(i > 0)
                def _():
                    to_sib(i - 1).wait_send()

                rows = span(other(1 - i // 2, 1 - lax.rem(i, 2), 1), R)

                def put(cols, n):
                    buf[0:R, cols] = product(rows, n).astype(BF)

                tiles(jnp.where(i == 0, 0, 2 * i - 1), put)
                to_sib(i).start()

            @pl.when(i > 0)
            def _():
                o = i - 1
                to_sib(o).wait_recv()
                rows = span(other(1 - o // 2, 1 - lax.rem(o, 2), 0), R)

                def put(cols, n):
                    total = product(rows, n) + buf[span(i, R), cols].astype(F32)
                    buf[span(i, R), cols] = total.astype(BF)

                tiles(jnp.where(o == 3, 7, 2 * o + 2), put)
                for at, kinds in ((0, (4, 5)), (1, (6,)), (2, (7,))):

                    @pl.when(o == at)
                    def _():
                        for kind in kinds:
                            steps[kind]().start()

        to_sib(3).wait_send()

        def add_half(dst, src):
            (db, dh), (sb, sh) = dst, src

            @pl.loop(0, half // 32)
            def _(i):
                a = pl.ds(pl.multiple_of(db * R + dh * half + i * 32, 32), 32)
                b = pl.ds(pl.multiple_of(sb * R + sh * half + i * 32, 32), 32)
                buf[a, :] = (buf[a, :].astype(F32) + buf[b, :].astype(F32)).astype(BF)

        def relay():
            steps[4]().wait_recv()
            add_half((3, 0), (5, 0))
            steps[8]().start()
            steps[5]().wait_recv()
            add_half((2, 1), (5, 1))
            steps[9]().start()

        def finish():
            for kind in (6, 7, 8, 9):
                steps[kind]().wait_recv()

        def drain():
            for kind in range(4, 10):
                steps[kind]().wait_send()

        def total_rows(i):
            at = [
                pl.ds(pl.multiple_of(b * R + i * LN_ROWS, LN_ROWS), LN_ROWS) for b in (4, 6, 7)
            ]
            return sum(buf[a, :].astype(F32) for a in at)

        return relay, finish, drain, total_rows

    def inner_product(rows, n):
        cols = span(n, WIDE)
        return dot(gp[rows, :], wup[cols, :], NT) + dot(dqkv[rows, :], wqkv[cols, :], NT)

    def outer_product(rows, n):
        cols = span(n, WIDE)
        return dot(act[rows, :], wdown[:, cols], NN) + dot(att[rows, :], wout[:, cols], NN)

    def more_qkv(step):
        @pl.when(step < 6)
        def _():
            @pl.when((step > 0) & (lax.rem(step, 2) == 0))
            def _():
                for item in qkv_keep(1 + step):
                    item.wait()

            qkv_rows(2 + step)

            @pl.when(lax.rem(step, 2) == 1)
            def _():
                for item in qkv_keep(2 + step):
                    item.start()

        @pl.when(step == 6)
        def _():
            for item in qkv_keep(7):
                item.wait()

    relay2, finish2, drain2, rows2 = reduce_rows(0, inner_product, gf, tick0, more_qkv)
    relay2()
    tick0 += 8

    for kind in range(13):
        gcopy(nf, kind, 8, every).wait_send()
    announce(1)
    pl.semaphore_wait(ready.at[1], 3)
    part("scatter_outer")
    cot_load = pltpu.make_async_copy(gloc, rows_b, w_sem.at[1])
    cot_load.start()

    relay1, finish1, drain1, rows1 = reduce_rows(1, outer_product, nf, tick0, lambda i: None)
    tick0 += 8

    part("norm_backward")
    near_tick(tick0)
    finish2()
    cot_load.wait()

    def norm_back(i):
        rows = span(i, LN_ROWS)
        scaled, inv = norm_rows(i)
        gn = rows2(i)
        cot = rows_b[rows, :].astype(F32)
        g = gn * gain[...]
        back = g - jnp.mean(g, axis=1, keepdims=True)
        back = back - scaled * jnp.mean(g * scaled, axis=1, keepdims=True)
        rows_b[rows, :] = (cot + back * inv).astype(BF)
        small[0:1, :] += jnp.sum(gn * scaled, axis=0, keepdims=True)
        small[1:2, :] += jnp.sum(gn, axis=0, keepdims=True)
        small[2:3, :] += jnp.sum(cot, axis=0, keepdims=True)

    pl.loop(0, 2)(norm_back)
    far_tick(tick0)
    pl.loop(2, R // LN_ROWS)(norm_back)
    gtok_store = pltpu.make_async_copy(rows_b, gtok_o, w_sem.at[2])
    gtok_store.start()
    tick0 += 1

    part("small_sums")
    for step, peer in enumerate((sib, xn, yn)):
        copy = pltpu.make_async_remote_copy(
            src_ref=small,
            dst_ref=small_in.at[step],
            send_sem=sm_send.at[step],
            recv_sem=sm_recv.at[step],
            device_id=to(peer),
            device_id_type=MESH,
        )
        copy.start()
        if step != 1:
            near_tick(tick0 + step // 2)
            far_tick(tick0 + step // 2)
        if step == 0:
            relay1()
        copy.wait()
        small[0:3, :] += small_in[step, 0:3, :]

    tick0 += 2

    def small_send(i, rep_id):
        return pltpu.make_async_remote_copy(
            src_ref=small,
            dst_ref=small_z.at[i],
            send_sem=smz_send.at[i],
            recv_sem=smz_recv.at[i],
            device_id=to_rep(rep_id),
            device_id_type=MESH,
        )

    @pl.when(outer)
    def _():
        small_send(0, far_r).start()

    part("rest")

    @pl.loop(tick0, TICKS - 2)
    def _(k):
        near_tick(k)
        far_tick(k)

    @pl.when(inner)
    def _():
        small_send(0, far_r).wait_recv()
        small[...] += small_z[0]
        small_send(1, far_r).start()

    part("output")
    finish1()
    gtok_store.wait()

    @pl.loop(0, R // LN_ROWS)
    def _(i):
        rows = span(i, LN_ROWS)
        total = tok[rows, :].astype(F32) + rows1(i) + bout[...] + bdown[...]
        rows_b[rows, :] = total.astype(BF)

    mixed_store = pltpu.make_async_copy(rows_b, mixed_o, w_sem.at[4])
    mixed_store.start()
    drain2()
    drain1()

    @pl.loop(TICKS - 2, TICKS)
    def _(k):
        near_tick(k)
        far_tick(k)

    part("last")
    @pl.when(inner)
    def _():
        small_send(1, far_r).wait()
        small[...] += small_z[1]
        small_send(2, near_r).start()
        small_send(2, near_r).wait_send()

    @pl.when(outer)
    def _():
        small_send(0, far_r).wait_send()
        small_send(2, far_r).wait_recv()
        small[...] = small_z[2]

    small_store = pltpu.make_async_copy(small, small_o, w_sem.at[3])
    small_store.start()
    small_store.wait()
    mixed_store.wait()
    for c in range(CHUNKS - RING, CHUNKS):

        @pl.when(outer)
        def _():
            near_send(c).wait_send()

        @pl.when(inner)
        def _():
            mid_send(c).wait_send()

    for c in (CHUNKS - 2, CHUNKS - 1):
        tot_wait(c)

        @pl.when(inner)
        def _():
            back_send(c).wait_send()

    scope.close()


PIECE_ROWS = 256


def widen(down_b, up_b, out_b, qkv_b, mixed_b, gtok_b, small, *refs):
    mixed_o, gtok_o, gain_o, shift_o, qkv_o, bqkv_o, up_o, bup_o, out_o, bout_o, down_o, bdown_o = refs[:12]
    scratch, load_sem, store_sem, pass_sem = refs[12:-3], *refs[-3:]
    small_v, line_v, bqkv_v, bup_v = scratch[9], scratch[10:13], scratch[13], scratch[14]
    small_load = pltpu.make_async_copy(small, small_v, pass_sem.at[2])
    small_load.start()
    D, FF = up_o.shape
    HC = out_o.shape[0]
    rows_b = scratch[8]
    passed = []
    for i, (src, dst) in enumerate(((mixed_b, mixed_o), (gtok_b, gtok_o))):
        load = pltpu.make_async_copy(src, rows_b.at[i], pass_sem.at[i])
        store = pltpu.make_async_copy(rows_b.at[i], dst, pass_sem.at[i])
        passed.append((load, store))
    work = []
    arrays = [(down_b, down_o), (up_b, up_o), (out_b, out_o)]
    arrays += [(qkv_b.at[t], qkv_o.at[t]) for t in range(3)]
    spaces = scratch[0:2], scratch[2:4], scratch[4:6]
    spaces += tuple(tuple(x.at[t] for x in scratch[6:8]) for t in range(3))
    for (src, dst), (low, wide) in zip(arrays, spaces):
        for row in range(0, src.shape[0], PIECE_ROWS):
            rows = pl.ds(row, PIECE_ROWS)
            n = len(work)
            load = pltpu.make_async_copy(src.at[rows, :], low.at[rows, :], load_sem.at[n])
            store = pltpu.make_async_copy(wide.at[rows, :], dst.at[rows, :], store_sem.at[n])
            work.append((load, store, low, wide, row))
    for load, _ in passed:
        load.start()
    for load, *_ in work:
        load.start()
    small_load.wait()
    for i in range(3):
        line_v[i][...] = small_v[i, :]
    for t in range(3):
        bqkv_v[t, :] = small_v[3, t * HC : (t + 1) * HC]
    bup_v[...] = small_v[3, 3 * HC : 3 * HC + FF]
    lines = (line_v[0], gain_o), (line_v[1], shift_o), (line_v[2], bout_o), (line_v[2], bdown_o)
    lines += (bqkv_v, bqkv_o), (bup_v, bup_o)
    lines = [
        pltpu.make_async_copy(src, dst, pass_sem.at[3 + i]) for i, (src, dst) in enumerate(lines)
    ]
    for item in lines:
        item.start()
    for load, store in passed:
        load.wait()
        store.start()
    for load, store, low, wide, row in work:
        load.wait()

        @pl.loop(0, PIECE_ROWS // 16)
        def _(i):
            at = pl.ds(pl.multiple_of(row + i * 16, 16), 16)
            wide[at, :] = low[at, :].astype(F32)

        store.start()
    for _, store, *_ in work:
        store.wait()
    for _, store in passed:
        store.wait()
    for item in lines:
        item.wait()


def frequencies():
    lane = np.arange(128) % HEAD_DIM
    frequency = np.exp(-(lane % (ROT // 2)) * (2.0 * math.log(10000.0) / ROT))
    return np.where(lane < ROT + ROT // 2, frequency, 0.0).astype(np.float32)[None]


def fused_body(
    tokens,
    segments,
    positions,
    ln_gain,
    ln_bias,
    w_qkv,
    b_qkv,
    w_up,
    b_up,
    w_out,
    b_out,
    w_down,
    b_down,
    grad_out,
):
    _, R, D = tokens.shape
    T = R * lax.axis_size("shard")
    HC = w_qkv.shape[2]
    FF = w_up.shape[1]
    vmem = pl.BlockSpec(memory_space=pltpu.VMEM)
    hbm = pl.BlockSpec(memory_space=pl.ANY)
    block = (CHUNKS, 2, TILE, TILE)
    piece = (2, TILE, TILE)
    out_shape = (
        jax.ShapeDtypeStruct((R, D), BF),
        jax.ShapeDtypeStruct((R, D), BF),
        jax.ShapeDtypeStruct((8, D), F32),
        jax.ShapeDtypeStruct((FF, D), SUM),
        jax.ShapeDtypeStruct((D, FF), SUM),
        jax.ShapeDtypeStruct((HC, D), SUM),
        jax.ShapeDtypeStruct((3, D, HC), SUM),
        jax.ShapeDtypeStruct(block, BF),
    )
    dma = pltpu.SemaphoreType.DMA
    scratch = [
        pltpu.VMEM((R, D), BF),
        pltpu.VMEM((R, D), BF),
        pltpu.VMEM((T, D), BF),
        pltpu.VMEM((T, D), BF),
        pltpu.VMEM((T, FF), BF),
        pltpu.VMEM((T, FF), BF),
        pltpu.VMEM((3, T, HC), BF),
        pltpu.VMEM((T, HC), BF),
        pltpu.VMEM((T, HC), BF),
        pltpu.VMEM((T, 3 * HC), BF),
        pltpu.VMEM((SEQ, HC), F32),
        pltpu.VMEM((SEQ, HC), F32),
        pltpu.VMEM((TILE, HC), F32),
        pltpu.VMEM((TILE, HC), F32),
        pltpu.VMEM((D, 3 * HC), BF),
        pltpu.VMEM((D, FF), BF),
        pltpu.VMEM((HC, D), BF),
        pltpu.VMEM((FF, D), BF),
        pltpu.VMEM((T, 128), F32),
        pltpu.VMEM((T, 128), BF),
        pltpu.VMEM((4,) + piece, BF),
        pltpu.VMEM((RING,) + piece, BF),
        pltpu.VMEM((RING,) + piece, BF),
        pltpu.VMEM((RING,) + piece, BF),
        pltpu.VMEM((RING,) + piece, BF),
        pltpu.VMEM((2,) + piece, BF),
        pltpu.VMEM((2,) + piece, SUM),
        pltpu.VMEM((8, D), F32),
        pltpu.VMEM((3, 8, D), F32),
        pltpu.VMEM((3, 8, D), F32),
        dma((9, 13)),
        dma((9, 13)),
        dma((9,)),
        dma((4,)),
        dma((RING,)),
        dma((RING,)),
        dma((2,)),
        dma((2, 2)),
        dma((CHUNKS,)),
        dma((CHUNKS,)),
        dma((2, 10)),
        dma((2, 10)),
        dma((3,)),
        dma((3,)),
        dma((3,)),
        dma((3,)),
        pltpu.SemaphoreType.REGULAR((2,)),
        pltpu.SemaphoreType.REGULAR((3,)),
    ]
    mixed, gtok, small, g_down, g_up, g_out, g_qkv, _ = pl.pallas_call(
        fused,
        out_shape=out_shape,
        in_specs=[hbm, hbm, vmem, vmem, hbm, vmem, hbm, vmem, hbm, vmem, hbm] + [vmem] * 4,
        out_specs=(hbm,) * 8,
        scratch_shapes=scratch,
        name="layer",
        compiler_params=pltpu.CompilerParams(
            collective_id=0, has_side_effects=True, vmem_limit_bytes=VMEM_BYTES
        ),
    )(
        tokens[0],
        grad_out[0],
        ln_gain[None],
        ln_bias[None],
        jnp.transpose(w_qkv, (1, 0, 2)),
        b_qkv,
        w_up,
        b_up[None],
        w_out,
        b_out[None],
        w_down,
        b_down[None],
        segments,
        positions,
        frequencies(),
    )
    pieces = (FF + D + HC + 3 * D) // PIECE_ROWS
    row = jax.ShapeDtypeStruct((D,), F32)
    outs = pl.pallas_call(
        widen,
        out_shape=(
            jax.ShapeDtypeStruct((R, D), BF),
            jax.ShapeDtypeStruct((R, D), BF),
            row,
            row,
            jax.ShapeDtypeStruct((3, D, HC), F32),
            jax.ShapeDtypeStruct((3, HC), F32),
            jax.ShapeDtypeStruct((D, FF), F32),
            jax.ShapeDtypeStruct((FF,), F32),
            jax.ShapeDtypeStruct((HC, D), F32),
            row,
            jax.ShapeDtypeStruct((FF, D), F32),
            row,
        ),
        in_specs=[hbm] * 7,
        out_specs=(hbm,) * 12,
        scratch_shapes=[
            pltpu.VMEM((FF, D), BF),
            pltpu.VMEM((FF, D), F32),
            pltpu.VMEM((D, FF), BF),
            pltpu.VMEM((D, FF), F32),
            pltpu.VMEM((HC, D), BF),
            pltpu.VMEM((HC, D), F32),
            pltpu.VMEM((3, D, HC), BF),
            pltpu.VMEM((3, D, HC), F32),
            pltpu.VMEM((2, R, D), BF),
            pltpu.VMEM((8, D), F32),
            pltpu.VMEM((D,), F32),
            pltpu.VMEM((D,), F32),
            pltpu.VMEM((D,), F32),
            pltpu.VMEM((3, HC), F32),
            pltpu.VMEM((FF,), F32),
            dma((pieces,)),
            dma((pieces,)),
            dma((9,)),
        ],
        name="widen",
        compiler_params=pltpu.CompilerParams(vmem_limit_bytes=VMEM_BYTES),
    )(g_down, g_up, g_out, g_qkv, mixed, gtok, small)
    mixed, gtok, gain, shift, g_qkv, bqkv, g_up, bup, g_out, bout, g_down, bdown = outs
    return (
        mixed[None],
        gtok[None],
        gain,
        shift,
        jnp.transpose(g_qkv, (1, 0, 2)),
        bqkv,
        g_up,
        bup,
        g_out,
        bout,
        g_down,
        bdown,
    )


def fits_fused(mesh):
    return dict(mesh.shape) == {"shard": 8, "replica": 4}


def solution(mesh):
    placed = (
        P("replica", "shard", None),
        P("replica", None),
        P("replica", None),
        P(),
        P(),
        P(None, None, "shard"),
        P(None, "shard"),
        P(None, "shard"),
        P("shard"),
        P("shard", None),
        P(),
        P("shard", None),
        P(),
        P("replica", "shard", None),
    )
    return jax.shard_map(
        fused_body if fits_fused(mesh) else body,
        mesh=mesh,
        in_specs=placed,
        out_specs=(
            P("replica", "shard", None),
            P("replica", "shard", None),
            P(),
            P(),
            P(None, None, "shard"),
            P(None, "shard"),
            P(None, "shard"),
            P("shard"),
            P("shard", None),
            P(),
            P("shard", None),
            P(),
        ),
        check_vma=False,
    )
```
